256 devices in a mesh: branch: 64 (over y, z, core), head: 4 (over x).
Axes of the slice: x: 4, y: 4, z: 8, core: 2. Of those that a mesh axis runs over, the one named last changes fastest.
Arguments:
- queries: bfloat16 [8192, 64, 128], P('branch', 'head'), may hold values from -120 to 120
- keys: bfloat16 [8192, 8, 128], P('branch', 'head'), may hold values from -6 to 6
- values: bfloat16 [8192, 8, 128], P('branch', 'head'), may hold values from -6 to 6
- cotangent: bfloat16 [8192, 64, 128], P('branch', 'head'), may hold values from -216 to 216
- rewards: bfloat16 [64], P('branch'), may hold values from 0 to 2
- groups: int32 [64], P('branch'), may hold values from 0 to 15, as said below
- ancestors: int32 [64, 8], P('branch'), may hold values from -1 to 63, as said below
- step_ids: int32 [64, 128], P('branch'), may hold values from 0 to 3, never falling along the last dimension, each value on 1 to 64 neighbouring positions
Outputs:
- query_grad: float32 [8192, 64, 128], P('branch', 'head')
- key_grad: float32 [8192, 8, 128], P('branch', 'head')
- value_grad: float32 [8192, 8, 128], P('branch', 'head')
- grad_rms: float32 [], replicated
The draws below stay inside these ranges and needn't reach their ends.
Inputs may be any that keep to these rules, and one draw needn't show every extreme that they name: `groups`: each group id names exactly 4 blocks; blocks of one group have the same ancestor list. Row b lists block b's ancestors nearest first, each entry the parent of the one before, then -1 to the end; a block never lists itself; some block has exactly 8 ancestors.
All inputs are finite; a program needn't handle non-finite values.
Results may differ from the reference program's by a relative error of at most 0.02.
Values may be sent and summed in bfloat16 or wider, within the bound.
No kernel may reach another device: no remote copies, remote signals or barrier semaphores. Data moves between devices by JAX's collectives and lax.ppermute only.
A program may use at most 128 MiB of HBM per device.

```python
import math
import jax
import jax.numpy as jnp
import numpy as np
from jax import lax

HQ = 64
KVH = 8
HD = 128
TOK_DEV = 128
GROUP = 4
STEPS = 4
NBLK = 64
NGROUP = 16
DEPTH = 8
TOKENS = 8192


def tree_layout(key):
    key_parent, key_chain, key_order = jax.random.split(key, 3)
    chain_pick = jax.random.randint(key_chain, (NGROUP,), 0, GROUP)
    upper_bound = jnp.maximum(jnp.arange(NGROUP, dtype=jnp.int32) * GROUP, 1)
    candidates = jax.random.randint(key_parent, (NGROUP,), 0, upper_bound)

    def grow(group_index, state):
        parent, level = state
        chained = (group_index - 1) * GROUP + chain_pick[group_index]
        fallback = candidates[group_index]
        fallback = jnp.where(level[fallback] >= DEPTH, parent[fallback], fallback)
        chosen = jnp.where(group_index <= DEPTH, chained, fallback)
        members = group_index * GROUP + jnp.arange(GROUP, dtype=jnp.int32)
        parent = parent.at[members].set(chosen)
        level = level.at[members].set(level[chosen] + 1)
        return (parent, level)
    parent_init = jnp.full((NBLK,), -1, jnp.int32)
    level_init = jnp.zeros((NBLK,), jnp.int32)
    parent, level = lax.fori_loop(1, NGROUP, grow, (parent_init, level_init))
    lineage = []
    current = parent
    for depth_index in range(DEPTH):
        lineage.append(current)
        current = jnp.where(current >= 0, parent[jnp.maximum(current, 0)], -1)
    logical = jnp.stack(lineage, axis=1)
    shuffled = jax.random.permutation(key_order, NBLK).astype(jnp.int32)
    root_parent = chain_pick[1]
    holder = jnp.sum(jnp.where(shuffled == NBLK - 1, jnp.arange(NBLK, dtype=jnp.int32), 0))
    placement = shuffled.at[holder].set(shuffled[root_parent])
    placement = placement.at[root_parent].set(NBLK - 1)
    moved = jnp.where(logical >= 0, placement[jnp.maximum(logical, 0)], -1)
    ancestors_out = jnp.zeros((NBLK, DEPTH), jnp.int32).at[placement].set(moved)
    groups_out = jnp.zeros((NBLK,), jnp.int32).at[placement].set(jnp.arange(NBLK, dtype=jnp.int32) // GROUP)
    return (ancestors_out, groups_out)


def base_attention(key):
    key_query, key_key = jax.random.split(key)
    query_base = jnp.clip(jax.random.normal(key_query, (TOKENS, HQ, HD), jnp.float32), -6.0, 6.0)
    key_base = jnp.clip(jax.random.normal(key_key, (TOKENS, KVH, HD), jnp.float32), -6.0, 6.0)
    return (query_base, key_base)


def draw_queries(key, part):
    query_base, key_base = base_attention(key)
    return query_base.astype(jnp.bfloat16)


def draw_keys(key, part):
    query_base, key_base = base_attention(key)
    return key_base.astype(jnp.bfloat16)


def draw_cotangent(key, part):
    key = jax.random.fold_in(key, 13)
    key_noise, key_shared = jax.random.split(key)
    shared = jnp.clip(jax.random.normal(key_shared, (HQ, HD), jnp.float32), -3.0, 3.0)
    head_rise = 1.0 + 2.0 * jnp.arange(HQ, dtype=jnp.float32) / (HQ - 1)
    token_rise = 1.0 + 2.0 * jnp.arange(TOKENS, dtype=jnp.float32) / (TOKENS - 1)
    noise = jnp.clip(jax.random.normal(key_noise, (TOKENS, HQ, HD), jnp.float32), -6.0, 6.0)
    base = 0.6 * noise + 0.8 * shared[None, :, :]
    return (4.0 * base * head_rise[None, :, None] * token_rise[:, None, None]).astype(jnp.bfloat16)


def draw_ancestors(key, part):
    ancestors_out, groups_out = tree_layout(key)
    return ancestors_out


def draw_groups(key, part):
    ancestors_out, groups_out = tree_layout(key)
    return groups_out


def level_of(stream_key, dims, cuts, smallest, high):
    factor_of = 1.0
    for dim, shards_of in cuts:
        draws = jax.random.uniform(jax.random.fold_in(jax.random.fold_in(stream_key, 6), dim), (shards_of,), jnp.float32, smallest / len(cuts), high / len(cuts))
        factor_of = factor_of * jnp.repeat(jnp.exp(draws), dims[dim] // shards_of).reshape((-1,) + (1,) * (len(dims) - 1 - dim))
    return factor_of


def split_up(amount, total, limit, lean):
    weights = [(1 << 20) // math.isqrt(standing ** lean) + 1 for standing in range(2, amount + 1)]
    surplus, holding = total - limit - (amount - 1), [1] * (amount - 1)
    while surplus > 0:
        free = [i for i in range(amount - 1) if holding[i] < limit]
        pool, remaining = sum([weights[i] for i in free]), surplus
        for i in free:
            more = min(limit - holding[i], max(1, remaining * weights[i] // pool), surplus)
            holding[i] = holding[i] + more
            surplus = surplus - more
    return np.array([limit] + holding)


def ragged(stream_key, count, total, bound, skew):
    if count == 2:
        one = jax.random.randint(stream_key, (), max(1, total - bound), min(bound, total - 1) + 1)
        return jnp.stack([one, total - one])
    tallies = jnp.asarray(split_up(count, total, bound, skew), jnp.int32)
    pairs = (count - 1) // 2
    giver, receiver = tallies[1:1 + 2 * pairs:2], tallies[2:2 + 2 * pairs:2]
    margin = jnp.minimum(giver - 1, bound - receiver)
    passed = jax.random.randint(jax.random.fold_in(stream_key, 1), (pairs,), 0, 1 << 20) % (margin + 1)
    tallies = tallies.at[1:1 + 2 * pairs:2].set(giver - passed).at[2:2 + 2 * pairs:2].set(receiver + passed)
    return tallies[jax.random.permutation(jax.random.fold_in(stream_key, 2), count)]


def gaussian(rng, extent, width, reach, cuts=(), held_as=jnp.bfloat16):
    factor_of = level_of(rng, extent, cuts, -0.22, 0.18) if cuts else 1.0
    array = jax.random.normal(rng, extent, jnp.float32) * width * factor_of
    return jnp.minimum(jnp.maximum(array, -reach), reach).astype(held_as)


def setup_inputs(seed: int = 0) -> dict:
    key_of = jax.random.split(jax.random.key(seed), 9)
    queries = draw_queries(jax.random.fold_in(key_of[8], 71), 0)
    keys = draw_keys(jax.random.fold_in(key_of[8], 71), 0)
    values = gaussian(key_of[2], (TOKENS, KVH, HD), 1.0, 6.0, ((0, 64), (1, 4)))
    cotangent = draw_cotangent(jax.random.fold_in(key_of[8], 71), 0)
    rewards = jnp.clip(2.0 * jax.random.uniform(key_of[4], (NBLK,), jnp.float32) ** level_of(key_of[4], (NBLK,), ((0, 64),), -0.2, 0.2), 0.0, 2.0).astype(jnp.bfloat16)
    groups = draw_groups(jax.random.fold_in(key_of[8], 71), 0)
    ancestors = draw_ancestors(jax.random.fold_in(key_of[8], 71), 0)
    step_ids = jax.vmap(lambda own: jnp.searchsorted(jnp.cumsum(ragged(own, STEPS, TOK_DEV, TOK_DEV // 2, 0)), jnp.arange(TOK_DEV), side="right"))(jax.random.split(key_of[7], NBLK)).reshape((NBLK, TOK_DEV)).astype(jnp.int32)
    return dict(queries=queries, keys=keys, values=values, cotangent=cotangent, rewards=rewards, groups=groups, ancestors=ancestors, step_ids=step_ids)


def reference(queries, keys, values, cotangent, rewards, groups, ancestors, step_ids):
    head_ratio = HQ // KVH
    slot_count = DEPTH + 1
    score_scale = 1.0 / math.sqrt(HD)
    reward = rewards.astype(jnp.float32)
    membership = (groups[:, None] == jnp.arange(NGROUP, dtype=jnp.int32)[None, :]).astype(jnp.float32)
    group_sum = lax.optimization_barrier(jnp.sum(membership * reward[:, None], axis=0))
    group_sq = lax.optimization_barrier(jnp.sum(membership * (reward * reward)[:, None], axis=0))
    mean_here = group_sum[groups] / GROUP
    spread_here = jnp.sqrt(jnp.maximum(group_sq[groups] / GROUP - mean_here * mean_here, 0.25))
    advantage = (reward - mean_here) / spread_here
    trained = (step_ids % 2 == 0).astype(jnp.float32)
    weight = advantage[:, None] * trained
    query_blocks = queries.reshape(NBLK, TOK_DEV, KVH, head_ratio, HD)
    key_blocks = keys.reshape(NBLK, TOK_DEV, KVH, HD)
    value_blocks = values.reshape(NBLK, TOK_DEV, KVH, HD)
    grad_blocks = cotangent.reshape(NBLK, TOK_DEV, KVH, head_ratio, HD)
    query_pos = jnp.arange(TOK_DEV)
    key_slot = jnp.arange(slot_count * TOK_DEV) // TOK_DEV
    key_pos = jnp.arange(slot_count * TOK_DEV) % TOK_DEV

    def visit_block(state, block_index):
        key_acc, value_acc = state
        lineage = ancestors[block_index]
        slot_ids = jnp.concatenate([lineage, block_index[None].astype(jnp.int32)])
        slot_valid = slot_ids >= 0
        safe_ids = jnp.maximum(slot_ids, 0)
        near_keys = key_blocks[safe_ids].reshape(slot_count * TOK_DEV, KVH, HD).astype(jnp.float32)
        near_values = value_blocks[safe_ids].reshape(slot_count * TOK_DEV, KVH, HD).astype(jnp.float32)
        visible = jnp.where(key_slot[None, :] < DEPTH, slot_valid[key_slot][None, :], key_pos[None, :] <= query_pos[:, None])
        query_here = query_blocks[block_index].astype(jnp.float32)
        scores = jnp.einsum('qgrd,kgd->grqk', query_here, near_keys) * score_scale
        top_score = lax.optimization_barrier(jnp.max(jnp.where(visible, scores, -1e+30), axis=-1, keepdims=True))
        exponent = jnp.where(visible, jnp.exp(scores - top_score), 0.0)
        probs = exponent / lax.optimization_barrier(jnp.sum(exponent, axis=-1, keepdims=True))
        probs_low = lax.optimization_barrier(probs.astype(jnp.bfloat16)).astype(jnp.float32)
        grad_here = weight[block_index][:, None, None, None] * grad_blocks[block_index].astype(jnp.float32)
        grad_here = lax.optimization_barrier(grad_here.astype(jnp.bfloat16)).astype(jnp.float32)
        attended = jnp.einsum('grqk,kgd->qgrd', probs_low, near_values)
        row_delta = lax.optimization_barrier(jnp.sum(grad_here * attended, axis=-1))
        prob_grad = jnp.einsum('qgrd,kgd->grqk', grad_here, near_values)
        dscore = probs * (prob_grad - jnp.transpose(row_delta, (1, 2, 0))[..., None])
        dscore = lax.optimization_barrier(dscore.astype(jnp.bfloat16)).astype(jnp.float32)
        query_part = jnp.einsum('grqk,kgd->qgrd', dscore, near_keys) * score_scale
        key_part = jnp.einsum('grqk,qgrd->kgd', dscore, query_here) * score_scale
        value_part = jnp.einsum('grqk,qgrd->kgd', probs_low, grad_here)
        kept_slot = slot_valid.astype(jnp.float32)[:, None, None, None]
        key_acc = key_acc.at[safe_ids].add(key_part.reshape(slot_count, TOK_DEV, KVH, HD) * kept_slot)
        value_acc = value_acc.at[safe_ids].add(value_part.reshape(slot_count, TOK_DEV, KVH, HD) * kept_slot)
        return ((key_acc, value_acc), query_part.reshape(TOK_DEV, HQ, HD))
    zero_grads = jnp.zeros((NBLK, TOK_DEV, KVH, HD), jnp.float32)
    (key_all, value_all), query_all = lax.scan(visit_block, (zero_grads, zero_grads), jnp.arange(NBLK, dtype=jnp.int32))
    query_grad = query_all.reshape(TOKENS, HQ, HD)
    key_grad = key_all.reshape(TOKENS, KVH, HD)
    value_grad = value_all.reshape(TOKENS, KVH, HD)
    total = jnp.sum(query_grad * query_grad) + jnp.sum(key_grad * key_grad) + jnp.sum(value_grad * value_grad)
    grad_rms = jnp.sqrt(total / (TOKENS * (HQ + 2 * KVH) * HD))
    return (query_grad, key_grad, value_grad, grad_rms)
```

```python
import math

import jax
import jax.numpy as jnp
from jax import lax
from jax.experimental import pallas as pl
from jax.experimental.pallas import tpu as pltpu
from jax.sharding import PartitionSpec as P

NY, NZ, NC = 4, 8, 2
NBLK = NY * NZ * NC
NHEAD = 4
GROUP = 4
DEPTH = 8
TOK = 128
HD = 128
KV = 2
RATIO = 8
LANES = 128
HALF = 8
ENTRIES = DEPTH + 1
CHUNK = 256
F32 = jnp.float32
BF16 = jnp.bfloat16
VMEM = pltpu.VMEM
SMEM = pltpu.SMEM
NT = (((1,), (1,)), ((), ()))
NN = (((1,), (0,)), ((), ()))
TN = (((0,), (0,)), ((), ()))


def index_of(y, z, c):
    return ((y % NY) * NZ + z % NZ) * NC + c % NC


def every():
    return [(y, z, c) for y in range(NY) for z in range(NZ) for c in range(NC)]


def along_y(x, step):
    pairs = [(index_of(y, z, c), index_of(y + step, z, c)) for y, z, c in every()]
    return lax.ppermute(x, "branch", pairs)


def other_core(x):
    pairs = [(index_of(y, z, c), index_of(y, z, c + 1)) for y, z, c in every()]
    return lax.ppermute(x, "branch", pairs)


def along_head(x, step):
    pairs = [(i, (i + step) % NHEAD) for i in range(NHEAD)]
    return lax.ppermute(x, "head", pairs)


def swap_z(x):
    groups = [[index_of(y, z, c) for z in range(NZ)] for y in range(NY) for c in range(NC)]
    return lax.all_to_all(x, "branch", 0, 0, axis_index_groups=groups, tiled=False)


def swap_yz(x):
    groups = [[index_of(y, z, c) for y in range(NY) for z in range(NZ)] for c in range(NC)]
    return lax.all_to_all(x, "branch", 0, 0, axis_index_groups=groups, tiled=False)


def call(body, outs, scratch=(), vmem_mb=32):
    return dict(
        out_shape=outs,
        scratch_shapes=list(scratch),
        compiler_params=pltpu.CompilerParams(vmem_limit_bytes=vmem_mb << 20),
    )


def in_vmem():
    return pl.BlockSpec(memory_space=VMEM)


def in_smem():
    return pl.BlockSpec(memory_space=SMEM)


def plan_kernel(pos, mine, other, picked, table, scale, index_v, index_s, sem):
    y, z, c = pos[0], pos[1], pos[2]
    own = y * NZ + z
    meta_m = mine[...].astype(F32)[:, 16:24, :]
    meta_o = other[...].astype(F32)[:, 16:24, :]
    lane = lax.broadcasted_iota(jnp.int32, (8, LANES), 1)
    lane_f = lane.astype(F32)
    is_block = lane < NBLK
    wide = lax.broadcasted_iota(jnp.int32, (NY * NZ, LANES), 1).astype(F32)
    hit = jnp.maximum(
        jnp.where(meta_m[:, 0, :] == wide, 1.0, 0.0), jnp.where(meta_o[:, 0, :] == wide, 1.0, 0.0)
    )
    inner = jnp.max(hit, axis=0, keepdims=True)
    inner = jnp.where(is_block, jnp.broadcast_to(inner, (8, LANES)), 0.0)
    before = (
        lax.broadcasted_iota(jnp.int32, (LANES, LANES), 0)
        < lax.broadcasted_iota(jnp.int32, (LANES, LANES), 1)
    ).astype(F32).astype(BF16)
    rank = lax.dot_general(inner.astype(BF16), before, NN, preferred_element_type=F32)
    row = lax.broadcasted_iota(jnp.int32, (8, LANES), 0)
    wanted = (row * 2 + c).astype(F32)
    chosen = jnp.where((rank == wanted) & (inner > 0.0), lane_f, 0.0)
    index = jnp.sum(chosen, axis=1, keepdims=True).astype(jnp.int32)
    index_v[...] = jnp.broadcast_to(index, (8, LANES))
    copy = pltpu.make_async_copy(index_v, index_s, sem)
    copy.start()
    for yy in range(NY):
        line = mine[yy * NZ + z].astype(F32)[16:24, :]
        same = (line == lane_f) & is_block
        slot = jnp.sum(jnp.where(same, rank + 1.0, 0.0), axis=1, keepdims=True) - 1.0
        table[yy * 8 : yy * 8 + 8, :] = jnp.broadcast_to(slot.astype(jnp.int32), (8, LANES))
    table[32:40, :] = jnp.where(inner > 0.0, rank, -1.0).astype(jnp.int32)
    here = mine[own].astype(F32)[16:24, :]
    group, reward = here[0:1, :], here[1:2, :]
    in_m = jnp.where(meta_m[:, 0, :] == group, meta_m[:, 1, :], 0.0)
    in_o = jnp.where(meta_o[:, 0, :] == group, meta_o[:, 1, :], 0.0)
    total = jnp.sum(in_m + in_o, axis=0, keepdims=True)
    squares = jnp.sum(in_m * in_m + in_o * in_o, axis=0, keepdims=True)
    mean = total / GROUP
    spread = jnp.sqrt(jnp.maximum(squares / GROUP - mean * mean, 0.25))
    advantage = (reward - mean) / spread
    advantage = jnp.sum(jnp.where(lane[0:1] == NBLK, advantage, 0.0), axis=1, keepdims=True)
    scale[...] = jnp.broadcast_to(advantage, (8, LANES))
    copy.wait()
    for s in range(HALF):
        block = index_s[s, 0]
        place = block // 2

        @pl.when(block % 2 == c)
        def _():
            picked[:, s] = jnp.broadcast_to(mine[place, 0:16, :][None], (NZ, 16, LANES))

        @pl.when(block % 2 != c)
        def _():
            picked[:, s] = jnp.broadcast_to(other[place, 0:16, :][None], (NZ, 16, LANES))


def plan(pos, mine, other):
    return pl.pallas_call(
        plan_kernel,
        in_specs=[in_smem(), in_vmem(), in_vmem()],
        out_specs=(in_vmem(), in_vmem(), in_vmem()),
        **call(
            plan_kernel,
            (
                jax.ShapeDtypeStruct((NZ, HALF, 16, LANES), BF16),
                jax.ShapeDtypeStruct((40, LANES), jnp.int32),
                jax.ShapeDtypeStruct((8, LANES), F32),
            ),
            [
                VMEM((8, LANES), jnp.int32),
                SMEM((8, LANES), jnp.int32),
                pltpu.SemaphoreType.DMA,
            ],
        ),
        name="plan",
    )(pos, mine, other)


def deal_kernel(pos, table, mine, other, *outs):
    y, c = pos[0], pos[2]
    for k in range(NY):
        target = lax.rem(y + k, NY)
        for d in range(DEPTH):
            slot = jnp.maximum(table[target * 8 + d, 0], 0)
            place = slot // 2

            @pl.when(slot % 2 == c)
            def _():
                outs[k][d] = mine[:, place]

            @pl.when(slot % 2 != c)
            def _():
                outs[k][d] = other[:, place]


def deal(pos, table, mine, other):
    return pl.pallas_call(
        deal_kernel,
        in_specs=[in_smem(), in_smem(), in_vmem(), in_vmem()],
        out_specs=(in_vmem(),) * NY,
        **call(deal_kernel, (jax.ShapeDtypeStruct((DEPTH, NZ, 16, LANES), BF16),) * NY),
        name="deal",
    )(pos, table, mine, other)


def attend_kernel(
    pos, table, scale, queries, cotangent, own_kv, a0, a1, a2, a3,
    query_grad, own_grad, c0, c1, c2, c3, squares,
    keys_all, values_all, q_all, g_all, key_sum, value_sum,
):
    y = pos[0]
    parts = (a0, a1, a2, a3)
    contribs = (c0, c1, c2, c3)
    factor = 1.0 / math.sqrt(HD)
    weight = scale[0:1, :]
    total = jnp.zeros((8, LANES), F32)
    for h in range(KV):
        keys_all[0:TOK, :] = own_kv[h]
        values_all[0:TOK, :] = own_kv[KV + h]
        for d in range(DEPTH):
            for k in range(NY):
                at = TOK * (d + 1) + 32 * k
                keys_all[at : at + 32, :] = parts[k][d, 2 * h : 2 * h + 2].reshape(32, LANES)
                values_all[at : at + 32, :] = parts[k][d, 4 + 2 * h : 6 + 2 * h].reshape(32, LANES)
        heads = slice(RATIO * h, RATIO * (h + 1))
        q_all[...] = queries[...].astype(F32)[:, heads, :].reshape(TOK * RATIO, HD).astype(BF16)
        g_all[...] = (
            (cotangent[...].astype(F32)[:, heads, :] * weight[None])
            .reshape(TOK * RATIO, HD)
            .astype(BF16)
        )
        for step in range(TOK * RATIO // CHUNK):
            rows = slice(step * CHUNK, (step + 1) * CHUNK)
            q, g = q_all[rows, :], g_all[rows, :]
            scores = []
            for d in range(ENTRIES):
                s = lax.dot_general(
                    keys_all[d * TOK : (d + 1) * TOK, :], q, NT, preferred_element_type=F32
                ) * factor
                if d == 0:
                    key_pos = lax.broadcasted_iota(jnp.int32, (TOK, CHUNK), 0)
                    query_pos = step * (CHUNK // RATIO) + lax.broadcasted_iota(
                        jnp.int32, (TOK, CHUNK), 1
                    ) // RATIO
                    s = jnp.where(key_pos <= query_pos, s, -1e30)
                else:
                    s = jnp.where(table[y * 8 + d - 1, 0] >= 0, s, -1e30)
                scores.append(s)
            top = scores[0]
            for s in scores[1:]:
                top = jnp.maximum(top, s)
            top = jnp.max(top, axis=0, keepdims=True)
            exps = [jnp.exp(s - top) for s in scores]
            norm = exps[0]
            for e in exps[1:]:
                norm = norm + e
            norm = 1.0 / jnp.sum(norm, axis=0, keepdims=True)
            probs = [e * norm for e in exps]
            lows = [p.astype(BF16) for p in probs]
            pgs = [
                lax.dot_general(
                    values_all[d * TOK : (d + 1) * TOK, :], g, NT, preferred_element_type=F32
                )
                for d in range(ENTRIES)
            ]
            delta = lows[0].astype(F32) * pgs[0]
            for d in range(1, ENTRIES):
                delta = delta + lows[d].astype(F32) * pgs[d]
            delta = jnp.sum(delta, axis=0, keepdims=True)
            dscores = [(probs[d] * (pgs[d] - delta)).astype(BF16) for d in range(ENTRIES)]
            low = jnp.concatenate(lows, 0)
            ds = jnp.concatenate(dscores, 0)
            value_part = lax.dot_general(low, g, NN, preferred_element_type=F32)
            key_part = lax.dot_general(ds, q, NN, preferred_element_type=F32)
            if step == 0:
                value_sum[...] = value_part
                key_sum[...] = key_part
            else:
                value_sum[...] += value_part
                key_sum[...] += key_part
            dq = lax.dot_general(ds, keys_all[...], TN, preferred_element_type=F32) * factor
            total = total + jnp.sum((dq * dq).reshape(CHUNK // 8, 8, HD), axis=0)
            toks = slice(step * (CHUNK // RATIO), (step + 1) * (CHUNK // RATIO))
            query_grad[toks, heads, :] = dq.reshape(CHUNK // RATIO, RATIO, HD)
        own_grad[h] = key_sum[0:TOK, :] * factor
        own_grad[KV + h] = value_sum[0:TOK, :]
        for k in range(NY):
            for d in range(DEPTH):
                at = TOK * (d + 1) + 32 * k
                contribs[k][d, 2 * h : 2 * h + 2] = (
                    (key_sum[at : at + 32, :] * factor).astype(BF16).reshape(2, 16, LANES)
                )
                contribs[k][d, 4 + 2 * h : 6 + 2 * h] = (
                    value_sum[at : at + 32, :].astype(BF16).reshape(2, 16, LANES)
                )
    for k in range(NY):
        piece = lax.rem(y + NY - k, NY)
        for kind in range(2):
            for h in range(KV):
                for half in range(2):
                    rows = pl.ds(pl.multiple_of(half * 64 + piece * 16, 16), 16)
                    contribs[k][DEPTH, kind * 4 + h * 2 + half] = own_grad[kind * 2 + h, rows, :].astype(BF16)
    squares[...] = total


def attend(pos, table, scale, queries, cotangent, own_kv, parts):
    rows = TOK * RATIO
    keys = TOK * ENTRIES
    return pl.pallas_call(
        attend_kernel,
        in_specs=[in_smem(), in_smem()] + [in_vmem()] * 8,
        out_specs=(in_vmem(),) * 7,
        **call(
            attend_kernel,
            (
                jax.ShapeDtypeStruct((TOK, KV * RATIO, HD), F32),
                jax.ShapeDtypeStruct((2 * KV, TOK, HD), F32),
            )
            + (jax.ShapeDtypeStruct((ENTRIES, NZ, 16, LANES), BF16),) * NY
            + (jax.ShapeDtypeStruct((8, LANES), F32),),
            [
                VMEM((keys, HD), BF16),
                VMEM((keys, HD), BF16),
                VMEM((rows, HD), BF16),
                VMEM((rows, HD), BF16),
                VMEM((keys, HD), F32),
                VMEM((keys, HD), F32),
            ],
            vmem_mb=48,
        ),
        name="attend",
    )(pos, table, scale, queries, cotangent, own_kv, *parts)


def gather_kernel(pos, table, r0, r1, r2, r3, keep, send, acc):
    y, z, c = pos[0], pos[1], pos[2]
    acc[...] = jnp.zeros_like(acc)
    for k, r in enumerate((r0, r1, r2, r3)):
        source = lax.rem(y + k, NY)
        for d in range(ENTRIES):
            if d < DEPTH:
                slot = table[source * 8 + d, 0]
            else:
                slot = table[32, (source * NZ + z) * NC + c]

            @pl.when(slot >= 0)
            def _():
                acc[slot % 2, slot // 2] += r[d].astype(F32)

    for s in range(HALF):
        keep[:, s] = acc[c, s]
        send[:, s] = acc[1 - c, s].astype(BF16)


def gather(pos, table, parts):
    return pl.pallas_call(
        gather_kernel,
        in_specs=[in_smem(), in_smem()] + [in_vmem()] * NY,
        out_specs=(in_vmem(), in_vmem()),
        **call(
            gather_kernel,
            (
                jax.ShapeDtypeStruct((NZ, HALF, 16, LANES), F32),
                jax.ShapeDtypeStruct((NZ, HALF, 16, LANES), BF16),
            ),
            [VMEM((2, HALF, NZ, 16, LANES), F32)],
        ),
        name="combine",
    )(pos, table, *parts)


def total_kernel(pos, table, parts, own_grad, squares, sums, pack):
    b = pos[3]
    sums_now = parts[0].astype(F32)
    for z in range(1, NZ):
        sums_now = sums_now + parts[z].astype(F32)
    pack[0:HALF] = sums_now.astype(BF16)
    own = own_grad[...]
    own_sq = jnp.sum((own * own).reshape(2 * KV * TOK // 8, 8, LANES), axis=0)
    leaf = table[32, b] < 0
    tile = squares[...] + jnp.where(leaf, own_sq, 0.0)
    tile = tile + jnp.sum((sums_now * sums_now).reshape(HALF * 2, 8, LANES), axis=0)
    value = jnp.sum(jnp.sum(tile, axis=0, keepdims=True), axis=1, keepdims=True)
    value = jnp.broadcast_to(value, (8, LANES))
    sums[...] = value
    pack[HALF] = split_rows(value, 16)


def split_rows(value, rows):
    high = value.astype(BF16).astype(F32)
    middle = (value - high).astype(BF16).astype(F32)
    low = value - high - middle
    row = lax.broadcasted_iota(jnp.int32, (8, LANES), 0)
    tile = jnp.where(row == 0, high, jnp.where(row == 1, middle, jnp.where(row == 2, low, 0.0)))
    if rows > 8:
        tile = jnp.concatenate([tile, jnp.zeros((rows - 8, LANES), F32)], 0)
    return tile.astype(BF16)


def total_of(pos, table, parts, own_grad, squares):
    return pl.pallas_call(
        total_kernel,
        in_specs=[in_smem(), in_smem()] + [in_vmem()] * 3,
        out_specs=(in_vmem(), in_vmem()),
        **call(
            total_kernel,
            (
                jax.ShapeDtypeStruct((8, LANES), F32),
                jax.ShapeDtypeStruct((HALF + 1, 16, LANES), BF16),
            ),
        ),
        name="total",
    )(pos, table, parts, own_grad, squares)


def route_kernel(pos, table, sums, mine, other, out):
    c = pos[2]
    tail = other[HALF].astype(F32)[0:8, :]
    value = sums[...] + jnp.sum(tail, axis=0, keepdims=True)
    rows = split_rows(value, 8).astype(F32)
    for place in range(NY * NZ):
        slot = table[32, place * NC + c]
        at = jnp.maximum(slot, 0) // 2
        picked = jnp.where(slot % 2 == c, mine[at].astype(F32), other[at].astype(F32))
        out[place] = jnp.concatenate([picked, rows], 0).astype(BF16)


def route(pos, table, sums, mine, other):
    return pl.pallas_call(
        route_kernel,
        in_specs=[in_smem(), in_smem()] + [in_vmem()] * 3,
        out_specs=in_vmem(),
        **call(route_kernel, jax.ShapeDtypeStruct((NY * NZ, 24, LANES), BF16)),
        name="route",
    )(pos, table, sums, mine, other)


def finish_kernel(pos, table, arrived, own_grad, grads, sums):
    b = pos[3]
    inner = table[32, b] >= 0

    @pl.when(inner)
    def _():
        for z in range(NZ):
            kind_head, half = z // 2, z % 2
            for y in range(NY):
                at = half * 64 + y * 16
                grads[kind_head, at : at + 16, :] = arrived[y * NZ + z, 0:16, :].astype(F32)

    @pl.when(jnp.logical_not(inner))
    def _():
        grads[...] = own_grad[...]

    tails = jnp.sum(arrived[...].astype(F32)[:, 16:24, :], axis=0)
    sums[...] = jnp.broadcast_to(jnp.sum(tails, axis=0, keepdims=True), (8, LANES))


def finish(pos, table, arrived, own_grad):
    return pl.pallas_call(
        finish_kernel,
        in_specs=[in_smem(), in_smem(), in_vmem(), in_vmem()],
        out_specs=(in_vmem(), in_vmem()),
        **call(
            finish_kernel,
            (
                jax.ShapeDtypeStruct((2 * KV, TOK, HD), F32),
                jax.ShapeDtypeStruct((8, LANES), F32),
            ),
        ),
        name="finish",
    )(pos, table, arrived, own_grad)


def local(queries, keys, values, cotangent, rewards, groups, ancestors, step_ids):
    b = lax.axis_index("branch")
    pos = jnp.stack([b // (NZ * NC), (b // NC) % NZ, b % NC, b]).astype(jnp.int32)
    own_kv = jnp.stack([keys, values]).transpose(0, 2, 1, 3)
    pieces = (
        own_kv.reshape(2, KV, 2, NY, 16, HD).transpose(3, 0, 1, 2, 4, 5).reshape(NY * NZ, 16, HD)
    )
    own_kv = own_kv.reshape(2 * KV, TOK, HD)
    line = jnp.broadcast_to(ancestors[0].astype(BF16)[:, None], (8, NBLK))
    facts = jnp.concatenate(
        [groups.astype(BF16), rewards, jnp.zeros((6,), BF16)]
    )
    meta = jnp.concatenate([line, jnp.broadcast_to(facts[:, None], (8, LANES - NBLK))], 1)
    packet = jnp.concatenate([pieces, jnp.broadcast_to(meta[None], (NY * NZ, 8, LANES))], 1)
    mine = swap_yz(packet)
    other = other_core(mine)
    trained = (step_ids[0] % 2 == 0)[:, None, None]
    masked = jnp.where(trained, cotangent, jnp.zeros_like(cotangent))
    picked, table, scale = plan(pos, mine, other)
    column = swap_z(picked)
    column_other = other_core(column)
    dealt = deal(pos, table, column, column_other)
    parts = [dealt[0]] + [along_y(dealt[k], k) for k in (1, 2, 3)]
    query_grad, own_grad, c0, c1, c2, c3, squares = attend(
        pos, table, scale, queries, masked, own_kv, parts
    )
    back = [c0] + [along_y(x, -k) for k, x in ((1, c1), (2, c2), (3, c3))]
    keep, send = gather(pos, table, back)
    halves = (keep + other_core(send).astype(F32)).astype(BF16)
    sums, pack = total_of(pos, table, swap_z(halves), own_grad, squares)
    packet_back = route(pos, table, sums, pack, other_core(pack))
    grads, sums = finish(pos, table, swap_yz(packet_back), own_grad)
    mine_sum = sums[0:1, :]
    all_sum = mine_sum
    for k in (1, 2, 3):
        all_sum = all_sum + along_head(mine_sum, k)
    count = float(NBLK * TOK * NHEAD * (KV * RATIO + 2 * KV) * HD)
    grad_rms = jnp.sqrt(all_sum[0, 0] / count)
    out = grads.reshape(2, KV, TOK, HD).transpose(0, 2, 1, 3)
    return query_grad, out[0], out[1], grad_rms


def solution(mesh):
    in_specs = (
        P("branch", "head", None),
        P("branch", "head", None),
        P("branch", "head", None),
        P("branch", "head", None),
        P("branch"),
        P("branch"),
        P("branch", None),
        P("branch", None),
    )
    out_specs = (
        P("branch", "head", None),
        P("branch", "head", None),
        P("branch", "head", None),
        P(),
    )
    return jax.shard_map(local, mesh=mesh, in_specs=in_specs, out_specs=out_specs, check_vma=False)
```

```python
import functools
import math

import jax
import jax.numpy as jnp
from jax import lax
from jax.experimental import pallas as pl
from jax.experimental.pallas import tpu as pltpu
from jax.sharding import PartitionSpec as P

NY, NZ, NC = 4, 8, 2
NBLK = NY * NZ * NC
NHEAD = 4
GROUP = 4
DEPTH = 8
TOK = 128
HD = 128
KV = 2
RATIO = 8
LANES = 128
HALF = 8
ROWS = TOK * RATIO
KINDS = 2 * KV
PART = 32 * DEPTH
F32 = jnp.float32
BF16 = jnp.bfloat16
VMEM = pltpu.VMEM
NT = (((1,), (1,)), ((), ()))
NN = (((1,), (0,)), ((), ()))
TN = (((0,), (0,)), ((), ()))


def index_of(y, z, c):
    return ((y % NY) * NZ + z % NZ) * NC + c % NC


def every():
    return [(y, z, c) for y in range(NY) for z in range(NZ) for c in range(NC)]


def along_y(x, step):
    pairs = [(index_of(y, z, c), index_of(y + step, z, c)) for y, z, c in every()]
    return lax.ppermute(x, "branch", pairs)


def other_core(x):
    pairs = [(index_of(y, z, c), index_of(y, z, c + 1)) for y, z, c in every()]
    return lax.ppermute(x, "branch", pairs)


def along_head(x, step):
    pairs = [(i, (i + step) % NHEAD) for i in range(NHEAD)]
    return lax.ppermute(x, "head", pairs)


def swap_z(x):
    groups = [[index_of(y, z, c) for z in range(NZ)] for y in range(NY) for c in range(NC)]
    return lax.all_to_all(x, "branch", 0, 0, axis_index_groups=groups, tiled=False)


def swap_yz(x):
    groups = [[index_of(y, z, c) for y in range(NY) for z in range(NZ)] for c in range(NC)]
    return lax.all_to_all(x, "branch", 0, 0, axis_index_groups=groups, tiled=False)


def call(body, outs, scratch=(), vmem_mb=32):
    return dict(
        out_shape=outs,
        scratch_shapes=list(scratch),
        compiler_params=pltpu.CompilerParams(vmem_limit_bytes=vmem_mb << 20),
    )


def in_vmem():
    return pl.BlockSpec(memory_space=VMEM)


def place():
    b = lax.axis_index("branch")
    return b // (NZ * NC), (b // NC) % NZ, b % NC


LINE = 0
DEAL = 8
BACK = 16
HOLD = 24
INNER = 32
SELF = 40
WORDS = 48


def pack_rows(x, base, first, count):
    row = lax.broadcasted_iota(jnp.int32, (8, LANES), 0)
    weight = jnp.zeros((8, LANES), F32)
    for i in range(count):
        weight = jnp.where(row == first + i, float(base**i), weight)
    return jnp.sum(x * weight, axis=0, keepdims=True)


def plan_kernel(mine, other, picked, table, scale):
    y, z, c = place()
    meta_m = mine[...].astype(F32)[:, 16:24, :]
    meta_o = other[...].astype(F32)[:, 16:24, :]
    row = lax.broadcasted_iota(jnp.int32, (8, LANES), 0)
    row_f = row.astype(F32)
    lane = lax.broadcasted_iota(jnp.int32, (8, LANES), 1)
    lane_f = lane.astype(F32)
    is_block = lane < NBLK
    wide_lane = lax.broadcasted_iota(jnp.int32, (NY * NZ, LANES), 1).astype(F32)
    hit = jnp.maximum(
        jnp.where(meta_m[:, 0, :] == wide_lane, 1.0, 0.0),
        jnp.where(meta_o[:, 0, :] == wide_lane, 1.0, 0.0),
    )
    inner = jnp.max(hit, axis=0, keepdims=True)
    inner = jnp.where(is_block, jnp.broadcast_to(inner, (8, LANES)), 0.0)
    before = (
        lax.broadcasted_iota(jnp.int32, (LANES, LANES), 0)
        < lax.broadcasted_iota(jnp.int32, (LANES, LANES), 1)
    ).astype(F32).astype(BF16)
    rank = lax.dot_general(inner.astype(BF16), before, NN, preferred_element_type=F32)
    slots = jnp.where(inner > 0.0, rank + 1.0, 0.0)

    wanted = (row * 2 + c + 1).astype(F32)
    index = jnp.sum(jnp.where(slots == wanted, lane_f, 0.0), axis=1, keepdims=True)
    index = jnp.broadcast_to(index, (8, LANES))
    low = pack_rows(index, 64, 0, 4).astype(jnp.int32)[0, 0]
    high = pack_rows(index, 64, 4, 4).astype(jnp.int32)[0, 0]
    for s in range(HALF):
        block = ((low if s < 4 else high) >> (6 * (s % 4))) & 63
        at = block >> 1
        piece = jnp.where((block & 1) == c, mine[at].astype(F32), other[at].astype(F32))
        piece = piece[0:16].astype(BF16)
        picked[:, s] = jnp.broadcast_to(piece[None], (NZ, 16, LANES))

    for k in range(NY):
        yy = lax.rem(y + k, NY)
        line = mine[yy * NZ + z].astype(F32)[16:24, :]
        same = (line == lane_f) & is_block
        slot = jnp.sum(jnp.where(same, slots, 0.0), axis=1, keepdims=True)
        slot = jnp.broadcast_to(slot, (8, LANES))
        block = (yy * NZ + z) * NC + c
        own = jnp.sum(jnp.where(lane == block, slots, 0.0), axis=1, keepdims=True)
        own = jnp.broadcast_to(own, (8, LANES))
        depth = jnp.sum(jnp.where(slot > 0.0, 1.0, 0.0), axis=0, keepdims=True)
        entry = jnp.where(row_f == depth, own, slot)
        dealt = jnp.maximum(slot - 1.0, 0.0)
        for half in range(2):
            at = 2 * k + half
            table[DEAL + at : DEAL + at + 1, :] = pack_rows(dealt, 16, 4 * half, 4).astype(jnp.int32)
            table[BACK + at : BACK + at + 1, :] = pack_rows(entry, 32, 4 * half, 4).astype(jnp.int32)
        if k == 0:
            table[LINE : LINE + 8, :] = slot.astype(jnp.int32)
            table[INNER : INNER + 8, :] = own.astype(jnp.int32)
            table[SELF : SELF + 8, :] = jnp.where(row_f == depth, own, 0.0).astype(jnp.int32)
    for i in range(6):
        word = jnp.zeros((8, 1), F32)
        for j in range(3):
            held = jnp.where(slots == float(3 * i + j + 1), lane_f + 1.0, 0.0)
            word = word + jnp.sum(held, axis=1, keepdims=True) * float(128**j)
        table[HOLD + i : HOLD + i + 1, :] = jnp.broadcast_to(word, (8, LANES)).astype(jnp.int32)[0:1]

    here = mine[y * NZ + z].astype(F32)[16:24, :]
    group, reward = here[0:1, :], here[1:2, :]
    in_m = jnp.where(meta_m[:, 0, :] == group, meta_m[:, 1, :], 0.0)
    in_o = jnp.where(meta_o[:, 0, :] == group, meta_o[:, 1, :], 0.0)
    total = jnp.sum(in_m + in_o, axis=0, keepdims=True)
    squares = jnp.sum(in_m * in_m + in_o * in_o, axis=0, keepdims=True)
    mean = total / GROUP
    spread = jnp.sqrt(jnp.maximum(squares / GROUP - mean * mean, 0.25))
    advantage = (reward - mean) / spread
    advantage = jnp.sum(jnp.where(lane[0:1] == NBLK, advantage, 0.0), axis=1, keepdims=True)
    scale[...] = jnp.broadcast_to(advantage, (8, LANES))


def plan(mine, other):
    return pl.pallas_call(
        plan_kernel,
        in_specs=[in_vmem()] * 2,
        out_specs=(in_vmem(),) * 3,
        **call(
            plan_kernel,
            (
                jax.ShapeDtypeStruct((NZ, HALF, 16, LANES), BF16),
                jax.ShapeDtypeStruct((WORDS, LANES), jnp.int32),
                jax.ShapeDtypeStruct((8, LANES), F32),
            ),
        ),
        name="plan",
    )(mine, other)


def deal_kernel(table, mine, other, *outs):
    c = place()[2]
    words = table[DEAL : DEAL + 8, :]
    for k in range(NY):
        for d in range(DEPTH):
            slot = (words[2 * k + d // 4, 0] >> (4 * (d % 4))) & 15
            at = slot >> 1
            outs[k][d] = jnp.where((slot & 1) == c, mine[:, at], other[:, at])


def deal(table, mine, other):
    return pl.pallas_call(
        deal_kernel,
        in_specs=[in_vmem()] * 3,
        out_specs=(in_vmem(),) * NY,
        **call(deal_kernel, (jax.ShapeDtypeStruct((DEPTH, NZ, 16, LANES), BF16),) * NY),
        name="deal",
    )(table, mine, other)


def prepare_kernel(scale, queries, cotangent, q_all, g_all):
    weight = scale[0:1, :]
    for h in range(KV):
        heads = slice(RATIO * h, RATIO * (h + 1))
        q_all[h] = queries[...].astype(F32)[:, heads, :].reshape(ROWS, HD).astype(BF16)
        g_all[h] = (
            (cotangent[...].astype(F32)[:, heads, :] * weight[None]).reshape(ROWS, HD).astype(BF16)
        )


def prepare(scale, queries, cotangent):
    return pl.pallas_call(
        prepare_kernel,
        in_specs=[in_vmem()] * 3,
        out_specs=(in_vmem(),) * 2,
        **call(prepare_kernel, (jax.ShapeDtypeStruct((KV, ROWS, HD), BF16),) * 2),
        cost_estimate=pl.CostEstimate(flops=10**6, bytes_accessed=2**20, transcendentals=0),
        name="prepare",
    )(scale, queries, cotangent)


def rows_of(part, kind, h):
    at = kind * KINDS + 2 * h
    return part[:, at : at + 2].reshape(PART, HD)


def one_part(h, keys, values, q, g, mask, exps, pgs, stats, at):
    s = lax.dot_general(keys, q, NT, preferred_element_type=F32) * (
        math.log2(math.e) / math.sqrt(HD)
    )
    s = mask(s)
    top = jnp.max(s, axis=0, keepdims=True)
    e = jnp.exp2(s - top)
    pg = lax.dot_general(values, g, NT, preferred_element_type=F32)
    exps[h] = e
    pgs[h] = pg
    stats[h, at : at + 1, :] = top
    stats[h, at + 1 : at + 2, :] = jnp.sum(e, axis=0, keepdims=True)
    stats[h, at + 2 : at + 3, :] = jnp.sum(e * pg, axis=0, keepdims=True)


def causal(s):
    key_pos = lax.broadcasted_iota(jnp.int32, s.shape, 0)
    query_pos = lax.broadcasted_iota(jnp.int32, s.shape, 1) // RATIO
    return jnp.where(key_pos <= query_pos, s, -1e30)


def listed(table):
    def mask(s):
        parts = []
        for d in range(DEPTH):
            seen = jnp.concatenate([table[LINE + d : LINE + d + 1, :]] * (ROWS // LANES), 1) > 0
            parts.append(jnp.where(seen, s[32 * d : 32 * d + 32], -1e30))
        return jnp.concatenate(parts, 0)

    return mask


def scores_kernel(table, q_all, g_all, part, after, exps, pgs, stats):
    for h in range(KV):
        keys, values = rows_of(part, 0, h), rows_of(part, 1, h)
        one_part(h, keys, values, q_all[h], g_all[h], listed(table), exps, pgs, stats, 0)


def first_scores_kernel(
    table, q_all, g_all, part, own_kv, exps, pgs, stats, own_exps, own_pgs
):
    for h in range(KV):
        keys, values = rows_of(part, 0, h), rows_of(part, 1, h)
        one_part(h, keys, values, q_all[h], g_all[h], listed(table), exps, pgs, stats, 0)
        one_part(
            h, own_kv[h], own_kv[KV + h], q_all[h], g_all[h], causal, own_exps, own_pgs, stats, 4
        )


def wide(keys):
    return jax.ShapeDtypeStruct((KV, keys, ROWS), F32)


def scores_of(table, q_all, g_all, part, after):
    return pl.pallas_call(
        scores_kernel,
        in_specs=[in_vmem()] * 4 + [pl.BlockSpec(memory_space=pl.ANY)],
        out_specs=(in_vmem(),) * 3,
        **call(
            scores_kernel,
            (wide(PART), wide(PART), jax.ShapeDtypeStruct((KV, 8, ROWS), F32)),
            vmem_mb=16,
        ),
        cost_estimate=cost(PART, 2),
        name="scores",
    )(table, q_all, g_all, part, after)


def first_scores_of(table, q_all, g_all, part, own_kv):
    return pl.pallas_call(
        first_scores_kernel,
        in_specs=[in_vmem()] * 5,
        out_specs=(in_vmem(),) * 5,
        **call(
            first_scores_kernel,
            (wide(PART), wide(PART), jax.ShapeDtypeStruct((KV, 8, ROWS), F32), wide(TOK), wide(TOK)),
            vmem_mb=16,
        ),
        cost_estimate=cost(PART + TOK, 2),
        name="scores_first",
    )(table, q_all, g_all, part, own_kv)


def cost(keys, products):
    return pl.CostEstimate(
        flops=2 * products * KV * ROWS * keys * HD,
        bytes_accessed=8 * KV * ROWS * keys,
        transcendentals=KV * ROWS * keys,
    )


def merge(h, stats):
    rows = [(ref, 0) for ref in stats] + [(stats[0], 4)]
    tops = [ref[h, at : at + 1, :] for ref, at in rows]
    top = tops[0]
    for t in tops[1:]:
        top = jnp.maximum(top, t)
    shares = [jnp.exp2(t - top) for t in tops]
    norm = sum(s * ref[h, at + 1 : at + 2, :] for s, (ref, at) in zip(shares, rows))
    norm = 1.0 / norm
    shares = [s * norm for s in shares]
    delta = sum(s * ref[h, at + 2 : at + 3, :] for s, (ref, at) in zip(shares, rows))
    return shares, delta


def one_grad(h, e, pg, share, delta, q, g, keys):
    p = e * share
    low = p.astype(BF16)
    ds = (p * (pg - delta)).astype(BF16)
    factor = 1.0 / math.sqrt(HD)
    dv = lax.dot_general(low, g, NN, preferred_element_type=F32)
    dk = lax.dot_general(ds, q, NN, preferred_element_type=F32) * factor
    turned = keys.astype(F32).T.astype(BF16)
    dq = lax.dot_general(turned, ds, NN, preferred_element_type=F32)
    return dq, dk, dv


def part_grad(k, h, table, stats, exps, pgs, q_all, g_all, part, own_grad, contrib):
    shares, delta = merge(h, stats)
    dq, dk, dv = one_grad(
        h, exps[h], pgs[h], shares[k], delta, q_all[h], g_all[h], rows_of(part, 0, h)
    )
    piece = lax.rem(place()[0] + NY - k, NY)
    for kind, grad in enumerate((dk, dv)):
        at = kind * KINDS + 2 * h
        own = [
            own_grad[kind * KV + h, pl.ds(pl.multiple_of(half * 64 + piece * 16, 16), 16), :]
            for half in range(2)
        ]
        own = jnp.concatenate(own, 0)
        for d in range(DEPTH):
            mark = table[SELF + d : SELF + d + 1, :] > 0
            both = jnp.where(mark, own, grad[32 * d : 32 * d + 32])
            contrib[d, at : at + 2] = both.astype(BF16).reshape(2, 16, HD)
    return dq


def first_grads_kernel(
    k, table, s0, s1, s2, s3, exps, pgs, q_all, g_all, part, own_exps, own_pgs, own_kv,
    dq_sum, own_grad, contrib,
):
    stats = (s0, s1, s2, s3)
    for h in range(KV):
        shares, delta = merge(h, stats)
        dq, dk, dv = one_grad(
            h, own_exps[h], own_pgs[h], shares[NY], delta, q_all[h], g_all[h], own_kv[h]
        )
        own_grad[h] = dk
        own_grad[KV + h] = dv
        dq_sum[h] = dq + part_grad(
            k, h, table, stats, exps, pgs, q_all, g_all, part, own_grad, contrib
        )


def grads_kernel(
    k, table, s0, s1, s2, s3, exps, pgs, q_all, g_all, part, own_grad, dq_in, dq_sum, contrib
):
    for h in range(KV):
        dq_sum[h] = dq_in[h] + part_grad(
            k, h, table, (s0, s1, s2, s3), exps, pgs, q_all, g_all, part, own_grad, contrib
        )


def last_grads_kernel(
    k, table, s0, s1, s2, s3, exps, pgs, q_all, g_all, part, own_grad, dq_in,
    query_grad, contrib, squares,
):
    total = jnp.zeros((8, HD), F32)
    for h in range(KV):
        dq = dq_in[h] + part_grad(
            k, h, table, (s0, s1, s2, s3), exps, pgs, q_all, g_all, part, own_grad, contrib
        )
        dq = dq.T * (1.0 / math.sqrt(HD))
        total = total + jnp.sum((dq * dq).reshape(ROWS // 8, 8, HD), axis=0)
        query_grad[:, RATIO * h : RATIO * (h + 1), :] = dq.reshape(TOK, RATIO, HD)
    own = own_grad[...]
    own_squares = jnp.sum((own * own).reshape(2 * KV * TOK // 8, 8, HD), axis=0)
    squares[...] = total + jnp.where(table[INNER : INNER + 8, :] > 0, 0.0, own_squares)


DQ_SUM = (KV, HD, TOK * RATIO)
OWN = (2 * KV, TOK, HD)
CONTRIB = (DEPTH, NZ, 16, LANES)


def grads_of(body, name, outs, k, *arrays):
    return pl.pallas_call(
        functools.partial(body, k),
        in_specs=[in_vmem()] * len(arrays),
        out_specs=(in_vmem(),) * len(outs),
        **call(body, outs, vmem_mb=16),
        cost_estimate=pl.CostEstimate(flops=1000, bytes_accessed=1000, transcendentals=0),
        name=name,
    )(*arrays)


def attend(table, scale, queries, cotangent, own_kv, parts):
    q_all, g_all = prepare(scale, queries, cotangent)
    e, pg, st = [None] * NY, [None] * NY, [None] * NY
    e[0], pg[0], st[0], own_e, own_pg = first_scores_of(table, q_all, g_all, parts[0], own_kv)
    after = st[0]
    for k in (1, 2, 3):
        e[k], pg[k], st[k] = scores_of(table, q_all, g_all, parts[k], after)
        after = st[k]
    back = [None] * NY
    dq_type = jax.ShapeDtypeStruct(DQ_SUM, F32)
    own_type = jax.ShapeDtypeStruct(OWN, F32)
    contrib_type = jax.ShapeDtypeStruct(CONTRIB, BF16)
    for k in (2, 1, 3, 0):
        shared = (table, *st, e[k], pg[k], q_all, g_all, parts[k])
        if k == 2:
            dq, own_grad, back[k] = grads_of(
                first_grads_kernel, "grads_first", (dq_type, own_type, contrib_type), k,
                *shared, own_e, own_pg, own_kv,
            )
        elif k:
            dq, back[k] = grads_of(
                grads_kernel, "grads", (dq_type, contrib_type), k, *shared, own_grad, dq
            )
        else:
            query_grad, back[k], squares = grads_of(
                last_grads_kernel, "grads_last",
                (
                    jax.ShapeDtypeStruct((TOK, KV * RATIO, HD), F32),
                    contrib_type,
                    jax.ShapeDtypeStruct((8, LANES), F32),
                ),
                k, *shared, own_grad, dq,
            )
    return query_grad, own_grad, *back, squares


def add_part(k, table, part, acc):
    words = table[BACK + 2 * k : BACK + 2 * k + 2, :]
    for d in range(DEPTH):
        slot = (words[d // 4, 0] >> (5 * (d % 4))) & 31
        at = jnp.maximum(slot - 1, 0)
        acc[at & 1, at >> 1] += jnp.where(slot > 0, part[d].astype(F32), 0.0)


def combine_first_kernel(table, part, acc):
    acc[...] = jnp.zeros_like(acc)
    add_part(1, table, part, acc)


def combine_kernel(table, part, acc_in, acc):
    add_part(2, table, part, acc)


def combine_last_kernel(table, part, part_here, acc_in, keep, send, acc):
    c = place()[2]
    add_part(0, table, part_here, acc)
    add_part(3, table, part, acc)
    for s in range(HALF):
        send[:, s] = acc[1 - c, s].astype(BF16)
        keep[:, s] = acc[c, s]


def combine(table, parts):
    acc_type = jax.ShapeDtypeStruct((2, HALF, NZ, 16, LANES), F32)
    small = pl.CostEstimate(flops=1000, bytes_accessed=1000, transcendentals=0)
    acc = pl.pallas_call(
        combine_first_kernel,
        in_specs=[in_vmem()] * 2,
        out_specs=in_vmem(),
        **call(combine_first_kernel, acc_type, vmem_mb=16),
        cost_estimate=small,
        name="combine_first",
    )(table, parts[1])
    acc = pl.pallas_call(
        combine_kernel,
        in_specs=[in_vmem()] * 3,
        out_specs=in_vmem(),
        input_output_aliases={2: 0},
        **call(combine_kernel, acc_type, vmem_mb=16),
        cost_estimate=small,
        name="combine",
    )(table, parts[2], acc)
    keep, send, _ = pl.pallas_call(
        combine_last_kernel,
        in_specs=[in_vmem()] * 4,
        out_specs=(in_vmem(),) * 3,
        input_output_aliases={3: 2},
        **call(
            combine_last_kernel,
            (
                jax.ShapeDtypeStruct((NZ, HALF, 16, LANES), F32),
                jax.ShapeDtypeStruct((NZ, HALF, 16, LANES), BF16),
                acc_type,
            ),
            vmem_mb=16,
        ),
        cost_estimate=small,
        name="combine_last",
    )(table, parts[3], parts[0], acc)
    return keep, send


def split_rows(value, rows):
    high = value.astype(BF16).astype(F32)
    middle = (value - high).astype(BF16).astype(F32)
    low = value - high - middle
    row = lax.broadcasted_iota(jnp.int32, (8, LANES), 0)
    tile = jnp.where(row == 0, high, jnp.where(row == 1, middle, jnp.where(row == 2, low, 0.0)))
    if rows > 8:
        tile = jnp.concatenate([tile, jnp.zeros((rows - 8, LANES), F32)], 0)
    return tile


def total_kernel(parts, squares, sums, pack):
    sums_now = parts[0].astype(F32)
    for z in range(1, NZ):
        sums_now = sums_now + parts[z].astype(F32)
    pack[0:HALF] = sums_now.astype(BF16)
    tile = squares[...] + jnp.sum((sums_now * sums_now).reshape(HALF * 2, 8, LANES), axis=0)
    value = jnp.broadcast_to(jnp.sum(tile, axis=0, keepdims=True), (8, LANES))
    sums[...] = value
    pack[HALF] = split_rows(value, 16).astype(BF16)


def total_of(parts, squares):
    return pl.pallas_call(
        total_kernel,
        in_specs=[in_vmem()] * 2,
        out_specs=(in_vmem(), in_vmem()),
        **call(
            total_kernel,
            (
                jax.ShapeDtypeStruct((8, LANES), F32),
                jax.ShapeDtypeStruct((HALF + 1, 16, LANES), BF16),
            ),
        ),
        name="total",
    )(parts, squares)


def route_kernel(table, sums, mine, other, out):
    c = place()[2]
    words = table[HOLD : HOLD + 8, :]
    tail = other[HALF].astype(F32)[0:8, :]
    value = sums[...] + jnp.sum(tail, axis=0, keepdims=True)
    blank = jnp.concatenate([jnp.zeros((16, LANES), F32), split_rows(value, 8)], 0)
    out[...] = jnp.broadcast_to(blank.astype(BF16)[None], (NY * NZ, 24, LANES))
    for s in range(2 * HALF):
        block = ((words[s // 3, 0] >> (7 * (s % 3))) & 127) - 1
        piece = jnp.where((s % 2) == c, mine[s // 2], other[s // 2])

        @pl.when((block >= 0) & ((block & 1) == c))
        def _():
            out[block >> 1, 0:16, :] = piece


def route(table, sums, mine, other):
    return pl.pallas_call(
        route_kernel,
        in_specs=[in_vmem()] * 4,
        out_specs=in_vmem(),
        **call(route_kernel, jax.ShapeDtypeStruct((NY * NZ, 24, LANES), BF16)),
        name="route",
    )(table, sums, mine, other)


def tally_kernel(arrived, sums):
    tails = jnp.sum(arrived[...].astype(F32)[:, 16:24, :], axis=0)
    tails = jnp.sum(jnp.sum(tails, axis=0, keepdims=True), axis=1, keepdims=True)
    sums[...] = jnp.broadcast_to(tails, (1, LANES))


def tally(arrived):
    return pl.pallas_call(
        tally_kernel,
        in_specs=[in_vmem()],
        out_specs=in_vmem(),
        **call(tally_kernel, jax.ShapeDtypeStruct((1, LANES), F32)),
        name="tally",
    )(arrived)


def finish_kernel(table, arrived, own_grad, key_grad, value_grad):
    inner = table[INNER : INNER + 1, :] > 0
    for z in range(NZ):
        kind, h, half = z // 4, z // 2 % 2, z % 2
        out = value_grad if kind else key_grad
        for y in range(NY):
            at = half * 64 + y * 16
            piece = arrived[y * NZ + z].astype(F32)[0:16, :]
            own = own_grad[kind * KV + h, at : at + 16, :]
            out[at : at + 16, h, :] = jnp.where(inner, piece, own)


def finish(table, arrived, own_grad):
    return pl.pallas_call(
        finish_kernel,
        in_specs=[in_vmem()] * 3,
        out_specs=(in_vmem(),) * 2,
        **call(finish_kernel, (jax.ShapeDtypeStruct((TOK, KV, HD), F32),) * 2),
        cost_estimate=pl.CostEstimate(flops=1000, bytes_accessed=1000, transcendentals=0),
        name="finish",
    )(table, arrived, own_grad)


def local(queries, keys, values, cotangent, rewards, groups, ancestors, step_ids):
    own_kv = jnp.stack([keys, values]).transpose(0, 2, 1, 3)
    pieces = (
        own_kv.reshape(2, KV, 2, NY, 16, HD).transpose(3, 0, 1, 2, 4, 5).reshape(NY * NZ, 16, HD)
    )
    own_kv = own_kv.reshape(2 * KV, TOK, HD)
    line = jnp.broadcast_to(ancestors[0].astype(BF16)[:, None], (8, NBLK))
    facts = jnp.concatenate(
        [groups.astype(BF16), rewards, jnp.zeros((6,), BF16)]
    )
    meta = jnp.concatenate([line, jnp.broadcast_to(facts[:, None], (8, LANES - NBLK))], 1)
    packet = jnp.concatenate([pieces, jnp.broadcast_to(meta[None], (NY * NZ, 8, LANES))], 1)
    mine = swap_yz(packet)
    other = other_core(mine)
    trained = (step_ids[0] % 2 == 0)[:, None, None]
    masked = jnp.where(trained, cotangent, jnp.zeros_like(cotangent))
    picked, table, scale = plan(mine, other)
    column = swap_z(picked)
    dealt = deal(table, column, other_core(column))
    parts = [dealt[0]] + [along_y(dealt[k], k) for k in (1, 2, 3)]
    query_grad, own_grad, c0, c1, c2, c3, squares = attend(
        table, scale, queries, masked, own_kv, parts
    )
    back = [c0] + [along_y(x, -k) for k, x in ((1, c1), (2, c2), (3, c3))]
    keep, send = combine(table, back)
    halves = (keep + other_core(send).astype(F32)).astype(BF16)
    sums, pack = total_of(swap_z(halves), squares)
    arrived = swap_yz(route(table, sums, pack, other_core(pack)))
    mine_sum = tally(arrived)
    all_sum = mine_sum
    for k in (1, 2, 3):
        all_sum = all_sum + along_head(mine_sum, k)
    key_grad, value_grad = finish(table, arrived, own_grad)
    count = float(NBLK * TOK * NHEAD * (KV * RATIO + 2 * KV) * HD)
    grad_rms = jnp.sqrt(all_sum[0, 0] / count)
    return query_grad, key_grad, value_grad, grad_rms


def solution(mesh):
    in_specs = (
        P("branch", "head", None),
        P("branch", "head", None),
        P("branch", "head", None),
        P("branch", "head", None),
        P("branch"),
        P("branch"),
        P("branch", None),
        P("branch", None),
    )
    out_specs = (
        P("branch", "head", None),
        P("branch", "head", None),
        P("branch", "head", None),
        P(),
    )
    return jax.shard_map(local, mesh=mesh, in_specs=in_specs, out_specs=out_specs, check_vma=False)
```

```python
import functools
import math

import jax
import jax.numpy as jnp
from jax import lax
from jax.experimental import pallas as pl
from jax.experimental.pallas import tpu as pltpu
from jax.sharding import PartitionSpec as P

NY, NZ, NC = 4, 8, 2
NBLK = NY * NZ * NC
NHEAD = 4
GROUP = 4
DEPTH = 8
TOK = 128
HD = 128
KV = 2
RATIO = 8
LANES = 128
HALF = 8
ROWS = TOK * RATIO
QUAD = 4
PART = 32 * DEPTH
HAND = (DEPTH, QUAD, 16, LANES)
F32 = jnp.float32
BF16 = jnp.bfloat16
VMEM = pltpu.VMEM
NT = (((1,), (1,)), ((), ()))
NN = (((1,), (0,)), ((), ()))
TN = (((0,), (0,)), ((), ()))


def index_of(y, z, c):
    return ((y % NY) * NZ + z % NZ) * NC + c % NC


def every():
    return [(y, z, c) for y in range(NY) for z in range(NZ) for c in range(NC)]


def along_y(x, step):
    pairs = [(index_of(y, z, c), index_of(y + step, z, c)) for y, z, c in every()]
    return lax.ppermute(x, "branch", pairs)


def other_core(x):
    pairs = [(index_of(y, z, c), index_of(y, z, c + 1)) for y, z, c in every()]
    return lax.ppermute(x, "branch", pairs)


def along_head(x, step):
    pairs = [(i, (i + step) % NHEAD) for i in range(NHEAD)]
    return lax.ppermute(x, "head", pairs)


def swap_z(x):
    groups = [[index_of(y, z, c) for z in range(NZ)] for y in range(NY) for c in range(NC)]
    return lax.all_to_all(x, "branch", 0, 0, axis_index_groups=groups, tiled=False)


def swap_yz(x):
    groups = [[index_of(y, z, c) for y in range(NY) for z in range(NZ)] for c in range(NC)]
    return lax.all_to_all(x, "branch", 0, 0, axis_index_groups=groups, tiled=False)


def call(body, outs, scratch=(), vmem_mb=32):
    return dict(
        out_shape=outs,
        scratch_shapes=list(scratch),
        compiler_params=pltpu.CompilerParams(vmem_limit_bytes=vmem_mb << 20),
    )


def in_vmem():
    return pl.BlockSpec(memory_space=VMEM)


def place():
    b = lax.axis_index("branch")
    return b // (NZ * NC), (b // NC) % NZ, b % NC


LINE = 0
DEAL = 8
BACK = 16
HOLD = 24
INNER = 32
SELF = 40
WORDS = 48


def packet_kernel(
    keys_far, values_far, ancestors_far, group, reward, packet, own_kv,
    keys, values, ancestors, sems,
):
    pairs = (
        (ancestors_far, ancestors),
        (keys_far, keys),
        (values_far, values),
    )
    copies = [pltpu.make_async_copy(a, b, sems.at[i]) for i, (a, b) in enumerate(pairs)]
    for copy in copies:
        copy.start()
    for copy in copies[:1]:
        copy.wait()
    row = lax.broadcasted_iota(jnp.int32, (8, LANES), 0)
    lane = lax.broadcasted_iota(jnp.int32, (8, LANES), 1)
    spot = lax.broadcasted_iota(jnp.int32, (8, DEPTH), 0) == lax.broadcasted_iota(
        jnp.int32, (8, DEPTH), 1
    )
    line = jnp.broadcast_to(ancestors[...].astype(F32), (8, DEPTH))
    line = jnp.sum(jnp.where(spot, line, 0.0), axis=1, keepdims=True)
    facts = jnp.where(
        row == 0, group[0].astype(F32), jnp.where(row == 1, reward[0].astype(F32), 0.0)
    )
    meta = jnp.where(lane < NBLK, line, facts)
    for copy in copies[1:]:
        copy.wait()
    for h in range(KV):
        own_kv[2 * h] = keys[:, h, :]
        own_kv[2 * h + 1] = values[:, h, :]
    for z in range(NZ):
        for y in range(NY):
            at = (z % 2) * 64 + y * 16
            rows = own_kv[z // 2, at : at + 16, :].astype(F32)
            packet[y * NZ + z] = jnp.concatenate([rows, meta], 0).astype(BF16)


def packet_of(keys, values, ancestors, group, reward):
    return pl.pallas_call(
        packet_kernel,
        in_specs=[pl.BlockSpec(memory_space=pltpu.HBM)] * 3
        + [pl.BlockSpec(memory_space=pltpu.SMEM)] * 2,
        out_specs=(in_vmem(),) * 2,
        **call(
            packet_kernel,
            (
                jax.ShapeDtypeStruct((NY * NZ, 24, LANES), BF16),
                jax.ShapeDtypeStruct((2 * KV, TOK, HD), BF16),
            ),
            [VMEM(x.shape, x.dtype) for x in (keys, values, ancestors)]
            + [pltpu.SemaphoreType.DMA((3,))],
            vmem_mb=62,
        ),
        name="packet",
    )(keys, values, ancestors, group, reward)


def pack_rows(x, base, first, count):
    row = lax.broadcasted_iota(jnp.int32, (8, LANES), 0)
    weight = jnp.zeros((8, LANES), F32)
    for i in range(count):
        weight = jnp.where(row == first + i, float(base**i), weight)
    return jnp.sum(x * weight, axis=0, keepdims=True)


def plan_kernel(mine, other, picked, table, scale):
    y, z, c = place()
    meta_m = mine[...].astype(F32)[:, 16:24, :]
    meta_o = other[...].astype(F32)[:, 16:24, :]
    row = lax.broadcasted_iota(jnp.int32, (8, LANES), 0)
    row_f = row.astype(F32)
    lane = lax.broadcasted_iota(jnp.int32, (8, LANES), 1)
    lane_f = lane.astype(F32)
    is_block = lane < NBLK
    wide_lane = lax.broadcasted_iota(jnp.int32, (NY * NZ, LANES), 1).astype(F32)
    hit = jnp.maximum(
        jnp.where(meta_m[:, 0, :] == wide_lane, 1.0, 0.0),
        jnp.where(meta_o[:, 0, :] == wide_lane, 1.0, 0.0),
    )
    inner = jnp.max(hit, axis=0, keepdims=True)
    inner = jnp.where(is_block, jnp.broadcast_to(inner, (8, LANES)), 0.0)
    before = (
        lax.broadcasted_iota(jnp.int32, (LANES, LANES), 0)
        < lax.broadcasted_iota(jnp.int32, (LANES, LANES), 1)
    ).astype(F32).astype(BF16)
    rank = lax.dot_general(inner.astype(BF16), before, NN, preferred_element_type=F32)
    slots = jnp.where(inner > 0.0, rank + 1.0, 0.0)

    wanted = (row * 2 + c + 1).astype(F32)
    index = jnp.sum(jnp.where(slots == wanted, lane_f, 0.0), axis=1, keepdims=True)
    index = jnp.broadcast_to(index, (8, LANES))
    low = pack_rows(index, 64, 0, 4).astype(jnp.int32)[0, 0]
    high = pack_rows(index, 64, 4, 4).astype(jnp.int32)[0, 0]
    for s in range(HALF):
        block = ((low if s < 4 else high) >> (6 * (s % 4))) & 63
        at = block >> 1
        piece = jnp.where((block & 1) == c, mine[at].astype(F32), other[at].astype(F32))
        piece = piece[0:16].astype(BF16)
        picked[:, s] = jnp.broadcast_to(piece[None], (NZ, 16, LANES))

    for k in range(NY):
        yy = lax.rem(y + k, NY)
        line = mine[yy * NZ + z].astype(F32)[16:24, :]
        same = (line == lane_f) & is_block
        slot = jnp.sum(jnp.where(same, slots, 0.0), axis=1, keepdims=True)
        slot = jnp.broadcast_to(slot, (8, LANES))
        block = (yy * NZ + z) * NC + c
        own = jnp.sum(jnp.where(lane == block, slots, 0.0), axis=1, keepdims=True)
        own = jnp.broadcast_to(own, (8, LANES))
        depth = jnp.sum(jnp.where(slot > 0.0, 1.0, 0.0), axis=0, keepdims=True)
        entry = jnp.where(row_f == depth, own, slot)
        dealt = jnp.maximum(slot - 1.0, 0.0)
        for half in range(2):
            at = 2 * k + half
            table[DEAL + at : DEAL + at + 1, :] = pack_rows(dealt, 16, 4 * half, 4).astype(jnp.int32)
            table[BACK + at : BACK + at + 1, :] = pack_rows(entry, 32, 4 * half, 4).astype(jnp.int32)
        if k == 0:
            table[LINE : LINE + 8, :] = slot.astype(jnp.int32)
            table[INNER : INNER + 8, :] = own.astype(jnp.int32)
            table[SELF : SELF + 8, :] = jnp.where(row_f == depth, own, 0.0).astype(jnp.int32)
    for i in range(6):
        word = jnp.zeros((8, 1), F32)
        for j in range(3):
            held = jnp.where(slots == float(3 * i + j + 1), lane_f + 1.0, 0.0)
            word = word + jnp.sum(held, axis=1, keepdims=True) * float(128**j)
        table[HOLD + i : HOLD + i + 1, :] = jnp.broadcast_to(word, (8, LANES)).astype(jnp.int32)[0:1]

    here = mine[y * NZ + z].astype(F32)[16:24, :]
    group, reward = here[0:1, :], here[1:2, :]
    in_m = jnp.where(meta_m[:, 0, :] == group, meta_m[:, 1, :], 0.0)
    in_o = jnp.where(meta_o[:, 0, :] == group, meta_o[:, 1, :], 0.0)
    total = jnp.sum(in_m + in_o, axis=0, keepdims=True)
    squares = jnp.sum(in_m * in_m + in_o * in_o, axis=0, keepdims=True)
    mean = total / GROUP
    spread = jnp.sqrt(jnp.maximum(squares / GROUP - mean * mean, 0.25))
    advantage = (reward - mean) / spread
    advantage = jnp.sum(jnp.where(lane[0:1] == NBLK, advantage, 0.0), axis=1, keepdims=True)
    scale[...] = jnp.broadcast_to(advantage, (8, LANES))


def plan(mine, other):
    return pl.pallas_call(
        plan_kernel,
        in_specs=[in_vmem()] * 2,
        out_specs=(in_vmem(),) * 3,
        **call(
            plan_kernel,
            (
                jax.ShapeDtypeStruct((NZ, HALF, 16, LANES), BF16),
                jax.ShapeDtypeStruct((WORDS, LANES), jnp.int32),
                jax.ShapeDtypeStruct((8, LANES), F32),
            ),
        ),
        name="plan",
    )(mine, other)


def deal_kernel(h, table, mine, other, after, *outs):
    c = place()[2]
    words = table[DEAL : DEAL + 8, :]
    mine, other = mine.at[QUAD * h : QUAD * (h + 1)], other.at[QUAD * h : QUAD * (h + 1)]
    for k in range(NY):
        for d in range(DEPTH):
            slot = (words[2 * k + d // 4, 0] >> (4 * (d % 4))) & 15
            at = slot >> 1
            outs[k][d] = jnp.where((slot & 1) == c, mine[:, at], other[:, at])


def deal(h, table, mine, other, after):
    return pl.pallas_call(
        functools.partial(deal_kernel, h),
        in_specs=[in_vmem()] * 3 + [pl.BlockSpec(memory_space=pl.ANY)],
        out_specs=(in_vmem(),) * NY,
        **call(deal_kernel, (jax.ShapeDtypeStruct(HAND, BF16),) * NY),
        name="deal",
    )(table, mine, other, after)


def prepare_kernel(scale, queries, cotangent, q_all, g_all):
    weight = scale[0:1, :]
    for h in range(KV):
        heads = slice(RATIO * h, RATIO * (h + 1))
        q_all[h] = queries[...].astype(F32)[:, heads, :].reshape(ROWS, HD).astype(BF16)
        g_all[h] = (
            (cotangent[...].astype(F32)[:, heads, :] * weight[None]).reshape(ROWS, HD).astype(BF16)
        )


def prepare(scale, queries, cotangent):
    return pl.pallas_call(
        prepare_kernel,
        in_specs=[in_vmem()] * 3,
        out_specs=(in_vmem(),) * 2,
        **call(prepare_kernel, (jax.ShapeDtypeStruct((KV, ROWS, HD), BF16),) * 2),
        cost_estimate=pl.CostEstimate(flops=10**6, bytes_accessed=2**20, transcendentals=0),
        name="prepare",
    )(scale, queries, cotangent)


def rows_of(part, kind):
    return part[:, 2 * kind : 2 * kind + 2].reshape(PART, HD)


def one_part(keys, values, q, g, mask, exps, pgs, stats, at):
    s = lax.dot_general(keys, q, NT, preferred_element_type=F32) * (
        math.log2(math.e) / math.sqrt(HD)
    )
    s = mask(s)
    top = jnp.max(s, axis=0, keepdims=True)
    e = jnp.exp2(s - top)
    pg = lax.dot_general(values, g, NT, preferred_element_type=F32)
    exps[...] = e
    pgs[...] = pg
    stats[at : at + 1, :] = top
    stats[at + 1 : at + 2, :] = jnp.sum(e, axis=0, keepdims=True)
    stats[at + 2 : at + 3, :] = jnp.sum(e * pg, axis=0, keepdims=True)


def causal(s):
    key_pos = lax.broadcasted_iota(jnp.int32, s.shape, 0)
    query_pos = lax.broadcasted_iota(jnp.int32, s.shape, 1) // RATIO
    return jnp.where(key_pos <= query_pos, s, -1e30)


def listed(table):
    def mask(s):
        parts = []
        for d in range(DEPTH):
            seen = jnp.concatenate([table[LINE + d : LINE + d + 1, :]] * (ROWS // LANES), 1) > 0
            parts.append(jnp.where(seen, s[32 * d : 32 * d + 32], -1e30))
        return jnp.concatenate(parts, 0)

    return mask


def scores_kernel(h, table, q_all, g_all, part, after, exps, pgs, stats):
    keys, values = rows_of(part, 0), rows_of(part, 1)
    one_part(keys, values, q_all[h], g_all[h], listed(table), exps, pgs, stats, 0)


def first_scores_kernel(h, table, q_all, g_all, part, own_kv, exps, pgs, stats, own_exps, own_pgs):
    keys, values = rows_of(part, 0), rows_of(part, 1)
    q, g = q_all[h], g_all[h]
    one_part(keys, values, q, g, listed(table), exps, pgs, stats, 0)
    one_part(own_kv[2 * h], own_kv[2 * h + 1], q, g, causal, own_exps, own_pgs, stats, 4)


def wide(keys):
    return jax.ShapeDtypeStruct((keys, ROWS), F32)


STATS = jax.ShapeDtypeStruct((8, TOK * RATIO), F32)


def scores_of(h, table, q_all, g_all, part, after):
    return pl.pallas_call(
        functools.partial(scores_kernel, h),
        in_specs=[in_vmem()] * 4 + [pl.BlockSpec(memory_space=pl.ANY)],
        out_specs=(in_vmem(),) * 3,
        **call(scores_kernel, (wide(PART), wide(PART), STATS), vmem_mb=16),
        cost_estimate=cost(PART, 2),
        name="scores",
    )(table, q_all, g_all, part, after)


def first_scores_of(h, table, q_all, g_all, part, own_kv):
    return pl.pallas_call(
        functools.partial(first_scores_kernel, h),
        in_specs=[in_vmem()] * 5,
        out_specs=(in_vmem(),) * 5,
        **call(
            first_scores_kernel,
            (wide(PART), wide(PART), STATS, wide(TOK), wide(TOK)),
            vmem_mb=16,
        ),
        cost_estimate=cost(PART + TOK, 2),
        name="scores_first",
    )(table, q_all, g_all, part, own_kv)


def cost(keys, products):
    return pl.CostEstimate(
        flops=2 * products * ROWS * keys * HD,
        bytes_accessed=8 * ROWS * keys,
        transcendentals=ROWS * keys,
    )


SMALL = pl.CostEstimate(flops=1000, bytes_accessed=1000, transcendentals=0)


def merge(stats):
    rows = [(ref, 0) for ref in stats] + [(stats[0], 4)]
    tops = [ref[at : at + 1, :] for ref, at in rows]
    top = tops[0]
    for t in tops[1:]:
        top = jnp.maximum(top, t)
    shares = [jnp.exp2(t - top) for t in tops]
    norm = sum(s * ref[at + 1 : at + 2, :] for s, (ref, at) in zip(shares, rows))
    norm = 1.0 / norm
    shares = [s * norm for s in shares]
    delta = sum(s * ref[at + 2 : at + 3, :] for s, (ref, at) in zip(shares, rows))
    return shares, delta


def one_grad(e, pg, share, delta, q, g, keys):
    p = e * share
    low = p.astype(BF16)
    ds = (p * (pg - delta)).astype(BF16)
    factor = 1.0 / math.sqrt(HD)
    dv = lax.dot_general(low, g, NN, preferred_element_type=F32)
    dk = lax.dot_general(ds, q, NN, preferred_element_type=F32) * factor
    turned = keys.astype(F32).T.astype(BF16)
    dq = lax.dot_general(turned, ds, NN, preferred_element_type=F32)
    return dq, dk, dv


def part_grad(k, h, table, stats, exps, pgs, q_all, g_all, part, own_grad, contrib):
    shares, delta = merge(stats)
    dq, dk, dv = one_grad(
        exps[...], pgs[...], shares[k], delta, q_all[h], g_all[h], rows_of(part, 0)
    )
    piece = lax.rem(place()[0] + NY - k, NY)
    for kind, grad in enumerate((dk, dv)):
        own = [
            own_grad[kind, pl.ds(pl.multiple_of(half * 64 + piece * 16, 16), 16), :]
            for half in range(2)
        ]
        own = jnp.concatenate(own, 0)
        for d in range(DEPTH):
            mark = table[SELF + d : SELF + d + 1, :] > 0
            both = jnp.where(mark, own, grad[32 * d : 32 * d + 32])
            contrib[d, 2 * kind : 2 * kind + 2] = both.astype(BF16).reshape(2, 16, HD)
    return dq


def first_grads_kernel(
    k, h, table, s0, s1, s2, s3, exps, pgs, q_all, g_all, part, own_exps, own_pgs, own_kv,
    dq_sum, own_grad, contrib,
):
    stats = (s0, s1, s2, s3)
    shares, delta = merge(stats)
    dq, dk, dv = one_grad(
        own_exps[...], own_pgs[...], shares[NY], delta, q_all[h], g_all[h], own_kv[2 * h]
    )
    own_grad[0] = dk
    own_grad[1] = dv
    dq_sum[...] = dq + part_grad(
        k, h, table, stats, exps, pgs, q_all, g_all, part, own_grad, contrib
    )


def grads_kernel(
    k, h, table, s0, s1, s2, s3, exps, pgs, q_all, g_all, part, own_grad, dq_in, *outs
):
    dq_sum, contrib = outs[-2:]
    dq_sum[...] = dq_in[...] + part_grad(
        k, h, table, (s0, s1, s2, s3), exps, pgs, q_all, g_all, part, own_grad, contrib
    )


def emit_kernel(table, dq_0, dq_1, own_0, own_1, query_grad, squares):
    total = jnp.zeros((8, HD), F32)
    own_total = jnp.zeros((8, HD), F32)
    for h, (dq, own) in enumerate(((dq_0, own_0), (dq_1, own_1))):
        dq = dq[...].T * (1.0 / math.sqrt(HD))
        total = total + jnp.sum((dq * dq).reshape(ROWS // 8, 8, HD), axis=0)
        query_grad[:, RATIO * h : RATIO * (h + 1), :] = dq.reshape(TOK, RATIO, HD)
        own = own[...]
        own_total = own_total + jnp.sum((own * own).reshape(2 * TOK // 8, 8, HD), axis=0)
    squares[...] = total + jnp.where(table[INNER : INNER + 8, :] > 0, 0.0, own_total)


def emit(table, dqs, owns):
    return pl.pallas_call(
        emit_kernel,
        in_specs=[in_vmem()] * 5,
        out_specs=(in_vmem(),) * 2,
        **call(
            emit_kernel,
            (
                jax.ShapeDtypeStruct((TOK, KV * RATIO, HD), F32),
                jax.ShapeDtypeStruct((8, LANES), F32),
            ),
            vmem_mb=16,
        ),
        cost_estimate=SMALL,
        name="emit",
    )(table, *dqs, *owns)


def grads_of(body, name, outs, k, h, *arrays):
    return pl.pallas_call(
        functools.partial(body, k, h),
        in_specs=[in_vmem()] * len(arrays),
        out_specs=(in_vmem(),) * len(outs),
        **call(body, outs, vmem_mb=16),
        cost_estimate=SMALL,
        name=name,
    )(*arrays)


def attend(h, table, q_all, g_all, own_kv, parts, after):
    e, pg, st = [None] * NY, [None] * NY, [None] * NY
    e[0], pg[0], st[0], own_e, own_pg = first_scores_of(h, table, q_all, g_all, parts[0], own_kv)
    after = st[0] if after is None else after
    for k in (1, 2, 3):
        e[k], pg[k], st[k] = scores_of(h, table, q_all, g_all, parts[k], after)
        after = st[k]
    back = [None] * NY
    dq_type = jax.ShapeDtypeStruct((HD, ROWS), F32)
    own_type = jax.ShapeDtypeStruct((2, TOK, HD), F32)
    contrib_type = jax.ShapeDtypeStruct(HAND, BF16)

    def shared(k):
        return (table, *st, e[k], pg[k], q_all, g_all, parts[k])

    dq, own_grad, back[2] = grads_of(
        first_grads_kernel, "grads_first", (dq_type, own_type, contrib_type), 2, h,
        *shared(2), own_e, own_pg, own_kv,
    )
    for k in (1, 3):
        dq, back[k] = grads_of(
            grads_kernel, "grads", (dq_type, contrib_type), k, h, *shared(k), own_grad, dq
        )

    def last(after):
        return grads_of(
            grads_kernel, "grads_last", (dq_type, contrib_type), 0, h, *shared(0), own_grad, dq, after
        )

    return dq, own_grad, back, last


def add_part(k, table, part, acc):
    words = table[BACK + 2 * k : BACK + 2 * k + 2, :]
    for d in range(DEPTH):
        slot = (words[d // 4, 0] >> (5 * (d % 4))) & 31
        at = jnp.maximum(slot - 1, 0)
        acc[at & 1, at >> 1] += jnp.where(slot > 0, part[d].astype(F32), 0.0)


def combine_first_kernel(table, part, after, acc):
    acc[...] = jnp.zeros_like(acc)
    add_part(1, table, part, acc)


def combine_kernel(table, part, acc_in, acc):
    add_part(2, table, part, acc)


def combine_last_kernel(table, part, part_here, acc_in, keep, send, acc):
    c = place()[2]
    add_part(0, table, part_here, acc)
    add_part(3, table, part, acc)
    for s in range(HALF):
        send[:, s] = acc[1 - c, s].astype(BF16)
        keep[:, s] = acc[c, s]


def combine(table, parts, after):
    acc_type = jax.ShapeDtypeStruct((2, HALF, QUAD, 16, LANES), F32)
    acc = pl.pallas_call(
        combine_first_kernel,
        in_specs=[in_vmem()] * 2 + [pl.BlockSpec(memory_space=pl.ANY)],
        out_specs=in_vmem(),
        **call(combine_first_kernel, acc_type, vmem_mb=16),
        cost_estimate=SMALL,
        name="combine_first",
    )(table, parts[1], after)
    acc = pl.pallas_call(
        combine_kernel,
        in_specs=[in_vmem()] * 3,
        out_specs=in_vmem(),
        input_output_aliases={2: 0},
        **call(combine_kernel, acc_type, vmem_mb=16),
        cost_estimate=SMALL,
        name="combine",
    )(table, parts[2], acc)
    keep, send, _ = pl.pallas_call(
        combine_last_kernel,
        in_specs=[in_vmem()] * 4,
        out_specs=(in_vmem(),) * 3,
        input_output_aliases={3: 2},
        **call(
            combine_last_kernel,
            (
                jax.ShapeDtypeStruct((QUAD, HALF, 16, LANES), F32),
                jax.ShapeDtypeStruct((QUAD, HALF, 16, LANES), BF16),
                acc_type,
            ),
            vmem_mb=16,
        ),
        cost_estimate=SMALL,
        name="combine_last",
    )(table, parts[3], parts[0], acc)
    return keep, send


def join_kernel(k0, r0, k1, r1, halves):
    for h, (keep, got) in enumerate(((k0, r0), (k1, r1))):
        halves[QUAD * h : QUAD * (h + 1)] = (keep[...] + got[...].astype(F32)).astype(BF16)


def join(*arrays):
    return pl.pallas_call(
        join_kernel,
        in_specs=[in_vmem()] * 4,
        out_specs=in_vmem(),
        **call(join_kernel, jax.ShapeDtypeStruct((NZ, HALF, 16, LANES), BF16)),
        cost_estimate=SMALL,
        name="join",
    )(*arrays)


def split_rows(value, rows):
    high = value.astype(BF16).astype(F32)
    middle = (value - high).astype(BF16).astype(F32)
    low = value - high - middle
    row = lax.broadcasted_iota(jnp.int32, (8, LANES), 0)
    tile = jnp.where(row == 0, high, jnp.where(row == 1, middle, jnp.where(row == 2, low, 0.0)))
    if rows > 8:
        tile = jnp.concatenate([tile, jnp.zeros((rows - 8, LANES), F32)], 0)
    return tile


def total_kernel(parts, squares, sums, pack):
    sums_now = parts[0].astype(F32)
    for z in range(1, NZ):
        sums_now = sums_now + parts[z].astype(F32)
    pack[0:HALF] = sums_now.astype(BF16)
    tile = squares[...] + jnp.sum((sums_now * sums_now).reshape(HALF * 2, 8, LANES), axis=0)
    value = jnp.broadcast_to(jnp.sum(tile, axis=0, keepdims=True), (8, LANES))
    sums[...] = value
    pack[HALF] = split_rows(value, 16).astype(BF16)


def total_of(parts, squares):
    return pl.pallas_call(
        total_kernel,
        in_specs=[in_vmem()] * 2,
        out_specs=(in_vmem(), in_vmem()),
        **call(
            total_kernel,
            (
                jax.ShapeDtypeStruct((8, LANES), F32),
                jax.ShapeDtypeStruct((HALF + 1, 16, LANES), BF16),
            ),
        ),
        name="total",
    )(parts, squares)


def route_kernel(table, sums, mine, other, out):
    c = place()[2]
    words = table[HOLD : HOLD + 8, :]
    tail = other[HALF].astype(F32)[0:8, :]
    value = sums[...] + jnp.sum(tail, axis=0, keepdims=True)
    blank = jnp.concatenate([jnp.zeros((16, LANES), F32), split_rows(value, 8)], 0)
    out[...] = jnp.broadcast_to(blank.astype(BF16)[None], (NY * NZ, 24, LANES))
    for s in range(2 * HALF):
        block = ((words[s // 3, 0] >> (7 * (s % 3))) & 127) - 1
        piece = jnp.where((s % 2) == c, mine[s // 2], other[s // 2])

        @pl.when((block >= 0) & ((block & 1) == c))
        def _():
            out[block >> 1, 0:16, :] = piece


def route(table, sums, mine, other):
    return pl.pallas_call(
        route_kernel,
        in_specs=[in_vmem()] * 4,
        out_specs=in_vmem(),
        **call(route_kernel, jax.ShapeDtypeStruct((NY * NZ, 24, LANES), BF16)),
        name="route",
    )(table, sums, mine, other)


def tally_kernel(arrived, sums):
    tails = jnp.sum(arrived[...].astype(F32)[:, 16:24, :], axis=0)
    tails = jnp.sum(jnp.sum(tails, axis=0, keepdims=True), axis=1, keepdims=True)
    sums[...] = jnp.broadcast_to(tails, (1, LANES))


def tally(arrived):
    return pl.pallas_call(
        tally_kernel,
        in_specs=[in_vmem()],
        out_specs=in_vmem(),
        **call(tally_kernel, jax.ShapeDtypeStruct((1, LANES), F32)),
        name="tally",
    )(arrived)


def finish_kernel(table, arrived, own_0, own_1, key_grad, value_grad):
    inner = table[INNER : INNER + 1, :] > 0
    for z in range(NZ):
        h, kind, half = z // 4, z // 2 % 2, z % 2
        out = value_grad if kind else key_grad
        own_grad = own_1 if h else own_0
        for y in range(NY):
            at = half * 64 + y * 16
            piece = arrived[y * NZ + z].astype(F32)[0:16, :]
            out[at : at + 16, h, :] = jnp.where(inner, piece, own_grad[kind, at : at + 16, :])


def finish(table, arrived, owns):
    return pl.pallas_call(
        finish_kernel,
        in_specs=[in_vmem()] * 4,
        out_specs=(in_vmem(),) * 2,
        **call(finish_kernel, (jax.ShapeDtypeStruct((TOK, KV, HD), F32),) * 2),
        cost_estimate=SMALL,
        name="finish",
    )(table, arrived, *owns)


def local(queries, keys, values, cotangent, rewards, groups, ancestors, step_ids):
    packet, own_kv = packet_of(
        keys, values, ancestors, groups, rewards
    )
    mine = swap_yz(packet)
    other = other_core(mine)
    trained = (step_ids[0] % 2 == 0)[:, None, None]
    masked = jnp.where(trained, cotangent, jnp.zeros_like(cotangent))
    picked, table, scale = plan(mine, other)
    column = swap_z(picked)
    column_other = other_core(column)
    q_all, g_all = prepare(scale, queries, masked)
    parts = []
    for h in range(KV):
        dealt = deal(h, table, column, column_other, g_all)
        parts.append([dealt[0]] + [along_y(dealt[k], k) for k in (1, 2, 3)])
    heads, after = [], None
    for h in range(KV):
        after, own_grad, sent, last = attend(h, table, q_all, g_all, own_kv, parts[h], after)
        back = [None] + [along_y(sent[k], -k) for k in (1, 2, 3)]
        heads.append((own_grad, back, last))
    owns = [own_grad for own_grad, _, _ in heads]
    dqs, halves = [], []
    for h, (_, back, last) in enumerate(heads):
        dq, back[0] = last(after)
        dqs.append(dq)
        after = dq
        if h == KV - 1:
            query_grad, squares = emit(table, dqs, owns)
            after = squares
        keep, send = combine(table, back, after)
        halves += [keep, other_core(send)]
    halves = join(*halves)
    sums, pack = total_of(swap_z(halves), squares)
    arrived = swap_yz(route(table, sums, pack, other_core(pack)))
    mine_sum = tally(arrived)
    all_sum = mine_sum
    for k in (1, 2, 3):
        all_sum = all_sum + along_head(mine_sum, k)
    key_grad, value_grad = finish(table, arrived, owns)
    count = float(NBLK * TOK * NHEAD * (KV * RATIO + 2 * KV) * HD)
    grad_rms = jnp.sqrt(all_sum[0, 0] / count)
    return query_grad, key_grad, value_grad, grad_rms


def solution(mesh):
    in_specs = (
        P("branch", "head", None),
        P("branch", "head", None),
        P("branch", "head", None),
        P("branch", "head", None),
        P("branch"),
        P("branch"),
        P("branch", None),
        P("branch", None),
    )
    out_specs = (
        P("branch", "head", None),
        P("branch", "head", None),
        P("branch", "head", None),
        P(),
    )
    return jax.shard_map(local, mesh=mesh, in_specs=in_specs, out_specs=out_specs, check_vma=False)
```

```python
import functools
import math

import jax
import jax.numpy as jnp
from jax import lax
from jax.experimental import pallas as pl
from jax.experimental.pallas import tpu as pltpu
from jax.sharding import PartitionSpec as P

NY, NZ, NC = 4, 8, 2
NBLK = NY * NZ * NC
NHEAD = 4
GROUP = 4
DEPTH = 8
TOK = 128
HD = 128
KV = 2
RATIO = 8
LANES = 128
HALF = 8
ROWS = TOK * RATIO
QUAD = 4
PART = 32 * DEPTH
HAND = (DEPTH, QUAD, 16, LANES)
F32 = jnp.float32
BF16 = jnp.bfloat16
VMEM = pltpu.VMEM
NT = (((1,), (1,)), ((), ()))
NN = (((1,), (0,)), ((), ()))
TN = (((0,), (0,)), ((), ()))


def index_of(y, z, c):
    return ((y % NY) * NZ + z % NZ) * NC + c % NC


def every():
    return [(y, z, c) for y in range(NY) for z in range(NZ) for c in range(NC)]


def along_y(x, step):
    pairs = [(index_of(y, z, c), index_of(y + step, z, c)) for y, z, c in every()]
    return lax.ppermute(x, "branch", pairs)


def other_core(x):
    pairs = [(index_of(y, z, c), index_of(y, z, c + 1)) for y, z, c in every()]
    return lax.ppermute(x, "branch", pairs)


def along_head(x, step):
    pairs = [(i, (i + step) % NHEAD) for i in range(NHEAD)]
    return lax.ppermute(x, "head", pairs)


def swap_z(x):
    groups = [[index_of(y, z, c) for z in range(NZ)] for y in range(NY) for c in range(NC)]
    return lax.all_to_all(x, "branch", 0, 0, axis_index_groups=groups, tiled=False)


def swap_yz(x):
    groups = [[index_of(y, z, c) for y in range(NY) for z in range(NZ)] for c in range(NC)]
    return lax.all_to_all(x, "branch", 0, 0, axis_index_groups=groups, tiled=False)


def call(body, outs, scratch=(), vmem_mb=32):
    return dict(
        out_shape=outs,
        scratch_shapes=list(scratch),
        compiler_params=pltpu.CompilerParams(vmem_limit_bytes=vmem_mb << 20),
    )


def in_vmem():
    return pl.BlockSpec(memory_space=VMEM)


def place():
    b = lax.axis_index("branch")
    return b // (NZ * NC), (b // NC) % NZ, b % NC


LINE = 0
DEAL = 16
BACK = 32
HOLD = 48
INNER = 56
SELF = 72
WORDS = 88


def row_of(y, z):
    return 32 * y + 8 * (z // 2)


def packet_kernel(
    keys_far, values_far, ancestors_far, group, reward, packet, own_kv,
    keys, values, ancestors, sems,
):
    pairs = (
        (ancestors_far, ancestors),
        (keys_far, keys),
        (values_far, values),
    )
    copies = [pltpu.make_async_copy(a, b, sems.at[i]) for i, (a, b) in enumerate(pairs)]
    for copy in copies:
        copy.start()
    for copy in copies[:1]:
        copy.wait()
    row = lax.broadcasted_iota(jnp.int32, (8, LANES), 0)
    lane = lax.broadcasted_iota(jnp.int32, (8, LANES), 1)
    spot = lax.broadcasted_iota(jnp.int32, (8, DEPTH), 0) == lax.broadcasted_iota(
        jnp.int32, (8, DEPTH), 1
    )
    line = jnp.broadcast_to(ancestors[...].astype(F32), (8, DEPTH))
    line = jnp.sum(jnp.where(spot, line, 0.0), axis=1, keepdims=True)
    facts = jnp.where(
        row == 0, group[0].astype(F32), jnp.where(row == 1, reward[0].astype(F32), 0.0)
    )
    meta = jnp.where(lane < NBLK, line, facts)
    for copy in copies[1:]:
        copy.wait()
    for h in range(KV):
        own_kv[2 * h] = keys[:, h, :]
        own_kv[2 * h + 1] = values[:, h, :]
    whole = [own_kv[i].astype(F32) for i in range(2 * KV)]
    for z in range(NZ):
        for y in range(NY):
            at = row_of(y, z)
            rows = [whole[2 * h + z % 2][at : at + 8] for h in range(KV)]
            packet[y * NZ + z] = jnp.concatenate(rows + [meta], 0).astype(BF16)


def packet_of(keys, values, ancestors, group, reward):
    return pl.pallas_call(
        packet_kernel,
        in_specs=[pl.BlockSpec(memory_space=pltpu.HBM)] * 3
        + [pl.BlockSpec(memory_space=pltpu.SMEM)] * 2,
        out_specs=(in_vmem(),) * 2,
        **call(
            packet_kernel,
            (
                jax.ShapeDtypeStruct((NY * NZ, 24, LANES), BF16),
                jax.ShapeDtypeStruct((2 * KV, TOK, HD), BF16),
            ),
            [VMEM(x.shape, x.dtype) for x in (keys, values, ancestors)]
            + [pltpu.SemaphoreType.DMA((3,))],
            vmem_mb=62,
        ),
        name="packet",
    )(keys, values, ancestors, group, reward)


def pack_rows(x, base, first, count):
    row = lax.broadcasted_iota(jnp.int32, (8, LANES), 0)
    weight = jnp.zeros((8, LANES), F32)
    for i in range(count):
        weight = jnp.where(row == first + i, float(base**i), weight)
    return jnp.sum(x * weight, axis=0, keepdims=True)


def plan_kernel(mine, other, picked, table, scale):
    y, z, c = place()
    meta_m = mine[...].astype(F32)[:, 16:24, :]
    meta_o = other[...].astype(F32)[:, 16:24, :]
    row = lax.broadcasted_iota(jnp.int32, (8, LANES), 0)
    row_f = row.astype(F32)
    lane = lax.broadcasted_iota(jnp.int32, (8, LANES), 1)
    lane_f = lane.astype(F32)
    is_block = lane < NBLK
    wide_lane = lax.broadcasted_iota(jnp.int32, (NY * NZ, LANES), 1).astype(F32)
    hit = jnp.maximum(
        jnp.where(meta_m[:, 0, :] == wide_lane, 1.0, 0.0),
        jnp.where(meta_o[:, 0, :] == wide_lane, 1.0, 0.0),
    )
    inner = jnp.max(hit, axis=0, keepdims=True)
    inner = jnp.where(is_block, jnp.broadcast_to(inner, (8, LANES)), 0.0)
    before = (
        lax.broadcasted_iota(jnp.int32, (LANES, LANES), 0)
        < lax.broadcasted_iota(jnp.int32, (LANES, LANES), 1)
    ).astype(F32).astype(BF16)
    rank = lax.dot_general(inner.astype(BF16), before, NN, preferred_element_type=F32)
    slots = jnp.where(inner > 0.0, rank + 1.0, 0.0)

    words = []
    for first in (0, 8):
        wanted = row_f + float(first + 1)
        index = jnp.sum(jnp.where(slots == wanted, lane_f, 0.0), axis=1, keepdims=True)
        index = jnp.broadcast_to(index, (8, LANES))
        words += [pack_rows(index, 64, at, 4).astype(jnp.int32)[0, 0] for at in (0, 4)]
    pieces = []
    for s in range(2 * HALF):
        block = (words[s // 4] >> (6 * (s % 4))) & 63
        at = block >> 1
        piece = jnp.where((block & 1) == c, mine[at].astype(F32), other[at].astype(F32))
        pieces.append(jnp.where(c == 0, piece[0:8], piece[8:16]))
    for j in range(HALF):
        pair = jnp.concatenate(pieces[2 * j : 2 * j + 2], 0).astype(BF16)
        picked[:, j] = jnp.broadcast_to(pair[None], (NZ, 16, LANES))

    for k in range(NY):
        yy = lax.rem(y + k, NY)
        for u, side in enumerate((mine, other)):
            line = side[yy * NZ + z].astype(F32)[16:24, :]
            same = (line == lane_f) & is_block
            slot = jnp.sum(jnp.where(same, slots, 0.0), axis=1, keepdims=True)
            slot = jnp.broadcast_to(slot, (8, LANES))
            block = (yy * NZ + z) * NC + (c if u == 0 else 1 - c)
            own = jnp.sum(jnp.where(lane == block, slots, 0.0), axis=1, keepdims=True)
            own = jnp.broadcast_to(own, (8, LANES))
            depth = jnp.sum(jnp.where(slot > 0.0, 1.0, 0.0), axis=0, keepdims=True)
            entry = jnp.where(row_f == depth, own, slot)
            dealt = jnp.maximum(slot - 1.0, 0.0)
            for half in range(2):
                at = 8 * u + 2 * k + half
                word = pack_rows(dealt, 16, 4 * half, 4)
                table[DEAL + at : DEAL + at + 1, :] = word.astype(jnp.int32)
                word = pack_rows(entry, 32, 4 * half, 4)
                table[BACK + at : BACK + at + 1, :] = word.astype(jnp.int32)
            if k == 0:
                at = 8 * u
                table[LINE + at : LINE + at + 8, :] = slot.astype(jnp.int32)
                table[INNER + at : INNER + at + 8, :] = own.astype(jnp.int32)
                mark = jnp.where(row_f == depth, own, 0.0)
                table[SELF + at : SELF + at + 8, :] = mark.astype(jnp.int32)
    for i in range(6):
        word = jnp.zeros((8, 1), F32)
        for j in range(3):
            held = jnp.where(slots == float(3 * i + j + 1), lane_f + 1.0, 0.0)
            word = word + jnp.sum(held, axis=1, keepdims=True) * float(128**j)
        table[HOLD + i : HOLD + i + 1, :] = jnp.broadcast_to(word, (8, LANES)).astype(jnp.int32)[0:1]

    for u, side in enumerate((mine, other)):
        here = side[y * NZ + z].astype(F32)[16:24, :]
        group, reward = here[0:1, :], here[1:2, :]
        in_m = jnp.where(meta_m[:, 0, :] == group, meta_m[:, 1, :], 0.0)
        in_o = jnp.where(meta_o[:, 0, :] == group, meta_o[:, 1, :], 0.0)
        total = jnp.sum(in_m + in_o, axis=0, keepdims=True)
        squares = jnp.sum(in_m * in_m + in_o * in_o, axis=0, keepdims=True)
        mean = total / GROUP
        spread = jnp.sqrt(jnp.maximum(squares / GROUP - mean * mean, 0.25))
        advantage = (reward - mean) / spread
        advantage = jnp.sum(jnp.where(lane[0:1] == NBLK, advantage, 0.0), axis=1, keepdims=True)
        scale[8 * u : 8 * u + 8] = jnp.broadcast_to(advantage, (8, LANES))


def plan(mine, other):
    return pl.pallas_call(
        plan_kernel,
        in_specs=[in_vmem()] * 2,
        out_specs=(in_vmem(),) * 3,
        **call(
            plan_kernel,
            (
                jax.ShapeDtypeStruct((NZ, HALF, 16, LANES), BF16),
                jax.ShapeDtypeStruct((WORDS, LANES), jnp.int32),
                jax.ShapeDtypeStruct((16, LANES), F32),
            ),
        ),
        name="plan",
    )(mine, other)


def deal_kernel(u, table, column, after, *outs):
    words = table[DEAL + 8 * u : DEAL + 8 * u + 8, :]
    for k in range(NY):
        for d in range(DEPTH):
            slot = (words[2 * k + d // 4, 0] >> (4 * (d % 4))) & 15
            pair = column[:, slot >> 1].astype(F32)
            rows = jnp.where((slot & 1) == 1, pair[:, 8:16], pair[:, 0:8])
            for kind in range(2):
                whole = jnp.concatenate([rows[2 * i + kind] for i in range(4)], 0)
                outs[k][d, 2 * kind : 2 * kind + 2] = whole.astype(BF16).reshape(2, 16, LANES)


def deal(u, table, column, after):
    return pl.pallas_call(
        functools.partial(deal_kernel, u),
        in_specs=[in_vmem()] * 2 + [pl.BlockSpec(memory_space=pl.ANY)],
        out_specs=(in_vmem(),) * NY,
        **call(deal_kernel, (jax.ShapeDtypeStruct(HAND, BF16),) * NY),
        name="deal",
    )(table, column, after)


def halve_kernel(queries, cotangent, own_kv, after, keep, send):
    first_core = place()[2] == 0
    for at, far in ((0, queries), (ROWS, cotangent)):
        whole = far[...].astype(F32)
        low = whole[:, 0:RATIO].reshape(ROWS, HD).astype(BF16)
        high = whole[:, RATIO:].reshape(ROWS, HD).astype(BF16)
        keep[at : at + ROWS] = jnp.where(first_core, low, high)
        send[at : at + ROWS] = jnp.where(first_core, high, low)
    for kind in range(2):
        at = 2 * ROWS + TOK * kind
        low, high = own_kv[kind], own_kv[2 + kind]
        keep[at : at + TOK] = jnp.where(first_core, low, high)
        send[at : at + TOK] = jnp.where(first_core, high, low)


def halve(queries, cotangent, own_kv, after):
    return pl.pallas_call(
        halve_kernel,
        in_specs=[in_vmem()] * 3 + [pl.BlockSpec(memory_space=pl.ANY)],
        out_specs=(in_vmem(),) * 2,
        **call(halve_kernel, (jax.ShapeDtypeStruct((2 * ROWS + 2 * TOK, HD), BF16),) * 2),
        name="halve",
    )(queries, cotangent, own_kv, after)


def prepare_kernel(scale, keep, got, q_all, g_all, kv_all):
    for u, side in enumerate((keep, got)):
        q_all[u] = side[0:ROWS]
        weight = scale[8 * u : 8 * u + 1, :]
        g_all[u] = (side[ROWS : 2 * ROWS].astype(F32) * weight).astype(BF16)
        for kind in range(2):
            at = 2 * ROWS + TOK * kind
            kv_all[2 * u + kind] = side[at : at + TOK]


def prepare(scale, keep, got):
    return pl.pallas_call(
        prepare_kernel,
        in_specs=[in_vmem()] * 3,
        out_specs=(in_vmem(),) * 3,
        **call(
            prepare_kernel,
            (jax.ShapeDtypeStruct((2, ROWS, HD), BF16),) * 2
            + (jax.ShapeDtypeStruct((4, TOK, HD), BF16),),
        ),
        name="prepare",
    )(scale, keep, got)


def rows_of(part, kind):
    return part[:, 2 * kind : 2 * kind + 2].reshape(PART, HD)


def one_part(keys, values, q, g, mask, exps, pgs, stats, at):
    s = lax.dot_general(keys, q, NT, preferred_element_type=F32) * (
        math.log2(math.e) / math.sqrt(HD)
    )
    s = mask(s)
    top = jnp.max(s, axis=0, keepdims=True)
    e = jnp.exp2(s - top)
    pg = lax.dot_general(values, g, NT, preferred_element_type=F32)
    exps[...] = e
    pgs[...] = pg
    stats[at : at + 1, :] = top
    stats[at + 1 : at + 2, :] = jnp.sum(e, axis=0, keepdims=True)
    stats[at + 2 : at + 3, :] = jnp.sum(e * pg, axis=0, keepdims=True)


def causal(s):
    key_pos = lax.broadcasted_iota(jnp.int32, s.shape, 0)
    query_pos = lax.broadcasted_iota(jnp.int32, s.shape, 1) // RATIO
    return jnp.where(key_pos <= query_pos, s, -1e30)


def listed(h, table):
    def mask(s):
        parts = []
        for d in range(DEPTH):
            seen = jnp.concatenate([table[LINE + 8 * h + d : LINE + 8 * h + d + 1, :]] * (ROWS // LANES), 1) > 0
            parts.append(jnp.where(seen, s[32 * d : 32 * d + 32], -1e30))
        return jnp.concatenate(parts, 0)

    return mask


def scores_kernel(h, table, q_all, g_all, part, after, exps, pgs, stats):
    keys, values = rows_of(part, 0), rows_of(part, 1)
    one_part(keys, values, q_all[h], g_all[h], listed(h, table), exps, pgs, stats, 0)


def first_scores_kernel(h, table, q_all, g_all, part, own_kv, exps, pgs, stats, own_exps, own_pgs):
    keys, values = rows_of(part, 0), rows_of(part, 1)
    q, g = q_all[h], g_all[h]
    one_part(keys, values, q, g, listed(h, table), exps, pgs, stats, 0)
    one_part(own_kv[2 * h], own_kv[2 * h + 1], q, g, causal, own_exps, own_pgs, stats, 4)


def wide(keys):
    return jax.ShapeDtypeStruct((keys, ROWS), F32)


STATS = jax.ShapeDtypeStruct((8, TOK * RATIO), F32)


def scores_of(h, table, q_all, g_all, part, after):
    return pl.pallas_call(
        functools.partial(scores_kernel, h),
        in_specs=[in_vmem()] * 4 + [pl.BlockSpec(memory_space=pl.ANY)],
        out_specs=(in_vmem(),) * 3,
        **call(scores_kernel, (wide(PART), wide(PART), STATS), vmem_mb=16),
        cost_estimate=cost(PART, 2),
        name="scores",
    )(table, q_all, g_all, part, after)


def first_scores_of(h, table, q_all, g_all, part, own_kv):
    return pl.pallas_call(
        functools.partial(first_scores_kernel, h),
        in_specs=[in_vmem()] * 5,
        out_specs=(in_vmem(),) * 5,
        **call(
            first_scores_kernel,
            (wide(PART), wide(PART), STATS, wide(TOK), wide(TOK)),
            vmem_mb=16,
        ),
        cost_estimate=cost(PART + TOK, 2),
        name="scores_first",
    )(table, q_all, g_all, part, own_kv)


def cost(keys, products):
    return pl.CostEstimate(
        flops=2 * products * ROWS * keys * HD,
        bytes_accessed=8 * ROWS * keys,
        transcendentals=ROWS * keys,
    )


SMALL = pl.CostEstimate(flops=1000, bytes_accessed=1000, transcendentals=0)


def merge(stats):
    rows = [(ref, 0) for ref in stats] + [(stats[0], 4)]
    tops = [ref[at : at + 1, :] for ref, at in rows]
    top = tops[0]
    for t in tops[1:]:
        top = jnp.maximum(top, t)
    shares = [jnp.exp2(t - top) for t in tops]
    norm = sum(s * ref[at + 1 : at + 2, :] for s, (ref, at) in zip(shares, rows))
    norm = 1.0 / norm
    shares = [s * norm for s in shares]
    delta = sum(s * ref[at + 2 : at + 3, :] for s, (ref, at) in zip(shares, rows))
    return shares, delta


def one_grad(e, pg, share, delta, q, g, keys):
    p = e * share
    low = p.astype(BF16)
    ds = (p * (pg - delta)).astype(BF16)
    factor = 1.0 / math.sqrt(HD)
    dv = lax.dot_general(low, g, NN, preferred_element_type=F32)
    dk = lax.dot_general(ds, q, NN, preferred_element_type=F32) * factor
    turned = keys.astype(F32).T.astype(BF16)
    dq = lax.dot_general(turned, ds, NN, preferred_element_type=F32)
    return dq, dk, dv


def part_grad(k, h, table, stats, exps, pgs, q_all, g_all, part, own_grad, contrib):
    shares, delta = merge(stats)
    dq, dk, dv = one_grad(
        exps[...], pgs[...], shares[k], delta, q_all[h], g_all[h], rows_of(part, 0)
    )
    piece = lax.rem(place()[0] + NY - k, NY)
    for kind, grad in enumerate((dk, dv)):
        own = own_grad[kind, pl.ds(pl.multiple_of(piece * 32, 32), 32), :]
        for d in range(DEPTH):
            mark = table[SELF + 8 * h + d : SELF + 8 * h + d + 1, :] > 0
            both = jnp.where(mark, own, grad[32 * d : 32 * d + 32])
            contrib[d, 2 * kind : 2 * kind + 2] = both.astype(BF16).reshape(2, 16, HD)
    return dq


def first_grads_kernel(
    k, h, table, s0, s1, s2, s3, exps, pgs, q_all, g_all, part, own_exps, own_pgs, own_kv,
    dq_sum, own_grad, contrib,
):
    stats = (s0, s1, s2, s3)
    shares, delta = merge(stats)
    dq, dk, dv = one_grad(
        own_exps[...], own_pgs[...], shares[NY], delta, q_all[h], g_all[h], own_kv[2 * h]
    )
    own_grad[0] = dk
    own_grad[1] = dv
    dq_sum[...] = dq + part_grad(
        k, h, table, stats, exps, pgs, q_all, g_all, part, own_grad, contrib
    )


def grads_kernel(
    k, h, table, s0, s1, s2, s3, exps, pgs, q_all, g_all, part, own_grad, dq_in, *outs
):
    dq_sum, contrib = outs[-2:]
    dq_sum[...] = dq_in[...] + part_grad(
        k, h, table, (s0, s1, s2, s3), exps, pgs, q_all, g_all, part, own_grad, contrib
    )


def emit_kernel(table, dq_0, dq_1, own_0, own_1, keep, send, squares):
    total = jnp.zeros((8, HD), F32)
    for u, (dq, own, out) in enumerate(((dq_0, own_0, keep), (dq_1, own_1, send))):
        dq = dq[...].T * (1.0 / math.sqrt(HD))
        total = total + jnp.sum((dq * dq).reshape(ROWS // 8, 8, HD), axis=0)
        out[0:ROWS] = dq
        own = own[...]
        own_squares = jnp.sum((own * own).reshape(2 * TOK // 8, 8, HD), axis=0)
        inner = table[INNER + 8 * u : INNER + 8 * u + 8, :] > 0
        total = total + jnp.where(inner, 0.0, own_squares)
    send[ROWS : ROWS + TOK] = own_1[0]
    send[ROWS + TOK :] = own_1[1]
    squares[...] = total


def emit(table, dqs, owns):
    return pl.pallas_call(
        emit_kernel,
        in_specs=[in_vmem()] * 5,
        out_specs=(in_vmem(),) * 3,
        **call(
            emit_kernel,
            (
                jax.ShapeDtypeStruct((ROWS, HD), F32),
                jax.ShapeDtypeStruct((ROWS + 2 * TOK, HD), F32),
                jax.ShapeDtypeStruct((8, LANES), F32),
            ),
            vmem_mb=16,
        ),
        cost_estimate=SMALL,
        name="emit",
    )(table, *dqs, *owns)


def assemble_kernel(keep, got, query_grad, token):
    first_core = place()[2] == 0
    near, far = keep[...], got[0:ROWS]
    low, high = jnp.where(first_core, near, far), jnp.where(first_core, far, near)
    query_grad[:, 0:RATIO, :] = low.reshape(TOK, RATIO, HD)
    query_grad[:, RATIO:, :] = high.reshape(TOK, RATIO, HD)
    token[...] = jnp.zeros_like(token)


def assemble(keep, got):
    return pl.pallas_call(
        assemble_kernel,
        in_specs=[in_vmem()] * 2,
        out_specs=(in_vmem(),) * 2,
        **call(
            assemble_kernel,
            (
                jax.ShapeDtypeStruct((TOK, KV * RATIO, HD), F32),
                jax.ShapeDtypeStruct((8, LANES), F32),
            ),
            vmem_mb=16,
        ),
        cost_estimate=SMALL,
        name="assemble",
    )(keep, got)


def grads_of(body, name, outs, k, h, *arrays):
    return pl.pallas_call(
        functools.partial(body, k, h),
        in_specs=[in_vmem()] * len(arrays),
        out_specs=(in_vmem(),) * len(outs),
        **call(body, outs, vmem_mb=16),
        cost_estimate=SMALL,
        name=name,
    )(*arrays)


def attend(h, table, q_all, g_all, own_kv, parts, after, hints):
    e, pg, st = [None] * NY, [None] * NY, [None] * NY
    e[0], pg[0], st[0], own_e, own_pg = first_scores_of(h, table, q_all, g_all, parts[0], own_kv)
    after = st[0] if after is None else after
    for k in (1, 2, 3):
        e[k], pg[k], st[k] = scores_of(h, table, q_all, g_all, parts[k], after)
        after = st[k]
    back = [None] * NY
    dq_type = jax.ShapeDtypeStruct((HD, ROWS), F32)
    own_type = jax.ShapeDtypeStruct((2, TOK, HD), F32)
    contrib_type = jax.ShapeDtypeStruct(HAND, BF16)

    def shared(k):
        return (table, *st, e[k], pg[k], q_all, g_all, parts[k])

    dq, own_grad, back[2] = grads_of(
        first_grads_kernel, "grads_first", (dq_type, own_type, contrib_type), 2, h,
        *shared(2), own_e, own_pg, own_kv,
    )
    for k, hint in ((1, hints[:1]), (3, hints[1:])):
        dq, back[k] = grads_of(
            grads_kernel, "grads", (dq_type, contrib_type), k, h, *shared(k), own_grad, dq, *hint
        )

    def last(after):
        return grads_of(
            grads_kernel, "grads_last", (dq_type, contrib_type), 0, h, *shared(0), own_grad, dq, after
        )

    return dq, own_grad, back, last


def add_part(k, u, table, part, acc):
    at = BACK + 8 * u + 2 * k
    words = table[at : at + 2, :]
    for d in range(DEPTH):
        slot = (words[d // 4, 0] >> (5 * (d % 4))) & 31
        acc[jnp.maximum(slot - 1, 0)] += jnp.where(slot > 0, part[d].astype(F32), 0.0)


def combine_first_kernel(table, part_1, part_2, acc, token):
    acc[...] = jnp.zeros_like(acc)
    add_part(1, 0, table, part_1, acc)
    add_part(2, 0, table, part_2, acc)
    token[...] = jnp.zeros_like(token)


def combine_kernel(ks, u, table, *refs):
    acc = refs[len(ks) + 2]
    for token in refs[len(ks) + 3 :]:
        token[...] = jnp.zeros_like(token)
    for k, part in zip(ks, refs):
        add_part(k, u, table, part, acc)


def leave_kernel(acc, halves):
    for z in range(NZ):
        at = 2 * (z % 2) + z // 4
        rows = slice(8 * (z // 2 % 2), 8 * (z // 2 % 2) + 8)
        for j in range(HALF):
            pair = [acc[2 * j + i, at, rows, :] for i in range(2)]
            halves[z, j] = jnp.concatenate(pair, 0).astype(BF16)


ACC = (2 * HALF, QUAD, 16, LANES)


def acc_and_token():
    return jax.ShapeDtypeStruct(ACC, F32), jax.ShapeDtypeStruct((8, LANES), F32)


def combine_start(table, part_1, part_2):
    return pl.pallas_call(
        combine_first_kernel,
        in_specs=[in_vmem()] * 3,
        out_specs=(in_vmem(),) * 2,
        **call(combine_first_kernel, acc_and_token(), vmem_mb=16),
        cost_estimate=SMALL,
        name="combine_first",
    )(table, part_1, part_2)


def combine_more(ks, u, table, parts, acc, after, outs=1):
    return pl.pallas_call(
        functools.partial(combine_kernel, ks, u),
        in_specs=[in_vmem()] * (2 + len(parts)) + [pl.BlockSpec(memory_space=pl.ANY)],
        out_specs=(in_vmem(),) * outs,
        input_output_aliases={1 + len(parts): 0},
        **call(combine_kernel, acc_and_token()[:outs], vmem_mb=16),
        cost_estimate=SMALL,
        name="combine",
    )(table, *parts, acc, after)


def leave(acc):
    return pl.pallas_call(
        leave_kernel,
        in_specs=[in_vmem()],
        out_specs=in_vmem(),
        **call(leave_kernel, jax.ShapeDtypeStruct((NZ, HALF, 16, LANES), BF16), vmem_mb=16),
        cost_estimate=SMALL,
        name="leave",
    )(acc)


def split_rows(value, rows):
    high = value.astype(BF16).astype(F32)
    middle = (value - high).astype(BF16).astype(F32)
    low = value - high - middle
    row = lax.broadcasted_iota(jnp.int32, (8, LANES), 0)
    tile = jnp.where(row == 0, high, jnp.where(row == 1, middle, jnp.where(row == 2, low, 0.0)))
    if rows > 8:
        tile = jnp.concatenate([tile, jnp.zeros((rows - 8, LANES), F32)], 0)
    return tile


def total_kernel(parts, squares, totals, sums):
    sums_now = parts[0].astype(F32)
    for z in range(1, NZ):
        sums_now = sums_now + parts[z].astype(F32)
    totals[...] = sums_now
    tile = squares[...] + jnp.sum((sums_now * sums_now).reshape(HALF * 2, 8, LANES), axis=0)
    sums[...] = jnp.broadcast_to(jnp.sum(tile, axis=0, keepdims=True), (8, LANES))


def route_kernel(table, parts, squares, out, room, totals, sums):
    total_kernel(parts, squares, totals, sums)
    c = place()[2]
    words = table[HOLD : HOLD + 8, :]
    blank = jnp.concatenate([jnp.zeros((16, LANES), F32), split_rows(sums[...], 8)], 0)
    room[0 : NY * NZ] = jnp.broadcast_to(blank[None], (NY * NZ, 24, LANES))
    for s in range(2 * HALF):
        block = ((words[s // 3, 0] >> (7 * (s % 3))) & 127) - 1
        side = jnp.where((block & 1) == c, 0, 8)
        to = jnp.where(block >= 0, block >> 1, NY * NZ)
        piece = totals[s // 2, 8 * (s % 2) : 8 * (s % 2) + 8, :]
        room[to, pl.ds(pl.multiple_of(side, 8), 8), :] = piece
    out[...] = room[0 : NY * NZ].astype(BF16)


def route(table, parts, squares):
    return pl.pallas_call(
        route_kernel,
        in_specs=[in_vmem()] * 3,
        out_specs=in_vmem(),
        **call(
            route_kernel,
            jax.ShapeDtypeStruct((NY * NZ, 24, LANES), BF16),
            [
                VMEM((NY * NZ + 1, 24, LANES), F32),
                VMEM((HALF, 16, LANES), F32),
                VMEM((8, LANES), F32),
            ],
        ),
        name="route",
    )(table, parts, squares)


def share_kernel(arrived, after, send, sums):
    whole = arrived[...].astype(F32)
    for i in range(NY * NZ // 2):
        pair = [whole[2 * i + j, 8:16, :] for j in range(2)]
        send[i] = jnp.concatenate(pair, 0).astype(BF16)
    tails = jnp.sum(jnp.sum(whole[:, 16:24, :], axis=0), axis=0, keepdims=True)
    value = jnp.broadcast_to(tails, (8, LANES))
    sums[...] = value
    send[NY * NZ // 2] = split_rows(value, 16).astype(BF16)


def share(arrived, after):
    return pl.pallas_call(
        share_kernel,
        in_specs=[in_vmem(), pl.BlockSpec(memory_space=pl.ANY)],
        out_specs=(in_vmem(),) * 2,
        **call(
            share_kernel,
            (
                jax.ShapeDtypeStruct((NY * NZ // 2 + 1, 16, LANES), BF16),
                jax.ShapeDtypeStruct((8, LANES), F32),
            ),
        ),
        name="share",
    )(arrived, after)


def tally_kernel(mine, got, sums):
    tails = mine[0:1, :] + jnp.sum(got[NY * NZ // 2].astype(F32), axis=0, keepdims=True)
    sums[...] = jnp.broadcast_to(jnp.sum(tails, axis=1, keepdims=True), (1, LANES))


def tally(mine, got):
    return pl.pallas_call(
        tally_kernel,
        in_specs=[in_vmem()] * 2,
        out_specs=in_vmem(),
        **call(tally_kernel, jax.ShapeDtypeStruct((1, LANES), F32)),
        name="tally",
    )(mine, got)


def finish_kernel(table, arrived, got, own, own_far, key_grad, value_grad):
    first_core = place()[2] == 0
    inner = table[INNER : INNER + 1, :] > 0
    for z in range(NZ):
        kind = z % 2
        out = value_grad if kind else key_grad
        for y in range(NY):
            at, src = row_of(y, z), y * NZ + z
            near = arrived[src].astype(F32)[0:8]
            far = got[src // 2].astype(F32)[8 * (src % 2) : 8 * (src % 2) + 8]
            near = jnp.where(inner, near, own[kind, at : at + 8, :])
            low = ROWS + TOK * kind + at
            far = jnp.where(inner, far, own_far[low : low + 8, :])
            out[at : at + 8, 0, :] = jnp.where(first_core, near, far)
            out[at : at + 8, 1, :] = jnp.where(first_core, far, near)


def finish(*arrays):
    return pl.pallas_call(
        finish_kernel,
        in_specs=[in_vmem()] * 5,
        out_specs=(in_vmem(),) * 2,
        **call(finish_kernel, (jax.ShapeDtypeStruct((TOK, KV, HD), F32),) * 2),
        cost_estimate=SMALL,
        name="finish",
    )(*arrays)


def local(queries, keys, values, cotangent, rewards, groups, ancestors, step_ids):
    packet, own_kv = packet_of(keys, values, ancestors, groups, rewards)
    mine = swap_yz(packet)
    other = other_core(mine)
    trained = (step_ids[0] % 2 == 0)[:, None, None]
    masked = jnp.where(trained, cotangent, jnp.zeros_like(cotangent))
    picked, table, scale = plan(mine, other)
    column = swap_z(picked)
    first = deal(0, table, column, table)
    keep, send = halve(queries, masked, own_kv, table)
    q_all, g_all, kv_all = prepare(scale, keep, other_core(send))
    parts = []
    for u in range(2):
        dealt = first if u == 0 else deal(u, table, column, first[0])
        parts.append([dealt[0]] + [along_y(dealt[k], k) for k in (1, 2, 3)])
    after, own_0, sent, last_0 = attend(0, table, q_all, g_all, kv_all, parts[0], None, ())
    back_0 = [None] + [along_y(sent[k], -k) for k in (1, 2, 3)]
    acc, token = combine_start(table, back_0[1], back_0[2])
    acc, late_token = combine_more((3,), 0, table, [back_0[3]], acc, table, 2)
    after, own_1, sent, last_1 = attend(
        1, table, q_all, g_all, kv_all, parts[1], after, (token, late_token)
    )
    back_1 = [None] + [along_y(sent[k], -k) for k in (1, 2, 3)]
    dq_0, back_0[0] = last_0(after)
    dq_1, back_1[0] = last_1(dq_0)
    near, far, squares = emit(table, (dq_0, dq_1), (own_0, own_1))
    far = other_core(far)
    query_grad, done = assemble(near, far)
    (acc,) = combine_more((0,), 0, table, [back_0[0]], acc, squares)
    (acc,) = combine_more((1, 0), 1, table, [back_1[1], back_1[0]], acc, squares)
    (acc,) = combine_more((2,), 1, table, [back_1[2]], acc, squares)
    (acc,) = combine_more((3,), 1, table, [back_1[3]], acc, squares)
    halves = leave(acc)
    arrived = swap_yz(route(table, swap_z(halves), squares))
    shared, mine_sum = share(arrived, done)
    shared = other_core(shared)
    mine_sum = tally(mine_sum, shared)
    all_sum = mine_sum
    for k in (1, 2, 3):
        all_sum = all_sum + along_head(mine_sum, k)
    key_grad, value_grad = finish(table, arrived, shared, own_0, far)
    count = float(NBLK * TOK * NHEAD * (KV * RATIO + 2 * KV) * HD)
    grad_rms = jnp.sqrt(all_sum[0, 0] / count)
    return query_grad, key_grad, value_grad, grad_rms


def solution(mesh):
    in_specs = (
        P("branch", "head", None),
        P("branch", "head", None),
        P("branch", "head", None),
        P("branch", "head", None),
        P("branch"),
        P("branch"),
        P("branch", None),
        P("branch", None),
    )
    out_specs = (
        P("branch", "head", None),
        P("branch", "head", None),
        P("branch", "head", None),
        P(),
    )
    return jax.shard_map(local, mesh=mesh, in_specs=in_specs, out_specs=out_specs, check_vma=False)
```

```python
import functools
import math

import jax
import jax.numpy as jnp
from jax import lax
from jax.experimental import pallas as pl
from jax.experimental.pallas import tpu as pltpu
from jax.sharding import PartitionSpec as P

NY, NZ, NC = 4, 8, 2
NBLK = NY * NZ * NC
NHEAD = 4
GROUP = 4
DEPTH = 8
TOK = 128
HD = 128
KV = 2
RATIO = 8
LANES = 128
HALF = 8
ROWS = TOK * RATIO
QUAD = 4
PART = 32 * DEPTH
HAND = (DEPTH, QUAD, 16, LANES)
F32 = jnp.float32
BF16 = jnp.bfloat16
VMEM = pltpu.VMEM
NT = (((1,), (1,)), ((), ()))
NN = (((1,), (0,)), ((), ()))
TN = (((0,), (0,)), ((), ()))


def index_of(y, z, c):
    return ((y % NY) * NZ + z % NZ) * NC + c % NC


def every():
    return [(y, z, c) for y in range(NY) for z in range(NZ) for c in range(NC)]


def along_y(x, step):
    pairs = [(index_of(y, z, c), index_of(y + step, z, c)) for y, z, c in every()]
    return lax.ppermute(x, "branch", pairs)


def other_core(x):
    pairs = [(index_of(y, z, c), index_of(y, z, c + 1)) for y, z, c in every()]
    return lax.ppermute(x, "branch", pairs)


def along_head(x, step):
    pairs = [(i, (i + step) % NHEAD) for i in range(NHEAD)]
    return lax.ppermute(x, "head", pairs)


def swap_z(x):
    groups = [[index_of(y, z, c) for z in range(NZ)] for y in range(NY) for c in range(NC)]
    return lax.all_to_all(x, "branch", 0, 0, axis_index_groups=groups, tiled=False)


def swap_yz(x):
    groups = [[index_of(y, z, c) for y in range(NY) for z in range(NZ)] for c in range(NC)]
    return lax.all_to_all(x, "branch", 0, 0, axis_index_groups=groups, tiled=False)


def call(body, outs, scratch=(), vmem_mb=32):
    return dict(
        out_shape=outs,
        scratch_shapes=list(scratch),
        compiler_params=pltpu.CompilerParams(vmem_limit_bytes=vmem_mb << 20),
    )


def in_vmem():
    return pl.BlockSpec(memory_space=VMEM)


def place():
    b = lax.axis_index("branch")
    return b // (NZ * NC), (b // NC) % NZ, b % NC


LINE = 0
DEAL = 16
BACK = 32
HOLD = 48
INNER = 56
SELF = 72
WORDS = 88


def row_of(y, z):
    return 32 * y + 8 * (z // 2)


def packet_kernel(
    keys_far, values_far, ancestors_far, group, reward, packet, own_kv,
    keys, values, ancestors, sems,
):
    pairs = (
        (ancestors_far, ancestors),
        (keys_far, keys),
        (values_far, values),
    )
    copies = [pltpu.make_async_copy(a, b, sems.at[i]) for i, (a, b) in enumerate(pairs)]
    for copy in copies:
        copy.start()
    for copy in copies[:1]:
        copy.wait()
    row = lax.broadcasted_iota(jnp.int32, (8, LANES), 0)
    lane = lax.broadcasted_iota(jnp.int32, (8, LANES), 1)
    spot = lax.broadcasted_iota(jnp.int32, (8, DEPTH), 0) == lax.broadcasted_iota(
        jnp.int32, (8, DEPTH), 1
    )
    line = jnp.broadcast_to(ancestors[...].astype(F32), (8, DEPTH))
    line = jnp.sum(jnp.where(spot, line, 0.0), axis=1, keepdims=True)
    facts = jnp.where(
        row == 0, group[0].astype(F32), jnp.where(row == 1, reward[0].astype(F32), 0.0)
    )
    meta = jnp.where(lane < NBLK, line, facts)
    for copy in copies[1:]:
        copy.wait()
    for h in range(KV):
        own_kv[2 * h] = keys[:, h, :]
        own_kv[2 * h + 1] = values[:, h, :]
    whole = [own_kv[i].astype(F32) for i in range(2 * KV)]
    for z in range(NZ):
        for y in range(NY):
            at = row_of(y, z)
            rows = [whole[2 * h + z % 2][at : at + 8] for h in range(KV)]
            packet[y * NZ + z] = jnp.concatenate(rows + [meta], 0).astype(BF16)


def packet_of(keys, values, ancestors, group, reward):
    return pl.pallas_call(
        packet_kernel,
        in_specs=[pl.BlockSpec(memory_space=pltpu.HBM)] * 3
        + [pl.BlockSpec(memory_space=pltpu.SMEM)] * 2,
        out_specs=(in_vmem(),) * 2,
        **call(
            packet_kernel,
            (
                jax.ShapeDtypeStruct((NY * NZ, 24, LANES), BF16),
                jax.ShapeDtypeStruct((2 * KV, TOK, HD), BF16),
            ),
            [VMEM(x.shape, x.dtype) for x in (keys, values, ancestors)]
            + [pltpu.SemaphoreType.DMA((3,))],
            vmem_mb=62,
        ),
        name="packet",
    )(keys, values, ancestors, group, reward)


def pack_rows(x, base, first, count):
    row = lax.broadcasted_iota(jnp.int32, (8, LANES), 0)
    weight = jnp.zeros((8, LANES), F32)
    for i in range(count):
        weight = jnp.where(row == first + i, float(base**i), weight)
    return jnp.sum(x * weight, axis=0, keepdims=True)


def plan_kernel(mine, other, picked, table, scale):
    y, z, c = place()
    meta_m = mine[...].astype(F32)[:, 16:24, :]
    meta_o = other[...].astype(F32)[:, 16:24, :]
    row = lax.broadcasted_iota(jnp.int32, (8, LANES), 0)
    row_f = row.astype(F32)
    lane = lax.broadcasted_iota(jnp.int32, (8, LANES), 1)
    lane_f = lane.astype(F32)
    is_block = lane < NBLK
    wide_lane = lax.broadcasted_iota(jnp.int32, (NY * NZ, LANES), 1).astype(F32)
    hit = jnp.maximum(
        jnp.where(meta_m[:, 0, :] == wide_lane, 1.0, 0.0),
        jnp.where(meta_o[:, 0, :] == wide_lane, 1.0, 0.0),
    )
    inner = jnp.max(hit, axis=0, keepdims=True)
    inner = jnp.where(is_block, jnp.broadcast_to(inner, (8, LANES)), 0.0)
    before = (
        lax.broadcasted_iota(jnp.int32, (LANES, LANES), 0)
        < lax.broadcasted_iota(jnp.int32, (LANES, LANES), 1)
    ).astype(F32).astype(BF16)
    rank = lax.dot_general(inner.astype(BF16), before, NN, preferred_element_type=F32)
    slots = jnp.where(inner > 0.0, rank + 1.0, 0.0)

    words = []
    for first in (0, 8):
        wanted = row_f + float(first + 1)
        index = jnp.sum(jnp.where(slots == wanted, lane_f, 0.0), axis=1, keepdims=True)
        index = jnp.broadcast_to(index, (8, LANES))
        words += [pack_rows(index, 64, at, 4).astype(jnp.int32)[0, 0] for at in (0, 4)]
    pieces = []
    for s in range(2 * HALF):
        block = (words[s // 4] >> (6 * (s % 4))) & 63
        at = block >> 1
        piece = jnp.where((block & 1) == c, mine[at].astype(F32), other[at].astype(F32))
        pieces.append(jnp.where(c == 0, piece[0:8], piece[8:16]))
    for j in range(HALF):
        pair = jnp.concatenate(pieces[2 * j : 2 * j + 2], 0).astype(BF16)
        picked[:, j] = jnp.broadcast_to(pair[None], (NZ, 16, LANES))

    for k in range(NY):
        yy = lax.rem(y + k, NY)
        for u, side in enumerate((mine, other)):
            line = side[yy * NZ + z].astype(F32)[16:24, :]
            same = (line == lane_f) & is_block
            slot = jnp.sum(jnp.where(same, slots, 0.0), axis=1, keepdims=True)
            slot = jnp.broadcast_to(slot, (8, LANES))
            block = (yy * NZ + z) * NC + (c if u == 0 else 1 - c)
            own = jnp.sum(jnp.where(lane == block, slots, 0.0), axis=1, keepdims=True)
            own = jnp.broadcast_to(own, (8, LANES))
            depth = jnp.sum(jnp.where(slot > 0.0, 1.0, 0.0), axis=0, keepdims=True)
            entry = jnp.where(row_f == depth, own, slot)
            dealt = jnp.maximum(slot - 1.0, 0.0)
            for half in range(2):
                at = 8 * u + 2 * k + half
                word = pack_rows(dealt, 16, 4 * half, 4)
                table[DEAL + at : DEAL + at + 1, :] = word.astype(jnp.int32)
                word = pack_rows(entry, 32, 4 * half, 4)
                table[BACK + at : BACK + at + 1, :] = word.astype(jnp.int32)
            if k == 0:
                at = 8 * u
                table[LINE + at : LINE + at + 8, :] = slot.astype(jnp.int32)
                table[INNER + at : INNER + at + 8, :] = own.astype(jnp.int32)
                mark = jnp.where(row_f == depth, own, 0.0)
                table[SELF + at : SELF + at + 8, :] = mark.astype(jnp.int32)
    for i in range(6):
        word = jnp.zeros((8, 1), F32)
        for j in range(3):
            held = jnp.where(slots == float(3 * i + j + 1), lane_f + 1.0, 0.0)
            word = word + jnp.sum(held, axis=1, keepdims=True) * float(128**j)
        table[HOLD + i : HOLD + i + 1, :] = jnp.broadcast_to(word, (8, LANES)).astype(jnp.int32)[0:1]

    for u, side in enumerate((mine, other)):
        here = side[y * NZ + z].astype(F32)[16:24, :]
        group, reward = here[0:1, :], here[1:2, :]
        in_m = jnp.where(meta_m[:, 0, :] == group, meta_m[:, 1, :], 0.0)
        in_o = jnp.where(meta_o[:, 0, :] == group, meta_o[:, 1, :], 0.0)
        total = jnp.sum(in_m + in_o, axis=0, keepdims=True)
        squares = jnp.sum(in_m * in_m + in_o * in_o, axis=0, keepdims=True)
        mean = total / GROUP
        spread = jnp.sqrt(jnp.maximum(squares / GROUP - mean * mean, 0.25))
        advantage = (reward - mean) / spread
        advantage = jnp.sum(jnp.where(lane[0:1] == NBLK, advantage, 0.0), axis=1, keepdims=True)
        scale[8 * u : 8 * u + 8] = jnp.broadcast_to(advantage, (8, LANES))


def plan(mine, other):
    return pl.pallas_call(
        plan_kernel,
        in_specs=[in_vmem()] * 2,
        out_specs=(in_vmem(),) * 3,
        **call(
            plan_kernel,
            (
                jax.ShapeDtypeStruct((NZ, HALF, 16, LANES), BF16),
                jax.ShapeDtypeStruct((WORDS, LANES), jnp.int32),
                jax.ShapeDtypeStruct((16, LANES), F32),
            ),
        ),
        name="plan",
    )(mine, other)


def deal_kernel(u, table, column, after, *outs):
    words = table[DEAL + 8 * u : DEAL + 8 * u + 8, :]
    for k in range(NY):
        for d in range(DEPTH):
            slot = (words[2 * k + d // 4, 0] >> (4 * (d % 4))) & 15
            pair = column[:, slot >> 1].astype(F32)
            rows = jnp.where((slot & 1) == 1, pair[:, 8:16], pair[:, 0:8])
            for kind in range(2):
                whole = jnp.concatenate([rows[2 * i + kind] for i in range(4)], 0)
                outs[k][d, 2 * kind : 2 * kind + 2] = whole.astype(BF16).reshape(2, 16, LANES)


def deal(u, table, column, after):
    return pl.pallas_call(
        functools.partial(deal_kernel, u),
        in_specs=[in_vmem()] * 2 + [pl.BlockSpec(memory_space=pl.ANY)],
        out_specs=(in_vmem(),) * NY,
        **call(deal_kernel, (jax.ShapeDtypeStruct(HAND, BF16),) * NY),
        name="deal",
    )(table, column, after)


def halve_kernel(queries, cotangent, own_kv, after, keep, send):
    first_core = place()[2] == 0
    for at, far in ((0, queries), (ROWS, cotangent)):
        whole = far[...].astype(F32)
        low = whole[:, 0:RATIO].reshape(ROWS, HD).astype(BF16)
        high = whole[:, RATIO:].reshape(ROWS, HD).astype(BF16)
        keep[at : at + ROWS] = jnp.where(first_core, low, high)
        send[at : at + ROWS] = jnp.where(first_core, high, low)
    for kind in range(2):
        at = 2 * ROWS + TOK * kind
        low, high = own_kv[kind], own_kv[2 + kind]
        keep[at : at + TOK] = jnp.where(first_core, low, high)
        send[at : at + TOK] = jnp.where(first_core, high, low)


def halve(queries, cotangent, own_kv, after):
    return pl.pallas_call(
        halve_kernel,
        in_specs=[in_vmem()] * 3 + [pl.BlockSpec(memory_space=pl.ANY)],
        out_specs=(in_vmem(),) * 2,
        **call(halve_kernel, (jax.ShapeDtypeStruct((2 * ROWS + 2 * TOK, HD), BF16),) * 2),
        name="halve",
    )(queries, cotangent, own_kv, after)


def prepare_kernel(scale, keep, got, q_all, g_all, kv_all):
    for u, side in enumerate((keep, got)):
        q_all[u] = side[0:ROWS]
        weight = scale[8 * u : 8 * u + 1, :]
        g_all[u] = (side[ROWS : 2 * ROWS].astype(F32) * weight).astype(BF16)
        for kind in range(2):
            at = 2 * ROWS + TOK * kind
            kv_all[2 * u + kind] = side[at : at + TOK]


def prepare(scale, keep, got):
    return pl.pallas_call(
        prepare_kernel,
        in_specs=[in_vmem()] * 3,
        out_specs=(in_vmem(),) * 3,
        **call(
            prepare_kernel,
            (jax.ShapeDtypeStruct((2, ROWS, HD), BF16),) * 2
            + (jax.ShapeDtypeStruct((4, TOK, HD), BF16),),
        ),
        name="prepare",
    )(scale, keep, got)


def rows_of(part, kind):
    return part[:, 2 * kind : 2 * kind + 2].reshape(PART, HD)


def one_part(keys, values, q, g, mask, exps, pgs, stats, at):
    s = lax.dot_general(keys, q, NT, preferred_element_type=F32) * (
        math.log2(math.e) / math.sqrt(HD)
    )
    s = mask(s)
    top = jnp.max(s, axis=0, keepdims=True)
    e = jnp.exp2(s - top)
    pg = lax.dot_general(values, g, NT, preferred_element_type=F32)
    exps[...] = e
    pgs[...] = pg
    stats[at : at + 1, :] = top
    stats[at + 1 : at + 2, :] = jnp.sum(e, axis=0, keepdims=True)
    stats[at + 2 : at + 3, :] = jnp.sum(e * pg, axis=0, keepdims=True)


def causal(s):
    key_pos = lax.broadcasted_iota(jnp.int32, s.shape, 0)
    query_pos = lax.broadcasted_iota(jnp.int32, s.shape, 1) // RATIO
    return jnp.where(key_pos <= query_pos, s, -1e30)


def listed(h, table):
    def mask(s):
        parts = []
        for d in range(DEPTH):
            seen = jnp.concatenate([table[LINE + 8 * h + d : LINE + 8 * h + d + 1, :]] * (ROWS // LANES), 1) > 0
            parts.append(jnp.where(seen, s[32 * d : 32 * d + 32], -1e30))
        return jnp.concatenate(parts, 0)

    return mask


def scores_kernel(h, table, q_all, g_all, part, after, exps, pgs, stats):
    keys, values = rows_of(part, 0), rows_of(part, 1)
    one_part(keys, values, q_all[h], g_all[h], listed(h, table), exps, pgs, stats, 0)


def first_scores_kernel(h, table, q_all, g_all, part, own_kv, exps, pgs, stats, own_exps, own_pgs):
    keys, values = rows_of(part, 0), rows_of(part, 1)
    q, g = q_all[h], g_all[h]
    one_part(keys, values, q, g, listed(h, table), exps, pgs, stats, 0)
    one_part(own_kv[2 * h], own_kv[2 * h + 1], q, g, causal, own_exps, own_pgs, stats, 4)


def wide(keys):
    return jax.ShapeDtypeStruct((keys, ROWS), F32)


STATS = jax.ShapeDtypeStruct((8, TOK * RATIO), F32)


def scores_of(h, table, q_all, g_all, part, after):
    return pl.pallas_call(
        functools.partial(scores_kernel, h),
        in_specs=[in_vmem()] * 4 + [pl.BlockSpec(memory_space=pl.ANY)],
        out_specs=(in_vmem(),) * 3,
        **call(scores_kernel, (wide(PART), wide(PART), STATS), vmem_mb=16),
        cost_estimate=cost(PART, 2),
        name="scores",
    )(table, q_all, g_all, part, after)


def first_scores_of(h, table, q_all, g_all, part, own_kv):
    return pl.pallas_call(
        functools.partial(first_scores_kernel, h),
        in_specs=[in_vmem()] * 5,
        out_specs=(in_vmem(),) * 5,
        **call(
            first_scores_kernel,
            (wide(PART), wide(PART), STATS, wide(TOK), wide(TOK)),
            vmem_mb=16,
        ),
        cost_estimate=cost(PART + TOK, 2),
        name="scores_first",
    )(table, q_all, g_all, part, own_kv)


def cost(keys, products):
    return pl.CostEstimate(
        flops=2 * products * ROWS * keys * HD,
        bytes_accessed=8 * ROWS * keys,
        transcendentals=ROWS * keys,
    )


SMALL = pl.CostEstimate(flops=1000, bytes_accessed=1000, transcendentals=0)


def merge(stats):
    rows = [(ref, 0) for ref in stats] + [(stats[0], 4)]
    tops = [ref[at : at + 1, :] for ref, at in rows]
    top = tops[0]
    for t in tops[1:]:
        top = jnp.maximum(top, t)
    shares = [jnp.exp2(t - top) for t in tops]
    norm = sum(s * ref[at + 1 : at + 2, :] for s, (ref, at) in zip(shares, rows))
    norm = 1.0 / norm
    shares = [s * norm for s in shares]
    delta = sum(s * ref[at + 2 : at + 3, :] for s, (ref, at) in zip(shares, rows))
    return shares, delta


def one_grad(e, pg, share, delta, q, g, keys):
    p = e * share
    low = p.astype(BF16)
    ds = (p * (pg - delta)).astype(BF16)
    factor = 1.0 / math.sqrt(HD)
    dv = lax.dot_general(low, g, NN, preferred_element_type=F32)
    dk = lax.dot_general(ds, q, NN, preferred_element_type=F32) * factor
    turned = keys.astype(F32).T.astype(BF16)
    dq = lax.dot_general(turned, ds, NN, preferred_element_type=F32)
    return dq, dk, dv


def part_grad(k, h, table, stats, exps, pgs, q_all, g_all, part, own_grad, contrib):
    shares, delta = merge(stats)
    dq, dk, dv = one_grad(
        exps[...], pgs[...], shares[k], delta, q_all[h], g_all[h], rows_of(part, 0)
    )
    piece = lax.rem(place()[0] + NY - k, NY)
    for kind, grad in enumerate((dk, dv)):
        own = own_grad[kind, pl.ds(pl.multiple_of(piece * 32, 32), 32), :]
        for d in range(DEPTH):
            mark = table[SELF + 8 * h + d : SELF + 8 * h + d + 1, :] > 0
            both = jnp.where(mark, own, grad[32 * d : 32 * d + 32])
            contrib[d, 2 * kind : 2 * kind + 2] = both.astype(BF16).reshape(2, 16, HD)
    return dq


def first_grads_kernel(
    k, h, table, s0, s1, s2, s3, exps, pgs, q_all, g_all, part, own_exps, own_pgs, own_kv,
    dq_sum, own_grad, contrib,
):
    stats = (s0, s1, s2, s3)
    shares, delta = merge(stats)
    dq, dk, dv = one_grad(
        own_exps[...], own_pgs[...], shares[NY], delta, q_all[h], g_all[h], own_kv[2 * h]
    )
    own_grad[0] = dk
    own_grad[1] = dv
    dq_sum[...] = dq + part_grad(
        k, h, table, stats, exps, pgs, q_all, g_all, part, own_grad, contrib
    )


def grads_kernel(
    k, h, table, s0, s1, s2, s3, exps, pgs, q_all, g_all, part, own_grad, dq_in, *outs
):
    dq_sum, contrib = outs[-2:]
    dq_sum[...] = dq_in[...] + part_grad(
        k, h, table, (s0, s1, s2, s3), exps, pgs, q_all, g_all, part, own_grad, contrib
    )


def emit_kernel(table, dq_0, dq_1, own_0, own_1, keep, send, squares):
    total = jnp.zeros((8, HD), F32)
    for u, (dq, own, out) in enumerate(((dq_0, own_0, keep), (dq_1, own_1, send))):
        dq = dq[...].T * (1.0 / math.sqrt(HD))
        total = total + jnp.sum((dq * dq).reshape(ROWS // 8, 8, HD), axis=0)
        out[0:ROWS] = dq
        own = own[...]
        own_squares = jnp.sum((own * own).reshape(2 * TOK // 8, 8, HD), axis=0)
        inner = table[INNER + 8 * u : INNER + 8 * u + 8, :] > 0
        total = total + jnp.where(inner, 0.0, own_squares)
    send[ROWS : ROWS + TOK] = own_1[0]
    send[ROWS + TOK :] = own_1[1]
    squares[...] = total


def emit(table, dqs, owns):
    return pl.pallas_call(
        emit_kernel,
        in_specs=[in_vmem()] * 5,
        out_specs=(in_vmem(),) * 3,
        **call(
            emit_kernel,
            (
                jax.ShapeDtypeStruct((ROWS, HD), F32),
                jax.ShapeDtypeStruct((ROWS + 2 * TOK, HD), F32),
                jax.ShapeDtypeStruct((8, LANES), F32),
            ),
            vmem_mb=16,
        ),
        cost_estimate=SMALL,
        name="emit",
    )(table, *dqs, *owns)


def assemble_kernel(keep, got, query_grad, token):
    first_core = place()[2] == 0
    near, far = keep[...], got[0:ROWS]
    low, high = jnp.where(first_core, near, far), jnp.where(first_core, far, near)
    query_grad[:, 0:RATIO, :] = low.reshape(TOK, RATIO, HD)
    query_grad[:, RATIO:, :] = high.reshape(TOK, RATIO, HD)
    token[...] = jnp.zeros_like(token)


def assemble(keep, got):
    return pl.pallas_call(
        assemble_kernel,
        in_specs=[in_vmem()] * 2,
        out_specs=(in_vmem(),) * 2,
        **call(
            assemble_kernel,
            (
                jax.ShapeDtypeStruct((TOK, KV * RATIO, HD), F32),
                jax.ShapeDtypeStruct((8, LANES), F32),
            ),
            vmem_mb=16,
        ),
        cost_estimate=SMALL,
        name="assemble",
    )(keep, got)


def grads_of(body, name, outs, k, h, *arrays):
    return pl.pallas_call(
        functools.partial(body, k, h),
        in_specs=[in_vmem()] * len(arrays),
        out_specs=(in_vmem(),) * len(outs),
        **call(body, outs, vmem_mb=16),
        cost_estimate=SMALL,
        name=name,
    )(*arrays)


def attend(h, table, q_all, g_all, own_kv, parts, after, hints):
    e, pg, st = [None] * NY, [None] * NY, [None] * NY
    e[0], pg[0], st[0], own_e, own_pg = first_scores_of(h, table, q_all, g_all, parts[0], own_kv)
    after = st[0] if after is None else after
    for k in (1, 2, 3):
        e[k], pg[k], st[k] = scores_of(h, table, q_all, g_all, parts[k], after)
        after = st[k]
    back = [None] * NY
    dq_type = jax.ShapeDtypeStruct((HD, ROWS), F32)
    own_type = jax.ShapeDtypeStruct((2, TOK, HD), F32)
    contrib_type = jax.ShapeDtypeStruct(HAND, BF16)

    def shared(k):
        return (table, *st, e[k], pg[k], q_all, g_all, parts[k])

    dq, own_grad, back[2] = grads_of(
        first_grads_kernel, "grads_first", (dq_type, own_type, contrib_type), 2, h,
        *shared(2), own_e, own_pg, own_kv,
    )
    for k, hint in ((1, hints[:1]), (3, hints[1:])):
        dq, back[k] = grads_of(
            grads_kernel, "grads", (dq_type, contrib_type), k, h, *shared(k), own_grad, dq, *hint
        )

    def last(after):
        return grads_of(
            grads_kernel, "grads_last", (dq_type, contrib_type), 0, h, *shared(0), own_grad, dq, after
        )

    return dq, own_grad, back, last


def add_part(k, u, table, part, acc):
    at = BACK + 8 * u + 2 * k
    words = table[at : at + 2, :]
    for d in range(DEPTH):
        slot = (words[d // 4, 0] >> (5 * (d % 4))) & 31
        acc[jnp.maximum(slot - 1, 0)] += jnp.where(slot > 0, part[d].astype(F32), 0.0)


def combine_first_kernel(table, part_1, part_2, acc, token):
    acc[...] = jnp.zeros_like(acc)
    add_part(1, 0, table, part_1, acc)
    add_part(2, 0, table, part_2, acc)
    token[...] = jnp.zeros_like(token)


def combine_kernel(ks, u, table, *refs):
    acc = refs[len(ks) + 2]
    for token in refs[len(ks) + 3 :]:
        token[...] = jnp.zeros_like(token)
    for k, part in zip(ks, refs):
        add_part(k, u, table, part, acc)


def leave_kernel(acc, halves):
    for z in range(NZ):
        at = 2 * (z % 2) + z // 4
        rows = slice(8 * (z // 2 % 2), 8 * (z // 2 % 2) + 8)
        halves[z] = acc[:, at, rows, :].reshape(HALF, 16, LANES).astype(BF16)


ACC = (2 * HALF, QUAD, 16, LANES)


def acc_and_token():
    return jax.ShapeDtypeStruct(ACC, F32), jax.ShapeDtypeStruct((8, LANES), F32)


def combine_start(table, part_1, part_2):
    return pl.pallas_call(
        combine_first_kernel,
        in_specs=[in_vmem()] * 3,
        out_specs=(in_vmem(),) * 2,
        **call(combine_first_kernel, acc_and_token(), vmem_mb=16),
        cost_estimate=SMALL,
        name="combine_first",
    )(table, part_1, part_2)


def combine_more(ks, u, table, parts, acc, after, outs=1):
    return pl.pallas_call(
        functools.partial(combine_kernel, ks, u),
        in_specs=[in_vmem()] * (2 + len(parts)) + [pl.BlockSpec(memory_space=pl.ANY)],
        out_specs=(in_vmem(),) * outs,
        input_output_aliases={1 + len(parts): 0},
        **call(combine_kernel, acc_and_token()[:outs], vmem_mb=16),
        cost_estimate=SMALL,
        name="combine",
    )(table, *parts, acc, after)


def leave(acc):
    return pl.pallas_call(
        leave_kernel,
        in_specs=[in_vmem()],
        out_specs=in_vmem(),
        **call(leave_kernel, jax.ShapeDtypeStruct((NZ, HALF, 16, LANES), BF16), vmem_mb=16),
        cost_estimate=SMALL,
        name="leave",
    )(acc)


def split_rows(value, rows):
    high = value.astype(BF16).astype(F32)
    middle = (value - high).astype(BF16).astype(F32)
    low = value - high - middle
    row = lax.broadcasted_iota(jnp.int32, (8, LANES), 0)
    tile = jnp.where(row == 0, high, jnp.where(row == 1, middle, jnp.where(row == 2, low, 0.0)))
    if rows > 8:
        tile = jnp.concatenate([tile, jnp.zeros((rows - 8, LANES), F32)], 0)
    return tile


def total_kernel(parts, squares, totals, sums):
    sums_now = parts[0].astype(F32)
    for z in range(1, NZ):
        sums_now = sums_now + parts[z].astype(F32)
    totals[...] = sums_now
    tile = squares[...] + jnp.sum((sums_now * sums_now).reshape(HALF * 2, 8, LANES), axis=0)
    sums[...] = jnp.broadcast_to(jnp.sum(tile, axis=0, keepdims=True), (8, LANES))


def route_kernel(table, parts, squares, out, room, totals, sums):
    total_kernel(parts, squares, totals, sums)
    c = place()[2]
    words = table[HOLD : HOLD + 8, :]
    room[...] = jnp.zeros_like(room)
    for s in range(2 * HALF):
        block = ((words[s // 3, 0] >> (7 * (s % 3))) & 127) - 1
        side = jnp.where((block & 1) == c, 0, 1)
        to = jnp.where(block >= 0, (block >> 1) * 2 + side, NBLK)
        room[to] = totals[s // 2, 8 * (s % 2) : 8 * (s % 2) + 8, :]
    tails = jnp.broadcast_to(split_rows(sums[...], 8)[None], (NY * NZ, 8, LANES))
    rows = room[0:NBLK].reshape(NY * NZ, 16, LANES)
    out[...] = jnp.concatenate([rows, tails], 1).astype(BF16)


def route(table, parts, squares):
    return pl.pallas_call(
        route_kernel,
        in_specs=[in_vmem()] * 3,
        out_specs=in_vmem(),
        **call(
            route_kernel,
            jax.ShapeDtypeStruct((NY * NZ, 24, LANES), BF16),
            [
                VMEM((NBLK + 1, 8, LANES), F32),
                VMEM((HALF, 16, LANES), F32),
                VMEM((8, LANES), F32),
            ],
        ),
        name="route",
    )(table, parts, squares)


def share_kernel(arrived, after, send, sums):
    whole = arrived[...].astype(F32)
    send[...] = whole[:, 8:16, :].reshape(NY * NZ // 2, 16, LANES).astype(BF16)
    tails = jnp.sum(jnp.sum(whole[:, 16:24, :], axis=0), axis=0, keepdims=True)
    sums[...] = jnp.broadcast_to(jnp.sum(tails, axis=1, keepdims=True), (1, LANES))


def share(arrived, after):
    return pl.pallas_call(
        share_kernel,
        in_specs=[in_vmem(), pl.BlockSpec(memory_space=pl.ANY)],
        out_specs=(in_vmem(),) * 2,
        **call(
            share_kernel,
            (
                jax.ShapeDtypeStruct((NY * NZ // 2, 16, LANES), BF16),
                jax.ShapeDtypeStruct((1, LANES), F32),
            ),
        ),
        name="share",
    )(arrived, after)


def finish_kernel(table, arrived, got, own, own_far, key_grad, value_grad, token):
    token[...] = jnp.zeros_like(token)
    first_core = place()[2] == 0
    inner = table[INNER : INNER + 1, :] > 0
    for z in range(NZ):
        kind = z % 2
        out = value_grad if kind else key_grad
        for y in range(NY):
            at, src = row_of(y, z), y * NZ + z
            near = arrived[src].astype(F32)[0:8]
            far = got[src // 2].astype(F32)[8 * (src % 2) : 8 * (src % 2) + 8]
            near = jnp.where(inner, near, own[kind, at : at + 8, :])
            low = ROWS + TOK * kind + at
            far = jnp.where(inner, far, own_far[low : low + 8, :])
            out[at : at + 8, 0, :] = jnp.where(first_core, near, far)
            out[at : at + 8, 1, :] = jnp.where(first_core, far, near)


def finish(*arrays):
    return pl.pallas_call(
        finish_kernel,
        in_specs=[in_vmem()] * 5,
        out_specs=(in_vmem(),) * 3,
        **call(
            finish_kernel,
            (jax.ShapeDtypeStruct((TOK, KV, HD), F32),) * 2
            + (jax.ShapeDtypeStruct((1, LANES), F32),),
        ),
        cost_estimate=SMALL,
        name="finish",
    )(*arrays)


def local(queries, keys, values, cotangent, rewards, groups, ancestors, step_ids):
    packet, own_kv = packet_of(keys, values, ancestors, groups, rewards)
    mine = swap_yz(packet)
    other = other_core(mine)
    trained = (step_ids[0] % 2 == 0)[:, None, None]
    masked = jnp.where(trained, cotangent, jnp.zeros_like(cotangent))
    picked, table, scale = plan(mine, other)
    column = swap_z(picked)
    first = deal(0, table, column, table)
    keep, send = halve(queries, masked, own_kv, table)
    q_all, g_all, kv_all = prepare(scale, keep, other_core(send))
    parts = []
    for u in range(2):
        dealt = first if u == 0 else deal(u, table, column, first[0])
        parts.append([dealt[0]] + [along_y(dealt[k], k) for k in (1, 2, 3)])
    after, own_0, sent, last_0 = attend(0, table, q_all, g_all, kv_all, parts[0], None, ())
    back_0 = [None] + [along_y(sent[k], -k) for k in (1, 2, 3)]
    acc, token = combine_start(table, back_0[1], back_0[2])
    acc, late_token = combine_more((3,), 0, table, [back_0[3]], acc, table, 2)
    after, own_1, sent, last_1 = attend(
        1, table, q_all, g_all, kv_all, parts[1], after, (token, late_token)
    )
    back_1 = [None] + [along_y(sent[k], -k) for k in (1, 2, 3)]
    dq_0, back_0[0] = last_0(after)
    dq_1, back_1[0] = last_1(dq_0)
    near, far, squares = emit(table, (dq_0, dq_1), (own_0, own_1))
    far = other_core(far)
    query_grad, done = assemble(near, far)
    (acc,) = combine_more((0,), 0, table, [back_0[0]], acc, squares)
    (acc,) = combine_more((1, 0), 1, table, [back_1[1], back_1[0]], acc, squares)
    (acc,) = combine_more((2,), 1, table, [back_1[2]], acc, squares)
    (acc,) = combine_more((3,), 1, table, [back_1[3]], acc, squares)
    halves = leave(acc)
    arrived = swap_yz(route(table, swap_z(halves), squares))
    shared, mine_sum = share(arrived, done)
    all_sum = mine_sum
    for k in (1, 2, 3):
        all_sum = all_sum + along_head(mine_sum, k)
    shared = other_core(shared)
    key_grad, value_grad, token = finish(table, arrived, shared, own_0, far)
    all_sum = all_sum + (other_core(all_sum) + token)
    count = float(NBLK * TOK * NHEAD * (KV * RATIO + 2 * KV) * HD)
    grad_rms = jnp.sqrt(all_sum[0, 0] / count)
    return query_grad, key_grad, value_grad, grad_rms


def solution(mesh):
    in_specs = (
        P("branch", "head", None),
        P("branch", "head", None),
        P("branch", "head", None),
        P("branch", "head", None),
        P("branch"),
        P("branch"),
        P("branch", None),
        P("branch", None),
    )
    out_specs = (
        P("branch", "head", None),
        P("branch", "head", None),
        P("branch", "head", None),
        P(),
    )
    return jax.shard_map(local, mesh=mesh, in_specs=in_specs, out_specs=out_specs, check_vma=False)
```

```python
import functools
import math

import jax
import jax.numpy as jnp
from jax import lax
from jax.experimental import pallas as pl
from jax.experimental.pallas import tpu as pltpu
from jax.sharding import PartitionSpec as P

NY, NZ, NC = 4, 8, 2
NBLK = NY * NZ * NC
NHEAD = 4
GROUP = 4
DEPTH = 8
TOK = 128
HD = 128
KV = 2
RATIO = 8
LANES = 128
HALF = 8
ROWS = TOK * RATIO
QUAD = 4
PART = 32 * DEPTH
HAND = (DEPTH, QUAD, 16, LANES)
F32 = jnp.float32
BF16 = jnp.bfloat16
VMEM = pltpu.VMEM
NT = (((1,), (1,)), ((), ()))
NN = (((1,), (0,)), ((), ()))
TN = (((0,), (0,)), ((), ()))


def index_of(y, z, c):
    return ((y % NY) * NZ + z % NZ) * NC + c % NC


def every():
    return [(y, z, c) for y in range(NY) for z in range(NZ) for c in range(NC)]


def along_y(x, step):
    pairs = [(index_of(y, z, c), index_of(y + step, z, c)) for y, z, c in every()]
    return lax.ppermute(x, "branch", pairs)


def other_core(x):
    pairs = [(index_of(y, z, c), index_of(y, z, c + 1)) for y, z, c in every()]
    return lax.ppermute(x, "branch", pairs)


def along_head(x, step):
    pairs = [(i, (i + step) % NHEAD) for i in range(NHEAD)]
    return lax.ppermute(x, "head", pairs)


def swap_z(x):
    groups = [[index_of(y, z, c) for z in range(NZ)] for y in range(NY) for c in range(NC)]
    return lax.all_to_all(x, "branch", 0, 0, axis_index_groups=groups, tiled=False)


def swap_yz(x):
    groups = [[index_of(y, z, c) for y in range(NY) for z in range(NZ)] for c in range(NC)]
    return lax.all_to_all(x, "branch", 0, 0, axis_index_groups=groups, tiled=False)


def call(body, outs, scratch=(), vmem_mb=32):
    return dict(
        out_shape=outs,
        scratch_shapes=list(scratch),
        compiler_params=pltpu.CompilerParams(vmem_limit_bytes=vmem_mb << 20),
    )


def in_vmem():
    return pl.BlockSpec(memory_space=VMEM)


def place():
    b = lax.axis_index("branch")
    return b // (NZ * NC), (b // NC) % NZ, b % NC


LINE = 0
DEAL = 16
BACK = 32
HOLD = 48
INNER = 56
SELF = 72
WORDS = 88


def row_of(y, z):
    return 32 * y + 8 * (z // 2)


def packet_kernel(
    keys_far, values_far, ancestors_far, group, reward, packet, own_kv,
    keys, values, ancestors, sems,
):
    pairs = (
        (ancestors_far, ancestors),
        (keys_far, keys),
        (values_far, values),
    )
    copies = [pltpu.make_async_copy(a, b, sems.at[i]) for i, (a, b) in enumerate(pairs)]
    for copy in copies:
        copy.start()
    for copy in copies[:1]:
        copy.wait()
    row = lax.broadcasted_iota(jnp.int32, (8, LANES), 0)
    lane = lax.broadcasted_iota(jnp.int32, (8, LANES), 1)
    spot = lax.broadcasted_iota(jnp.int32, (8, DEPTH), 0) == lax.broadcasted_iota(
        jnp.int32, (8, DEPTH), 1
    )
    line = jnp.broadcast_to(ancestors[...].astype(F32), (8, DEPTH))
    line = jnp.sum(jnp.where(spot, line, 0.0), axis=1, keepdims=True)
    facts = jnp.where(
        row == 0, group[0].astype(F32), jnp.where(row == 1, reward[0].astype(F32), 0.0)
    )
    meta = jnp.where(lane < NBLK, line, facts)
    for copy in copies[1:]:
        copy.wait()
    for h in range(KV):
        own_kv[2 * h] = keys[:, h, :]
        own_kv[2 * h + 1] = values[:, h, :]
    whole = [own_kv[i].astype(F32) for i in range(2 * KV)]
    for z in range(NZ):
        for y in range(NY):
            at = row_of(y, z)
            rows = [whole[2 * h + z % 2][at : at + 8] for h in range(KV)]
            packet[y * NZ + z] = jnp.concatenate(rows + [meta], 0).astype(BF16)


def packet_of(keys, values, ancestors, group, reward):
    return pl.pallas_call(
        packet_kernel,
        in_specs=[pl.BlockSpec(memory_space=pltpu.HBM)] * 3
        + [pl.BlockSpec(memory_space=pltpu.SMEM)] * 2,
        out_specs=(in_vmem(),) * 2,
        **call(
            packet_kernel,
            (
                jax.ShapeDtypeStruct((NY * NZ, 24, LANES), BF16),
                jax.ShapeDtypeStruct((2 * KV, TOK, HD), BF16),
            ),
            [VMEM(x.shape, x.dtype) for x in (keys, values, ancestors)]
            + [pltpu.SemaphoreType.DMA((3,))],
            vmem_mb=62,
        ),
        name="packet",
    )(keys, values, ancestors, group, reward)


def pack_rows(x, base, first, count):
    row = lax.broadcasted_iota(jnp.int32, (8, LANES), 0)
    weight = jnp.zeros((8, LANES), F32)
    for i in range(count):
        weight = jnp.where(row == first + i, float(base**i), weight)
    return jnp.sum(x * weight, axis=0, keepdims=True)


def plan_kernel(mine, other, picked, table, scale):
    y, z, c = place()
    meta_m = mine[...].astype(F32)[:, 16:24, :]
    meta_o = other[...].astype(F32)[:, 16:24, :]
    row = lax.broadcasted_iota(jnp.int32, (8, LANES), 0)
    row_f = row.astype(F32)
    lane = lax.broadcasted_iota(jnp.int32, (8, LANES), 1)
    lane_f = lane.astype(F32)
    is_block = lane < NBLK
    wide_lane = lax.broadcasted_iota(jnp.int32, (NY * NZ, LANES), 1).astype(F32)
    hit = jnp.maximum(
        jnp.where(meta_m[:, 0, :] == wide_lane, 1.0, 0.0),
        jnp.where(meta_o[:, 0, :] == wide_lane, 1.0, 0.0),
    )
    inner = jnp.max(hit, axis=0, keepdims=True)
    inner = jnp.where(is_block, jnp.broadcast_to(inner, (8, LANES)), 0.0)
    before = (
        lax.broadcasted_iota(jnp.int32, (LANES, LANES), 0)
        < lax.broadcasted_iota(jnp.int32, (LANES, LANES), 1)
    ).astype(F32).astype(BF16)
    rank = lax.dot_general(inner.astype(BF16), before, NN, preferred_element_type=F32)
    slots = jnp.where(inner > 0.0, rank + 1.0, 0.0)

    words = []
    for first in (0, 8):
        wanted = row_f + float(first + 1)
        index = jnp.sum(jnp.where(slots == wanted, lane_f, 0.0), axis=1, keepdims=True)
        index = jnp.broadcast_to(index, (8, LANES))
        words += [pack_rows(index, 64, at, 4).astype(jnp.int32)[0, 0] for at in (0, 4)]
    pieces = []
    for s in range(2 * HALF):
        block = (words[s // 4] >> (6 * (s % 4))) & 63
        at = block >> 1
        piece = jnp.where((block & 1) == c, mine[at].astype(F32), other[at].astype(F32))
        pieces.append(jnp.where(c == 0, piece[0:8], piece[8:16]))
    for j in range(HALF):
        pair = jnp.concatenate(pieces[2 * j : 2 * j + 2], 0).astype(BF16)
        picked[:, j] = jnp.broadcast_to(pair[None], (NZ, 16, LANES))

    for k in range(NY):
        yy = lax.rem(y + k, NY)
        for u, side in enumerate((mine, other)):
            line = side[yy * NZ + z].astype(F32)[16:24, :]
            same = (line == lane_f) & is_block
            slot = jnp.sum(jnp.where(same, slots, 0.0), axis=1, keepdims=True)
            slot = jnp.broadcast_to(slot, (8, LANES))
            block = (yy * NZ + z) * NC + (c if u == 0 else 1 - c)
            own = jnp.sum(jnp.where(lane == block, slots, 0.0), axis=1, keepdims=True)
            own = jnp.broadcast_to(own, (8, LANES))
            depth = jnp.sum(jnp.where(slot > 0.0, 1.0, 0.0), axis=0, keepdims=True)
            entry = jnp.where(row_f == depth, own, slot)
            dealt = jnp.maximum(slot - 1.0, 0.0)
            for half in range(2):
                at = 8 * u + 2 * k + half
                word = pack_rows(dealt, 16, 4 * half, 4)
                table[DEAL + at : DEAL + at + 1, :] = word.astype(jnp.int32)
                word = pack_rows(entry, 32, 4 * half, 4)
                table[BACK + at : BACK + at + 1, :] = word.astype(jnp.int32)
            if k == 0:
                at = 8 * u
                table[LINE + at : LINE + at + 8, :] = slot.astype(jnp.int32)
                table[INNER + at : INNER + at + 8, :] = own.astype(jnp.int32)
                mark = jnp.where(row_f == depth, own, 0.0)
                table[SELF + at : SELF + at + 8, :] = mark.astype(jnp.int32)
    for i in range(6):
        word = jnp.zeros((8, 1), F32)
        for j in range(3):
            held = jnp.where(slots == float(3 * i + j + 1), lane_f + 1.0, 0.0)
            word = word + jnp.sum(held, axis=1, keepdims=True) * float(128**j)
        table[HOLD + i : HOLD + i + 1, :] = jnp.broadcast_to(word, (8, LANES)).astype(jnp.int32)[0:1]

    for u, side in enumerate((mine, other)):
        here = side[y * NZ + z].astype(F32)[16:24, :]
        group, reward = here[0:1, :], here[1:2, :]
        in_m = jnp.where(meta_m[:, 0, :] == group, meta_m[:, 1, :], 0.0)
        in_o = jnp.where(meta_o[:, 0, :] == group, meta_o[:, 1, :], 0.0)
        total = jnp.sum(in_m + in_o, axis=0, keepdims=True)
        squares = jnp.sum(in_m * in_m + in_o * in_o, axis=0, keepdims=True)
        mean = total / GROUP
        spread = jnp.sqrt(jnp.maximum(squares / GROUP - mean * mean, 0.25))
        advantage = (reward - mean) / spread
        advantage = jnp.sum(jnp.where(lane[0:1] == NBLK, advantage, 0.0), axis=1, keepdims=True)
        scale[8 * u : 8 * u + 8] = jnp.broadcast_to(advantage, (8, LANES))


def plan(mine, other):
    return pl.pallas_call(
        plan_kernel,
        in_specs=[in_vmem()] * 2,
        out_specs=(in_vmem(),) * 3,
        **call(
            plan_kernel,
            (
                jax.ShapeDtypeStruct((NZ, HALF, 16, LANES), BF16),
                jax.ShapeDtypeStruct((WORDS, LANES), jnp.int32),
                jax.ShapeDtypeStruct((16, LANES), F32),
            ),
        ),
        name="plan",
    )(mine, other)


def deal_kernel(u, table, column, after, *outs):
    words = table[DEAL + 8 * u : DEAL + 8 * u + 8, :]
    for k in range(NY):
        for d in range(DEPTH):
            slot = (words[2 * k + d // 4, 0] >> (4 * (d % 4))) & 15
            pair = column[:, slot >> 1].astype(F32)
            rows = jnp.where((slot & 1) == 1, pair[:, 8:16], pair[:, 0:8])
            for kind in range(2):
                whole = jnp.concatenate([rows[2 * i + kind] for i in range(4)], 0)
                outs[k][d, 2 * kind : 2 * kind + 2] = whole.astype(BF16).reshape(2, 16, LANES)


def deal(u, table, column, after):
    return pl.pallas_call(
        functools.partial(deal_kernel, u),
        in_specs=[in_vmem()] * 2 + [pl.BlockSpec(memory_space=pl.ANY)],
        out_specs=(in_vmem(),) * NY,
        **call(deal_kernel, (jax.ShapeDtypeStruct(HAND, BF16),) * NY),
        name="deal",
    )(table, column, after)


def halve_kernel(queries, cotangent, own_kv, after, keep, send):
    first_core = place()[2] == 0
    for at, far in ((0, queries), (ROWS, cotangent)):
        whole = far[...].astype(F32)
        low = whole[:, 0:RATIO].reshape(ROWS, HD).astype(BF16)
        high = whole[:, RATIO:].reshape(ROWS, HD).astype(BF16)
        keep[at : at + ROWS] = jnp.where(first_core, low, high)
        send[at : at + ROWS] = jnp.where(first_core, high, low)
    for kind in range(2):
        at = 2 * ROWS + TOK * kind
        low, high = own_kv[kind], own_kv[2 + kind]
        keep[at : at + TOK] = jnp.where(first_core, low, high)
        send[at : at + TOK] = jnp.where(first_core, high, low)


def halve(queries, cotangent, own_kv, after):
    return pl.pallas_call(
        halve_kernel,
        in_specs=[in_vmem()] * 3 + [pl.BlockSpec(memory_space=pl.ANY)],
        out_specs=(in_vmem(),) * 2,
        **call(halve_kernel, (jax.ShapeDtypeStruct((2 * ROWS + 2 * TOK, HD), BF16),) * 2),
        name="halve",
    )(queries, cotangent, own_kv, after)


def prepare_kernel(scale, keep, got, q_all, g_all, kv_all):
    for u, side in enumerate((keep, got)):
        q_all[u] = side[0:ROWS]
        weight = scale[8 * u : 8 * u + 1, :]
        g_all[u] = (side[ROWS : 2 * ROWS].astype(F32) * weight).astype(BF16)
        for kind in range(2):
            at = 2 * ROWS + TOK * kind
            kv_all[2 * u + kind] = side[at : at + TOK]


def prepare(scale, keep, got):
    return pl.pallas_call(
        prepare_kernel,
        in_specs=[in_vmem()] * 3,
        out_specs=(in_vmem(),) * 3,
        **call(
            prepare_kernel,
            (jax.ShapeDtypeStruct((2, ROWS, HD), BF16),) * 2
            + (jax.ShapeDtypeStruct((4, TOK, HD), BF16),),
        ),
        name="prepare",
    )(scale, keep, got)


def rows_of(part, kind):
    return part[:, 2 * kind : 2 * kind + 2].reshape(PART, HD)


def one_part(keys, values, q, g, mask, exps, pgs, stats, at):
    s = lax.dot_general(keys, q, NT, preferred_element_type=F32) * (
        math.log2(math.e) / math.sqrt(HD)
    )
    s = mask(s)
    top = jnp.max(s, axis=0, keepdims=True)
    e = jnp.exp2(s - top)
    pg = lax.dot_general(values, g, NT, preferred_element_type=F32)
    exps[...] = e
    pgs[...] = pg
    stats[at : at + 1, :] = top
    stats[at + 1 : at + 2, :] = jnp.sum(e, axis=0, keepdims=True)
    stats[at + 2 : at + 3, :] = jnp.sum(e * pg, axis=0, keepdims=True)


def causal(s):
    key_pos = lax.broadcasted_iota(jnp.int32, s.shape, 0)
    query_pos = lax.broadcasted_iota(jnp.int32, s.shape, 1) // RATIO
    return jnp.where(key_pos <= query_pos, s, -1e30)


def listed(h, table):
    def mask(s):
        parts = []
        for d in range(DEPTH):
            seen = jnp.concatenate([table[LINE + 8 * h + d : LINE + 8 * h + d + 1, :]] * (ROWS // LANES), 1) > 0
            parts.append(jnp.where(seen, s[32 * d : 32 * d + 32], -1e30))
        return jnp.concatenate(parts, 0)

    return mask


def scores_kernel(h, table, q_all, g_all, part, after, exps, pgs, stats):
    keys, values = rows_of(part, 0), rows_of(part, 1)
    one_part(keys, values, q_all[h], g_all[h], listed(h, table), exps, pgs, stats, 0)


def first_scores_kernel(h, table, q_all, g_all, part, own_kv, exps, pgs, stats, own_exps, own_pgs):
    keys, values = rows_of(part, 0), rows_of(part, 1)
    q, g = q_all[h], g_all[h]
    one_part(keys, values, q, g, listed(h, table), exps, pgs, stats, 0)
    one_part(own_kv[2 * h], own_kv[2 * h + 1], q, g, causal, own_exps, own_pgs, stats, 4)


def wide(keys):
    return jax.ShapeDtypeStruct((keys, ROWS), F32)


STATS = jax.ShapeDtypeStruct((8, TOK * RATIO), F32)


def scores_of(h, table, q_all, g_all, part, after):
    return pl.pallas_call(
        functools.partial(scores_kernel, h),
        in_specs=[in_vmem()] * 4 + [pl.BlockSpec(memory_space=pl.ANY)],
        out_specs=(in_vmem(),) * 3,
        **call(scores_kernel, (wide(PART), wide(PART), STATS), vmem_mb=16),
        cost_estimate=cost(PART, 2),
        name="scores",
    )(table, q_all, g_all, part, after)


def first_scores_of(h, table, q_all, g_all, part, own_kv):
    return pl.pallas_call(
        functools.partial(first_scores_kernel, h),
        in_specs=[in_vmem()] * 5,
        out_specs=(in_vmem(),) * 5,
        **call(
            first_scores_kernel,
            (wide(PART), wide(PART), STATS, wide(TOK), wide(TOK)),
            vmem_mb=16,
        ),
        cost_estimate=cost(PART + TOK, 2),
        name="scores_first",
    )(table, q_all, g_all, part, own_kv)


def cost(keys, products):
    return pl.CostEstimate(
        flops=2 * products * ROWS * keys * HD,
        bytes_accessed=8 * ROWS * keys,
        transcendentals=ROWS * keys,
    )


SMALL = pl.CostEstimate(flops=1000, bytes_accessed=1000, transcendentals=0)


def merge(stats):
    rows = [(ref, 0) for ref in stats] + [(stats[0], 4)]
    tops = [ref[at : at + 1, :] for ref, at in rows]
    top = tops[0]
    for t in tops[1:]:
        top = jnp.maximum(top, t)
    shares = [jnp.exp2(t - top) for t in tops]
    norm = sum(s * ref[at + 1 : at + 2, :] for s, (ref, at) in zip(shares, rows))
    norm = 1.0 / norm
    shares = [s * norm for s in shares]
    delta = sum(s * ref[at + 2 : at + 3, :] for s, (ref, at) in zip(shares, rows))
    return shares, delta


def one_grad(e, pg, share, delta, q, g, keys):
    p = e * share
    low = p.astype(BF16)
    ds = (p * (pg - delta)).astype(BF16)
    factor = 1.0 / math.sqrt(HD)
    dv = lax.dot_general(low, g, NN, preferred_element_type=F32)
    dk = lax.dot_general(ds, q, NN, preferred_element_type=F32) * factor
    turned = keys.astype(F32).T.astype(BF16)
    dq = lax.dot_general(turned, ds, NN, preferred_element_type=F32)
    return dq, dk, dv


def part_grad(k, h, table, stats, exps, pgs, q_all, g_all, part, own_grad, contrib):
    shares, delta = merge(stats)
    dq, dk, dv = one_grad(
        exps[...], pgs[...], shares[k], delta, q_all[h], g_all[h], rows_of(part, 0)
    )
    piece = lax.rem(place()[0] + NY - k, NY)
    for kind, grad in enumerate((dk, dv)):
        own = own_grad[kind, pl.ds(pl.multiple_of(piece * 32, 32), 32), :]
        for d in range(DEPTH):
            mark = table[SELF + 8 * h + d : SELF + 8 * h + d + 1, :] > 0
            both = jnp.where(mark, own, grad[32 * d : 32 * d + 32])
            contrib[d, 2 * kind : 2 * kind + 2] = both.astype(BF16).reshape(2, 16, HD)
    return dq


def first_grads_kernel(
    k, h, table, s0, s1, s2, s3, exps, pgs, q_all, g_all, part, own_exps, own_pgs, own_kv,
    dq_sum, own_grad, contrib,
):
    stats = (s0, s1, s2, s3)
    shares, delta = merge(stats)
    dq, dk, dv = one_grad(
        own_exps[...], own_pgs[...], shares[NY], delta, q_all[h], g_all[h], own_kv[2 * h]
    )
    own_grad[0] = dk
    own_grad[1] = dv
    dq_sum[...] = dq + part_grad(
        k, h, table, stats, exps, pgs, q_all, g_all, part, own_grad, contrib
    )


def grads_kernel(
    k, h, table, s0, s1, s2, s3, exps, pgs, q_all, g_all, part, own_grad, dq_in, *outs
):
    dq_sum, contrib = outs[-2:]
    dq_sum[...] = dq_in[...] + part_grad(
        k, h, table, (s0, s1, s2, s3), exps, pgs, q_all, g_all, part, own_grad, contrib
    )


def emit_kernel(table, dq_0, dq_1, own_0, own_1, keep, send, squares):
    total = jnp.zeros((8, HD), F32)
    for u, (dq, own, out) in enumerate(((dq_0, own_0, keep), (dq_1, own_1, send))):
        dq = dq[...].T * (1.0 / math.sqrt(HD))
        total = total + jnp.sum((dq * dq).reshape(ROWS // 8, 8, HD), axis=0)
        out[0:ROWS] = dq
        own = own[...]
        own_squares = jnp.sum((own * own).reshape(2 * TOK // 8, 8, HD), axis=0)
        inner = table[INNER + 8 * u : INNER + 8 * u + 8, :] > 0
        total = total + jnp.where(inner, 0.0, own_squares)
    send[ROWS : ROWS + TOK] = own_1[0]
    send[ROWS + TOK :] = own_1[1]
    squares[...] = total


def emit(table, dqs, owns):
    return pl.pallas_call(
        emit_kernel,
        in_specs=[in_vmem()] * 5,
        out_specs=(in_vmem(),) * 3,
        **call(
            emit_kernel,
            (
                jax.ShapeDtypeStruct((ROWS, HD), F32),
                jax.ShapeDtypeStruct((ROWS + 2 * TOK, HD), F32),
                jax.ShapeDtypeStruct((8, LANES), F32),
            ),
            vmem_mb=16,
        ),
        cost_estimate=SMALL,
        name="emit",
    )(table, *dqs, *owns)


def ship_kernel(far, after, out):
    pass


def ship(far, after):
    return pl.pallas_call(
        ship_kernel,
        in_specs=[in_vmem(), pl.BlockSpec(memory_space=pl.ANY)],
        out_specs=in_vmem(),
        input_output_aliases={0: 0},
        **call(ship_kernel, jax.ShapeDtypeStruct(far.shape, F32), vmem_mb=16),
        cost_estimate=SMALL,
        name="ship",
    )(far, after)


def assemble_kernel(keep, got, query_grad, token):
    first_core = place()[2] == 0
    near, far = keep[...], got[0:ROWS]
    low, high = jnp.where(first_core, near, far), jnp.where(first_core, far, near)
    query_grad[:, 0:RATIO, :] = low.reshape(TOK, RATIO, HD)
    query_grad[:, RATIO:, :] = high.reshape(TOK, RATIO, HD)
    token[...] = jnp.zeros_like(token)


def assemble(keep, got):
    return pl.pallas_call(
        assemble_kernel,
        in_specs=[in_vmem()] * 2,
        out_specs=(in_vmem(),) * 2,
        **call(
            assemble_kernel,
            (
                jax.ShapeDtypeStruct((TOK, KV * RATIO, HD), F32),
                jax.ShapeDtypeStruct((1, LANES), F32),
            ),
            vmem_mb=16,
        ),
        cost_estimate=SMALL,
        name="assemble",
    )(keep, got)


def grads_of(body, name, outs, k, h, *arrays):
    return pl.pallas_call(
        functools.partial(body, k, h),
        in_specs=[in_vmem()] * len(arrays),
        out_specs=(in_vmem(),) * len(outs),
        **call(body, outs, vmem_mb=16),
        cost_estimate=SMALL,
        name=name,
    )(*arrays)


def attend(h, table, q_all, g_all, own_kv, parts, after, hints):
    e, pg, st = [None] * NY, [None] * NY, [None] * NY
    e[0], pg[0], st[0], own_e, own_pg = first_scores_of(h, table, q_all, g_all, parts[0], own_kv)
    after = st[0] if after is None else after
    for k in (1, 2, 3):
        e[k], pg[k], st[k] = scores_of(h, table, q_all, g_all, parts[k], after)
        after = st[k]
    back = [None] * NY
    dq_type = jax.ShapeDtypeStruct((HD, ROWS), F32)
    own_type = jax.ShapeDtypeStruct((2, TOK, HD), F32)
    contrib_type = jax.ShapeDtypeStruct(HAND, BF16)

    def shared(k):
        return (table, *st, e[k], pg[k], q_all, g_all, parts[k])

    dq, own_grad, back[2] = grads_of(
        first_grads_kernel, "grads_first", (dq_type, own_type, contrib_type), 2, h,
        *shared(2), own_e, own_pg, own_kv,
    )
    for k, hint in ((1, hints[:1]), (3, hints[1:])):
        dq, back[k] = grads_of(
            grads_kernel, "grads", (dq_type, contrib_type), k, h, *shared(k), own_grad, dq, *hint
        )

    def last(after):
        return grads_of(
            grads_kernel, "grads_last", (dq_type, contrib_type), 0, h, *shared(0), own_grad, dq, after
        )

    return dq, own_grad, back, last


def add_part(k, u, table, part, acc):
    at = BACK + 8 * u + 2 * k
    words = table[at : at + 2, :]
    for d in range(DEPTH):
        slot = (words[d // 4, 0] >> (5 * (d % 4))) & 31
        acc[jnp.maximum(slot - 1, 0)] += jnp.where(slot > 0, part[d].astype(F32), 0.0)


def combine_first_kernel(table, part_1, part_2, acc, token):
    acc[...] = jnp.zeros_like(acc)
    add_part(1, 0, table, part_1, acc)
    add_part(2, 0, table, part_2, acc)
    token[...] = jnp.zeros_like(token)


def combine_kernel(ks, u, table, *refs):
    acc = refs[len(ks) + 2]
    for token in refs[len(ks) + 3 :]:
        token[...] = jnp.zeros_like(token)
    for k, part in zip(ks, refs):
        add_part(k, u, table, part, acc)


def leave_kernel(acc, halves):
    for z in range(NZ):
        at = 2 * (z % 2) + z // 4
        rows = slice(8 * (z // 2 % 2), 8 * (z // 2 % 2) + 8)
        halves[z] = acc[:, at, rows, :].reshape(HALF, 16, LANES).astype(BF16)


ACC = (2 * HALF, QUAD, 16, LANES)


def acc_and_token():
    return jax.ShapeDtypeStruct(ACC, F32), jax.ShapeDtypeStruct((8, LANES), F32)


def combine_start(table, part_1, part_2):
    return pl.pallas_call(
        combine_first_kernel,
        in_specs=[in_vmem()] * 3,
        out_specs=(in_vmem(),) * 2,
        **call(combine_first_kernel, acc_and_token(), vmem_mb=16),
        cost_estimate=SMALL,
        name="combine_first",
    )(table, part_1, part_2)


def combine_more(ks, u, table, parts, acc, after, outs=1):
    return pl.pallas_call(
        functools.partial(combine_kernel, ks, u),
        in_specs=[in_vmem()] * (2 + len(parts)) + [pl.BlockSpec(memory_space=pl.ANY)],
        out_specs=(in_vmem(),) * outs,
        input_output_aliases={1 + len(parts): 0},
        **call(combine_kernel, acc_and_token()[:outs], vmem_mb=16),
        cost_estimate=SMALL,
        name="combine",
    )(table, *parts, acc, after)


def leave(acc):
    return pl.pallas_call(
        leave_kernel,
        in_specs=[in_vmem()],
        out_specs=in_vmem(),
        **call(leave_kernel, jax.ShapeDtypeStruct((NZ, HALF, 16, LANES), BF16), vmem_mb=16),
        cost_estimate=SMALL,
        name="leave",
    )(acc)


def split_rows(value, rows):
    high = value.astype(BF16).astype(F32)
    middle = (value - high).astype(BF16).astype(F32)
    low = value - high - middle
    row = lax.broadcasted_iota(jnp.int32, (8, LANES), 0)
    tile = jnp.where(row == 0, high, jnp.where(row == 1, middle, jnp.where(row == 2, low, 0.0)))
    if rows > 8:
        tile = jnp.concatenate([tile, jnp.zeros((rows - 8, LANES), F32)], 0)
    return tile


def total_kernel(parts, squares, totals, sums):
    sums_now = parts[0].astype(F32)
    for z in range(1, NZ):
        sums_now = sums_now + parts[z].astype(F32)
    totals[...] = sums_now
    tile = squares[...] + jnp.sum((sums_now * sums_now).reshape(HALF * 2, 8, LANES), axis=0)
    sums[...] = jnp.broadcast_to(jnp.sum(tile, axis=0, keepdims=True), (8, LANES))


def route_kernel(table, parts, squares, out, room, totals, sums):
    total_kernel(parts, squares, totals, sums)
    c = place()[2]
    words = table[HOLD : HOLD + 8, :]
    room[...] = jnp.zeros_like(room)
    for s in range(2 * HALF):
        block = ((words[s // 3, 0] >> (7 * (s % 3))) & 127) - 1
        side = jnp.where((block & 1) == c, 0, 1)
        to = jnp.where(block >= 0, (block >> 1) * 2 + side, NBLK)
        room[to] = totals[s // 2, 8 * (s % 2) : 8 * (s % 2) + 8, :]
    tails = jnp.broadcast_to(split_rows(sums[...], 8)[None], (NY * NZ, 8, LANES))
    rows = room[0:NBLK].reshape(NY * NZ, 16, LANES)
    out[...] = jnp.concatenate([rows, tails], 1).astype(BF16)


def route(table, parts, squares):
    return pl.pallas_call(
        route_kernel,
        in_specs=[in_vmem()] * 3,
        out_specs=in_vmem(),
        **call(
            route_kernel,
            jax.ShapeDtypeStruct((NY * NZ, 24, LANES), BF16),
            [
                VMEM((NBLK + 1, 8, LANES), F32),
                VMEM((HALF, 16, LANES), F32),
                VMEM((8, LANES), F32),
            ],
        ),
        name="route",
    )(table, parts, squares)


def share_kernel(arrived, send, sums):
    whole = arrived[...].astype(F32)
    for i in range(NY * NZ // 2):
        pair = [whole[2 * i + j, 8:16, :] for j in range(2)]
        send[i] = jnp.concatenate(pair, 0).astype(BF16)
    tails = jnp.sum(jnp.sum(whole[:, 16:24, :], axis=0), axis=0, keepdims=True)
    value = jnp.broadcast_to(tails, (8, LANES))
    sums[...] = value
    send[NY * NZ // 2] = split_rows(value, 16).astype(BF16)


def share(arrived):
    return pl.pallas_call(
        share_kernel,
        in_specs=[in_vmem()],
        out_specs=(in_vmem(),) * 2,
        **call(
            share_kernel,
            (
                jax.ShapeDtypeStruct((NY * NZ // 2 + 1, 16, LANES), BF16),
                jax.ShapeDtypeStruct((8, LANES), F32),
            ),
        ),
        name="share",
    )(arrived)


def tally_kernel(mine, got, sums):
    tails = mine[0:1, :] + jnp.sum(got[NY * NZ // 2].astype(F32), axis=0, keepdims=True)
    sums[...] = jnp.broadcast_to(jnp.sum(tails, axis=1, keepdims=True), (1, LANES))


def tally(mine, got):
    return pl.pallas_call(
        tally_kernel,
        in_specs=[in_vmem()] * 2,
        out_specs=in_vmem(),
        **call(tally_kernel, jax.ShapeDtypeStruct((1, LANES), F32)),
        name="tally",
    )(mine, got)


def finish_kernel(table, arrived, got, own, own_far, key_grad, value_grad, token):
    token[...] = jnp.zeros_like(token)
    first_core = place()[2] == 0
    inner = table[INNER : INNER + 1, :] > 0
    for z in range(NZ):
        kind = z % 2
        out = value_grad if kind else key_grad
        for y in range(NY):
            at, src = row_of(y, z), y * NZ + z
            near = arrived[src].astype(F32)[0:8]
            far = got[src // 2].astype(F32)[8 * (src % 2) : 8 * (src % 2) + 8]
            near = jnp.where(inner, near, own[kind, at : at + 8, :])
            low = ROWS + TOK * kind + at
            far = jnp.where(inner, far, own_far[low : low + 8, :])
            out[at : at + 8, 0, :] = jnp.where(first_core, near, far)
            out[at : at + 8, 1, :] = jnp.where(first_core, far, near)


def finish(*arrays):
    return pl.pallas_call(
        finish_kernel,
        in_specs=[in_vmem()] * 5,
        out_specs=(in_vmem(),) * 3,
        **call(
            finish_kernel,
            (jax.ShapeDtypeStruct((TOK, KV, HD), F32),) * 2
            + (jax.ShapeDtypeStruct((1, LANES), F32),),
        ),
        cost_estimate=SMALL,
        name="finish",
    )(*arrays)


def local(queries, keys, values, cotangent, rewards, groups, ancestors, step_ids):
    packet, own_kv = packet_of(keys, values, ancestors, groups, rewards)
    mine = swap_yz(packet)
    other = other_core(mine)
    trained = (step_ids[0] % 2 == 0)[:, None, None]
    masked = jnp.where(trained, cotangent, jnp.zeros_like(cotangent))
    picked, table, scale = plan(mine, other)
    column = swap_z(picked)
    first = deal(0, table, column, table)
    keep, send = halve(queries, masked, own_kv, table)
    q_all, g_all, kv_all = prepare(scale, keep, other_core(send))
    parts = []
    for u in range(2):
        dealt = first if u == 0 else deal(u, table, column, first[0])
        parts.append([dealt[0]] + [along_y(dealt[k], k) for k in (1, 2, 3)])
    after, own_0, sent, last_0 = attend(0, table, q_all, g_all, kv_all, parts[0], None, ())
    back_0 = [None] + [along_y(sent[k], -k) for k in (1, 2, 3)]
    acc, token = combine_start(table, back_0[1], back_0[2])
    acc, late_token = combine_more((3,), 0, table, [back_0[3]], acc, table, 2)
    after, own_1, sent, last_1 = attend(
        1, table, q_all, g_all, kv_all, parts[1], after, (token, late_token)
    )
    back_1 = [None] + [along_y(sent[k], -k) for k in (1, 2, 3)]
    dq_0, back_0[0] = last_0(after)
    dq_1, back_1[0] = last_1(dq_0)
    near, far, squares = emit(table, (dq_0, dq_1), (own_0, own_1))
    (acc,) = combine_more((0,), 0, table, [back_0[0]], acc, squares)
    (acc,) = combine_more((1, 0), 1, table, [back_1[1], back_1[0]], acc, squares)
    (acc,) = combine_more((2,), 1, table, [back_1[2]], acc, squares)
    (acc,) = combine_more((3,), 1, table, [back_1[3]], acc, squares)
    halves = leave(acc)
    arrived = swap_yz(route(table, swap_z(halves), squares))
    shared, mine_sum = share(arrived)
    shared = other_core(shared)
    mine_sum = tally(mine_sum, shared)
    far = other_core(ship(far, mine_sum))
    query_grad, done = assemble(near, far)
    key_grad, value_grad, token = finish(table, arrived, shared, own_0, far)
    all_sum = mine_sum + (done + token)
    for k in (1, 2, 3):
        all_sum = all_sum + along_head(mine_sum, k)
    count = float(NBLK * TOK * NHEAD * (KV * RATIO + 2 * KV) * HD)
    grad_rms = jnp.sqrt(all_sum[0, 0] / count)
    return query_grad, key_grad, value_grad, grad_rms


def solution(mesh):
    in_specs = (
        P("branch", "head", None),
        P("branch", "head", None),
        P("branch", "head", None),
        P("branch", "head", None),
        P("branch"),
        P("branch"),
        P("branch", None),
        P("branch", None),
    )
    out_specs = (
        P("branch", "head", None),
        P("branch", "head", None),
        P("branch", "head", None),
        P(),
    )
    return jax.shard_map(local, mesh=mesh, in_specs=in_specs, out_specs=out_specs, check_vma=False)
```

```python
import functools
import math

import jax
import jax.numpy as jnp
from jax import lax
from jax.experimental import pallas as pl
from jax.experimental.pallas import tpu as pltpu
from jax.sharding import PartitionSpec as P

NY, NZ, NC = 4, 8, 2
NBLK = NY * NZ * NC
NHEAD = 4
GROUP = 4
DEPTH = 8
TOK = 128
HD = 128
KV = 2
RATIO = 8
LANES = 128
HALF = 8
ROWS = TOK * RATIO
QUAD = 4
PART = 32 * DEPTH
HAND = (DEPTH, QUAD, 16, LANES)
F32 = jnp.float32
BF16 = jnp.bfloat16
VMEM = pltpu.VMEM
NT = (((1,), (1,)), ((), ()))
NN = (((1,), (0,)), ((), ()))
TN = (((0,), (0,)), ((), ()))


def index_of(y, z, c):
    return ((y % NY) * NZ + z % NZ) * NC + c % NC


def every():
    return [(y, z, c) for y in range(NY) for z in range(NZ) for c in range(NC)]


def along_y(x, step):
    pairs = [(index_of(y, z, c), index_of(y + step, z, c)) for y, z, c in every()]
    return lax.ppermute(x, "branch", pairs)


def other_core(x):
    pairs = [(index_of(y, z, c), index_of(y, z, c + 1)) for y, z, c in every()]
    return lax.ppermute(x, "branch", pairs)


def along_head(x, step):
    pairs = [(i, (i + step) % NHEAD) for i in range(NHEAD)]
    return lax.ppermute(x, "head", pairs)


def swap_z(x):
    groups = [[index_of(y, z, c) for z in range(NZ)] for y in range(NY) for c in range(NC)]
    return lax.all_to_all(x, "branch", 0, 0, axis_index_groups=groups, tiled=False)


def swap_yz(x):
    groups = [[index_of(y, z, c) for y in range(NY) for z in range(NZ)] for c in range(NC)]
    return lax.all_to_all(x, "branch", 0, 0, axis_index_groups=groups, tiled=False)


def call(body, outs, scratch=(), vmem_mb=32):
    return dict(
        out_shape=outs,
        scratch_shapes=list(scratch),
        compiler_params=pltpu.CompilerParams(vmem_limit_bytes=vmem_mb << 20),
    )


def in_vmem():
    return pl.BlockSpec(memory_space=VMEM)


def place():
    b = lax.axis_index("branch")
    return b // (NZ * NC), (b // NC) % NZ, b % NC


LINE = 0
DEAL = 16
BACK = 32
HOLD = 48
INNER = 56
SELF = 72
WORDS = 88


def row_of(y, z):
    return 32 * y + 8 * (z // 2)


def packet_kernel(
    keys_far, values_far, ancestors_far, group, reward, packet, own_kv,
    keys, values, ancestors, sems,
):
    pairs = (
        (ancestors_far, ancestors),
        (keys_far, keys),
        (values_far, values),
    )
    copies = [pltpu.make_async_copy(a, b, sems.at[i]) for i, (a, b) in enumerate(pairs)]
    for copy in copies:
        copy.start()
    for copy in copies[:1]:
        copy.wait()
    row = lax.broadcasted_iota(jnp.int32, (8, LANES), 0)
    lane = lax.broadcasted_iota(jnp.int32, (8, LANES), 1)
    spot = lax.broadcasted_iota(jnp.int32, (8, DEPTH), 0) == lax.broadcasted_iota(
        jnp.int32, (8, DEPTH), 1
    )
    line = jnp.broadcast_to(ancestors[...].astype(F32), (8, DEPTH))
    line = jnp.sum(jnp.where(spot, line, 0.0), axis=1, keepdims=True)
    facts = jnp.where(
        row == 0, group[0].astype(F32), jnp.where(row == 1, reward[0].astype(F32), 0.0)
    )
    meta = jnp.where(lane < NBLK, line, facts)
    for copy in copies[1:]:
        copy.wait()
    for h in range(KV):
        own_kv[2 * h] = keys[:, h, :]
        own_kv[2 * h + 1] = values[:, h, :]
    whole = [own_kv[i].astype(F32) for i in range(2 * KV)]
    for z in range(NZ):
        for y in range(NY):
            at = row_of(y, z)
            rows = [whole[2 * h + z % 2][at : at + 8] for h in range(KV)]
            packet[y * NZ + z] = jnp.concatenate(rows + [meta], 0).astype(BF16)


def packet_of(keys, values, ancestors, group, reward):
    return pl.pallas_call(
        packet_kernel,
        in_specs=[pl.BlockSpec(memory_space=pltpu.HBM)] * 3
        + [pl.BlockSpec(memory_space=pltpu.SMEM)] * 2,
        out_specs=(in_vmem(),) * 2,
        **call(
            packet_kernel,
            (
                jax.ShapeDtypeStruct((NY * NZ, 24, LANES), BF16),
                jax.ShapeDtypeStruct((2 * KV, TOK, HD), BF16),
            ),
            [VMEM(x.shape, x.dtype) for x in (keys, values, ancestors)]
            + [pltpu.SemaphoreType.DMA((3,))],
            vmem_mb=62,
        ),
        name="packet",
    )(keys, values, ancestors, group, reward)


def pack_rows(x, base, first, count):
    row = lax.broadcasted_iota(jnp.int32, (8, LANES), 0)
    weight = jnp.zeros((8, LANES), F32)
    for i in range(count):
        weight = jnp.where(row == first + i, float(base**i), weight)
    return jnp.sum(x * weight, axis=0, keepdims=True)


def plan_kernel(mine, other, picked, table, scale):
    y, z, c = place()
    meta_m = mine[...].astype(F32)[:, 16:24, :]
    meta_o = other[...].astype(F32)[:, 16:24, :]
    row = lax.broadcasted_iota(jnp.int32, (8, LANES), 0)
    row_f = row.astype(F32)
    lane = lax.broadcasted_iota(jnp.int32, (8, LANES), 1)
    lane_f = lane.astype(F32)
    is_block = lane < NBLK
    wide_lane = lax.broadcasted_iota(jnp.int32, (NY * NZ, LANES), 1).astype(F32)
    hit = jnp.maximum(
        jnp.where(meta_m[:, 0, :] == wide_lane, 1.0, 0.0),
        jnp.where(meta_o[:, 0, :] == wide_lane, 1.0, 0.0),
    )
    inner = jnp.max(hit, axis=0, keepdims=True)
    inner = jnp.where(is_block, jnp.broadcast_to(inner, (8, LANES)), 0.0)
    before = (
        lax.broadcasted_iota(jnp.int32, (LANES, LANES), 0)
        < lax.broadcasted_iota(jnp.int32, (LANES, LANES), 1)
    ).astype(F32).astype(BF16)
    rank = lax.dot_general(inner.astype(BF16), before, NN, preferred_element_type=F32)
    slots = jnp.where(inner > 0.0, rank + 1.0, 0.0)

    words = []
    for first in (0, 8):
        wanted = row_f + float(first + 1)
        index = jnp.sum(jnp.where(slots == wanted, lane_f, 0.0), axis=1, keepdims=True)
        index = jnp.broadcast_to(index, (8, LANES))
        words += [pack_rows(index, 64, at, 4).astype(jnp.int32)[0, 0] for at in (0, 4)]
    pieces = []
    for s in range(2 * HALF):
        block = (words[s // 4] >> (6 * (s % 4))) & 63
        at = block >> 1
        piece = jnp.where((block & 1) == c, mine[at].astype(F32), other[at].astype(F32))
        pieces.append(jnp.where(c == 0, piece[0:8], piece[8:16]))
    for j in range(HALF):
        pair = jnp.concatenate(pieces[2 * j : 2 * j + 2], 0).astype(BF16)
        picked[:, j] = jnp.broadcast_to(pair[None], (NZ, 16, LANES))

    for k in range(NY):
        yy = lax.rem(y + k, NY)
        for u, side in enumerate((mine, other)):
            line = side[yy * NZ + z].astype(F32)[16:24, :]
            same = (line == lane_f) & is_block
            slot = jnp.sum(jnp.where(same, slots, 0.0), axis=1, keepdims=True)
            slot = jnp.broadcast_to(slot, (8, LANES))
            block = (yy * NZ + z) * NC + (c if u == 0 else 1 - c)
            own = jnp.sum(jnp.where(lane == block, slots, 0.0), axis=1, keepdims=True)
            own = jnp.broadcast_to(own, (8, LANES))
            depth = jnp.sum(jnp.where(slot > 0.0, 1.0, 0.0), axis=0, keepdims=True)
            entry = jnp.where(row_f == depth, own, slot)
            dealt = jnp.maximum(slot - 1.0, 0.0)
            for half in range(2):
                at = 8 * u + 2 * k + half
                word = pack_rows(dealt, 16, 4 * half, 4)
                table[DEAL + at : DEAL + at + 1, :] = word.astype(jnp.int32)
                word = pack_rows(entry, 32, 4 * half, 4)
                table[BACK + at : BACK + at + 1, :] = word.astype(jnp.int32)
            if k == 0:
                at = 8 * u
                table[LINE + at : LINE + at + 8, :] = slot.astype(jnp.int32)
                table[INNER + at : INNER + at + 8, :] = own.astype(jnp.int32)
                mark = jnp.where(row_f == depth, own, 0.0)
                table[SELF + at : SELF + at + 8, :] = mark.astype(jnp.int32)
    for i in range(6):
        word = jnp.zeros((8, 1), F32)
        for j in range(3):
            held = jnp.where(slots == float(3 * i + j + 1), lane_f + 1.0, 0.0)
            word = word + jnp.sum(held, axis=1, keepdims=True) * float(128**j)
        table[HOLD + i : HOLD + i + 1, :] = jnp.broadcast_to(word, (8, LANES)).astype(jnp.int32)[0:1]

    for u, side in enumerate((mine, other)):
        here = side[y * NZ + z].astype(F32)[16:24, :]
        group, reward = here[0:1, :], here[1:2, :]
        in_m = jnp.where(meta_m[:, 0, :] == group, meta_m[:, 1, :], 0.0)
        in_o = jnp.where(meta_o[:, 0, :] == group, meta_o[:, 1, :], 0.0)
        total = jnp.sum(in_m + in_o, axis=0, keepdims=True)
        squares = jnp.sum(in_m * in_m + in_o * in_o, axis=0, keepdims=True)
        mean = total / GROUP
        spread = jnp.sqrt(jnp.maximum(squares / GROUP - mean * mean, 0.25))
        advantage = (reward - mean) / spread
        advantage = jnp.sum(jnp.where(lane[0:1] == NBLK, advantage, 0.0), axis=1, keepdims=True)
        scale[8 * u : 8 * u + 8] = jnp.broadcast_to(advantage, (8, LANES))


def plan(mine, other):
    return pl.pallas_call(
        plan_kernel,
        in_specs=[in_vmem()] * 2,
        out_specs=(in_vmem(),) * 3,
        **call(
            plan_kernel,
            (
                jax.ShapeDtypeStruct((NZ, HALF, 16, LANES), BF16),
                jax.ShapeDtypeStruct((WORDS, LANES), jnp.int32),
                jax.ShapeDtypeStruct((16, LANES), F32),
            ),
        ),
        name="plan",
    )(mine, other)


def deal_kernel(u, table, column, after, *outs):
    words = table[DEAL + 8 * u : DEAL + 8 * u + 8, :]
    for k in range(NY):
        for d in range(DEPTH):
            slot = (words[2 * k + d // 4, 0] >> (4 * (d % 4))) & 15
            pair = column[:, slot >> 1].astype(F32)
            rows = jnp.where((slot & 1) == 1, pair[:, 8:16], pair[:, 0:8])
            for kind in range(2):
                whole = jnp.concatenate([rows[2 * i + kind] for i in range(4)], 0)
                outs[k][d, 2 * kind : 2 * kind + 2] = whole.astype(BF16).reshape(2, 16, LANES)


def deal(u, table, column, after):
    return pl.pallas_call(
        functools.partial(deal_kernel, u),
        in_specs=[in_vmem()] * 2 + [pl.BlockSpec(memory_space=pl.ANY)],
        out_specs=(in_vmem(),) * NY,
        **call(deal_kernel, (jax.ShapeDtypeStruct(HAND, BF16),) * NY),
        name="deal",
    )(table, column, after)


def halve_kernel(queries, cotangent, own_kv, after, keep, send):
    first_core = place()[2] == 0
    for at, far in ((0, queries), (ROWS, cotangent)):
        whole = far[...].astype(F32)
        low = whole[:, 0:RATIO].reshape(ROWS, HD).astype(BF16)
        high = whole[:, RATIO:].reshape(ROWS, HD).astype(BF16)
        keep[at : at + ROWS] = jnp.where(first_core, low, high)
        send[at : at + ROWS] = jnp.where(first_core, high, low)
    for kind in range(2):
        at = 2 * ROWS + TOK * kind
        low, high = own_kv[kind], own_kv[2 + kind]
        keep[at : at + TOK] = jnp.where(first_core, low, high)
        send[at : at + TOK] = jnp.where(first_core, high, low)


def halve(queries, cotangent, own_kv, after):
    return pl.pallas_call(
        halve_kernel,
        in_specs=[in_vmem()] * 3 + [pl.BlockSpec(memory_space=pl.ANY)],
        out_specs=(in_vmem(),) * 2,
        **call(halve_kernel, (jax.ShapeDtypeStruct((2 * ROWS + 2 * TOK, HD), BF16),) * 2),
        name="halve",
    )(queries, cotangent, own_kv, after)


def prepare_kernel(scale, keep, got, q_all, g_all, kv_all):
    for u, side in enumerate((keep, got)):
        q_all[u] = side[0:ROWS]
        weight = scale[8 * u : 8 * u + 1, :]
        g_all[u] = (side[ROWS : 2 * ROWS].astype(F32) * weight).astype(BF16)
        for kind in range(2):
            at = 2 * ROWS + TOK * kind
            kv_all[2 * u + kind] = side[at : at + TOK]


def prepare(scale, keep, got):
    return pl.pallas_call(
        prepare_kernel,
        in_specs=[in_vmem()] * 3,
        out_specs=(in_vmem(),) * 3,
        **call(
            prepare_kernel,
            (jax.ShapeDtypeStruct((2, ROWS, HD), BF16),) * 2
            + (jax.ShapeDtypeStruct((4, TOK, HD), BF16),),
        ),
        name="prepare",
    )(scale, keep, got)


def rows_of(part, kind):
    return part[:, 2 * kind : 2 * kind + 2].reshape(PART, HD)


def one_part(keys, values, q, g, mask, exps, pgs, stats, at):
    s = lax.dot_general(keys, q, NT, preferred_element_type=F32) * (
        math.log2(math.e) / math.sqrt(HD)
    )
    s = mask(s)
    top = jnp.max(s, axis=0, keepdims=True)
    e = jnp.exp2(s - top)
    pg = lax.dot_general(values, g, NT, preferred_element_type=F32)
    exps[...] = e
    pgs[...] = pg
    stats[at : at + 1, :] = top
    stats[at + 1 : at + 2, :] = jnp.sum(e, axis=0, keepdims=True)
    stats[at + 2 : at + 3, :] = jnp.sum(e * pg, axis=0, keepdims=True)


def causal(s):
    key_pos = lax.broadcasted_iota(jnp.int32, s.shape, 0)
    query_pos = lax.broadcasted_iota(jnp.int32, s.shape, 1) // RATIO
    return jnp.where(key_pos <= query_pos, s, -1e30)


def listed(h, table):
    def mask(s):
        parts = []
        for d in range(DEPTH):
            seen = jnp.concatenate([table[LINE + 8 * h + d : LINE + 8 * h + d + 1, :]] * (ROWS // LANES), 1) > 0
            parts.append(jnp.where(seen, s[32 * d : 32 * d + 32], -1e30))
        return jnp.concatenate(parts, 0)

    return mask


def scores_kernel(h, table, q_all, g_all, part, after, exps, pgs, stats):
    keys, values = rows_of(part, 0), rows_of(part, 1)
    one_part(keys, values, q_all[h], g_all[h], listed(h, table), exps, pgs, stats, 0)


def first_scores_kernel(h, table, q_all, g_all, part, own_kv, exps, pgs, stats, own_exps, own_pgs):
    keys, values = rows_of(part, 0), rows_of(part, 1)
    q, g = q_all[h], g_all[h]
    one_part(keys, values, q, g, listed(h, table), exps, pgs, stats, 0)
    one_part(own_kv[2 * h], own_kv[2 * h + 1], q, g, causal, own_exps, own_pgs, stats, 4)


def wide(keys):
    return jax.ShapeDtypeStruct((keys, ROWS), F32)


STATS = jax.ShapeDtypeStruct((8, TOK * RATIO), F32)


def scores_of(h, table, q_all, g_all, part, after):
    return pl.pallas_call(
        functools.partial(scores_kernel, h),
        in_specs=[in_vmem()] * 4 + [pl.BlockSpec(memory_space=pl.ANY)],
        out_specs=(in_vmem(),) * 3,
        **call(scores_kernel, (wide(PART), wide(PART), STATS), vmem_mb=16),
        cost_estimate=cost(PART, 2),
        name="scores",
    )(table, q_all, g_all, part, after)


def first_scores_of(h, table, q_all, g_all, part, own_kv):
    return pl.pallas_call(
        functools.partial(first_scores_kernel, h),
        in_specs=[in_vmem()] * 5,
        out_specs=(in_vmem(),) * 5,
        **call(
            first_scores_kernel,
            (wide(PART), wide(PART), STATS, wide(TOK), wide(TOK)),
            vmem_mb=16,
        ),
        cost_estimate=cost(PART + TOK, 2),
        name="scores_first",
    )(table, q_all, g_all, part, own_kv)


def cost(keys, products):
    return pl.CostEstimate(
        flops=2 * products * ROWS * keys * HD,
        bytes_accessed=8 * ROWS * keys,
        transcendentals=ROWS * keys,
    )


SMALL = pl.CostEstimate(flops=1000, bytes_accessed=1000, transcendentals=0)


def merge(stats):
    rows = [(ref, 0) for ref in stats] + [(stats[0], 4)]
    tops = [ref[at : at + 1, :] for ref, at in rows]
    top = tops[0]
    for t in tops[1:]:
        top = jnp.maximum(top, t)
    shares = [jnp.exp2(t - top) for t in tops]
    norm = sum(s * ref[at + 1 : at + 2, :] for s, (ref, at) in zip(shares, rows))
    norm = 1.0 / norm
    shares = [s * norm for s in shares]
    delta = sum(s * ref[at + 2 : at + 3, :] for s, (ref, at) in zip(shares, rows))
    return shares, delta


def one_grad(e, pg, share, delta, q, g, keys):
    p = e * share
    low = p.astype(BF16)
    ds = (p * (pg - delta)).astype(BF16)
    factor = 1.0 / math.sqrt(HD)
    dv = lax.dot_general(low, g, NN, preferred_element_type=F32)
    dk = lax.dot_general(ds, q, NN, preferred_element_type=F32) * factor
    turned = keys.astype(F32).T.astype(BF16)
    dq = lax.dot_general(turned, ds, NN, preferred_element_type=F32)
    return dq, dk, dv


def part_grad(k, h, table, stats, exps, pgs, q_all, g_all, part, own_grad, contrib):
    shares, delta = merge(stats)
    dq, dk, dv = one_grad(
        exps[...], pgs[...], shares[k], delta, q_all[h], g_all[h], rows_of(part, 0)
    )
    piece = lax.rem(place()[0] + NY - k, NY)
    for kind, grad in enumerate((dk, dv)):
        own = own_grad[kind, pl.ds(pl.multiple_of(piece * 32, 32), 32), :]
        for d in range(DEPTH):
            mark = table[SELF + 8 * h + d : SELF + 8 * h + d + 1, :] > 0
            both = jnp.where(mark, own, grad[32 * d : 32 * d + 32])
            contrib[d, 2 * kind : 2 * kind + 2] = both.astype(BF16).reshape(2, 16, HD)
    return dq


def first_grads_kernel(
    k, h, table, s0, s1, s2, s3, exps, pgs, q_all, g_all, part, own_exps, own_pgs, own_kv,
    dq_sum, own_grad, contrib,
):
    stats = (s0, s1, s2, s3)
    shares, delta = merge(stats)
    dq, dk, dv = one_grad(
        own_exps[...], own_pgs[...], shares[NY], delta, q_all[h], g_all[h], own_kv[2 * h]
    )
    own_grad[0] = dk
    own_grad[1] = dv
    dq_sum[...] = dq + part_grad(
        k, h, table, stats, exps, pgs, q_all, g_all, part, own_grad, contrib
    )


def grads_kernel(
    k, h, table, s0, s1, s2, s3, exps, pgs, q_all, g_all, part, own_grad, dq_in, *outs
):
    dq_sum, contrib = outs[-2:]
    dq_sum[...] = dq_in[...] + part_grad(
        k, h, table, (s0, s1, s2, s3), exps, pgs, q_all, g_all, part, own_grad, contrib
    )


def emit_kernel(table, dq_0, dq_1, own_0, own_1, keep, send, squares):
    total = jnp.zeros((8, HD), F32)
    for u, (dq, own, out) in enumerate(((dq_0, own_0, keep), (dq_1, own_1, send))):
        dq = dq[...].T * (1.0 / math.sqrt(HD))
        total = total + jnp.sum((dq * dq).reshape(ROWS // 8, 8, HD), axis=0)
        out[0:ROWS] = dq
        own = own[...]
        own_squares = jnp.sum((own * own).reshape(2 * TOK // 8, 8, HD), axis=0)
        inner = table[INNER + 8 * u : INNER + 8 * u + 8, :] > 0
        total = total + jnp.where(inner, 0.0, own_squares)
    send[ROWS : ROWS + TOK] = own_1[0]
    send[ROWS + TOK :] = own_1[1]
    squares[...] = total


def emit(table, dqs, owns):
    return pl.pallas_call(
        emit_kernel,
        in_specs=[in_vmem()] * 5,
        out_specs=(in_vmem(),) * 3,
        **call(
            emit_kernel,
            (
                jax.ShapeDtypeStruct((ROWS, HD), F32),
                jax.ShapeDtypeStruct((ROWS + 2 * TOK, HD), F32),
                jax.ShapeDtypeStruct((8, LANES), F32),
            ),
            vmem_mb=16,
        ),
        cost_estimate=SMALL,
        name="emit",
    )(table, *dqs, *owns)


def ship_kernel(far, after, out):
    pass


def ship(far, after):
    return pl.pallas_call(
        ship_kernel,
        in_specs=[in_vmem(), pl.BlockSpec(memory_space=pl.ANY)],
        out_specs=in_vmem(),
        input_output_aliases={0: 0},
        **call(ship_kernel, jax.ShapeDtypeStruct(far.shape, F32), vmem_mb=16),
        cost_estimate=SMALL,
        name="ship",
    )(far, after)


def assemble_kernel(keep, got, query_grad, token):
    first_core = place()[2] == 0
    near, far = keep[...], got[0:ROWS]
    low, high = jnp.where(first_core, near, far), jnp.where(first_core, far, near)
    query_grad[:, 0:RATIO, :] = low.reshape(TOK, RATIO, HD)
    query_grad[:, RATIO:, :] = high.reshape(TOK, RATIO, HD)
    token[...] = jnp.zeros_like(token)


def assemble(keep, got):
    return pl.pallas_call(
        assemble_kernel,
        in_specs=[in_vmem()] * 2,
        out_specs=(in_vmem(),) * 2,
        **call(
            assemble_kernel,
            (
                jax.ShapeDtypeStruct((TOK, KV * RATIO, HD), F32),
                jax.ShapeDtypeStruct((1, LANES), F32),
            ),
            vmem_mb=16,
        ),
        cost_estimate=SMALL,
        name="assemble",
    )(keep, got)


def grads_of(body, name, outs, k, h, *arrays):
    return pl.pallas_call(
        functools.partial(body, k, h),
        in_specs=[in_vmem()] * len(arrays),
        out_specs=(in_vmem(),) * len(outs),
        **call(body, outs, vmem_mb=16),
        cost_estimate=SMALL,
        name=name,
    )(*arrays)


def attend(h, table, q_all, g_all, own_kv, parts, first, after, hints):
    e, pg, st = [None] * NY, [None] * NY, [None] * NY
    e[0], pg[0], st[0], own_e, own_pg = first
    for k in (1, 2, 3):
        e[k], pg[k], st[k] = scores_of(h, table, q_all, g_all, parts[k], after)
        after = st[k]
    back = [None] * NY
    dq_type = jax.ShapeDtypeStruct((HD, ROWS), F32)
    own_type = jax.ShapeDtypeStruct((2, TOK, HD), F32)
    contrib_type = jax.ShapeDtypeStruct(HAND, BF16)

    def shared(k):
        return (table, *st, e[k], pg[k], q_all, g_all, parts[k])

    dq, own_grad, back[2] = grads_of(
        first_grads_kernel, "grads_first", (dq_type, own_type, contrib_type), 2, h,
        *shared(2), own_e, own_pg, own_kv,
    )
    for k, hint in ((1, hints[:1]), (3, hints[1:])):
        dq, back[k] = grads_of(
            grads_kernel, "grads", (dq_type, contrib_type), k, h, *shared(k), own_grad, dq, *hint
        )

    def last(after):
        return grads_of(
            grads_kernel, "grads_last", (dq_type, contrib_type), 0, h, *shared(0), own_grad, dq, after
        )

    return dq, own_grad, back, last


def add_part(k, u, table, part, acc):
    at = BACK + 8 * u + 2 * k
    words = table[at : at + 2, :]
    for d in range(DEPTH):
        slot = (words[d // 4, 0] >> (5 * (d % 4))) & 31
        acc[jnp.maximum(slot - 1, 0)] += jnp.where(slot > 0, part[d].astype(F32), 0.0)


def combine_first_kernel(table, part_1, part_2, acc, token):
    acc[...] = jnp.zeros_like(acc)
    add_part(1, 0, table, part_1, acc)
    add_part(2, 0, table, part_2, acc)
    token[...] = jnp.zeros_like(token)


def combine_kernel(ks, u, table, *refs):
    acc = refs[len(ks) + 2]
    for token in refs[len(ks) + 3 :]:
        token[...] = jnp.zeros_like(token)
    for k, part in zip(ks, refs):
        add_part(k, u, table, part, acc)


def leave_kernel(acc, halves):
    for z in range(NZ):
        at = 2 * (z % 2) + z // 4
        rows = slice(8 * (z // 2 % 2), 8 * (z // 2 % 2) + 8)
        halves[z] = acc[:, at, rows, :].reshape(HALF, 16, LANES).astype(BF16)


ACC = (2 * HALF, QUAD, 16, LANES)


def acc_and_token():
    return jax.ShapeDtypeStruct(ACC, F32), jax.ShapeDtypeStruct((8, LANES), F32)


def combine_start(table, part_1, part_2):
    return pl.pallas_call(
        combine_first_kernel,
        in_specs=[in_vmem()] * 3,
        out_specs=(in_vmem(),) * 2,
        **call(combine_first_kernel, acc_and_token(), vmem_mb=16),
        cost_estimate=SMALL,
        name="combine_first",
    )(table, part_1, part_2)


def combine_more(ks, u, table, parts, acc, after, outs=1):
    return pl.pallas_call(
        functools.partial(combine_kernel, ks, u),
        in_specs=[in_vmem()] * (2 + len(parts)) + [pl.BlockSpec(memory_space=pl.ANY)],
        out_specs=(in_vmem(),) * outs,
        input_output_aliases={1 + len(parts): 0},
        **call(combine_kernel, acc_and_token()[:outs], vmem_mb=16),
        cost_estimate=SMALL,
        name="combine",
    )(table, *parts, acc, after)


def leave(acc):
    return pl.pallas_call(
        leave_kernel,
        in_specs=[in_vmem()],
        out_specs=in_vmem(),
        **call(leave_kernel, jax.ShapeDtypeStruct((NZ, HALF, 16, LANES), BF16), vmem_mb=16),
        cost_estimate=SMALL,
        name="leave",
    )(acc)


def split_rows(value, rows):
    high = value.astype(BF16).astype(F32)
    middle = (value - high).astype(BF16).astype(F32)
    low = value - high - middle
    row = lax.broadcasted_iota(jnp.int32, (8, LANES), 0)
    tile = jnp.where(row == 0, high, jnp.where(row == 1, middle, jnp.where(row == 2, low, 0.0)))
    if rows > 8:
        tile = jnp.concatenate([tile, jnp.zeros((rows - 8, LANES), F32)], 0)
    return tile


def total_kernel(parts, squares, totals, sums):
    sums_now = parts[0].astype(F32)
    for z in range(1, NZ):
        sums_now = sums_now + parts[z].astype(F32)
    totals[...] = sums_now
    tile = squares[...] + jnp.sum((sums_now * sums_now).reshape(HALF * 2, 8, LANES), axis=0)
    sums[...] = jnp.broadcast_to(jnp.sum(tile, axis=0, keepdims=True), (8, LANES))


def route_kernel(table, parts, squares, out, room, totals, sums):
    total_kernel(parts, squares, totals, sums)
    c = place()[2]
    words = table[HOLD : HOLD + 8, :]
    room[...] = jnp.zeros_like(room)
    for s in range(2 * HALF):
        block = ((words[s // 3, 0] >> (7 * (s % 3))) & 127) - 1
        side = jnp.where((block & 1) == c, 0, 1)
        to = jnp.where(block >= 0, (block >> 1) * 2 + side, NBLK)
        room[to] = totals[s // 2, 8 * (s % 2) : 8 * (s % 2) + 8, :]
    tails = jnp.broadcast_to(split_rows(sums[...], 8)[None], (NY * NZ, 8, LANES))
    rows = room[0:NBLK].reshape(NY * NZ, 16, LANES)
    out[...] = jnp.concatenate([rows, tails], 1).astype(BF16)


def route(table, parts, squares):
    return pl.pallas_call(
        route_kernel,
        in_specs=[in_vmem()] * 3,
        out_specs=in_vmem(),
        **call(
            route_kernel,
            jax.ShapeDtypeStruct((NY * NZ, 24, LANES), BF16),
            [
                VMEM((NBLK + 1, 8, LANES), F32),
                VMEM((HALF, 16, LANES), F32),
                VMEM((8, LANES), F32),
            ],
        ),
        name="route",
    )(table, parts, squares)


def share_kernel(arrived, send, sums):
    whole = arrived[...].astype(F32)
    for i in range(NY * NZ // 2):
        pair = [whole[2 * i + j, 8:16, :] for j in range(2)]
        send[i] = jnp.concatenate(pair, 0).astype(BF16)
    tails = jnp.sum(jnp.sum(whole[:, 16:24, :], axis=0), axis=0, keepdims=True)
    value = jnp.broadcast_to(tails, (8, LANES))
    sums[...] = value
    send[NY * NZ // 2] = split_rows(value, 16).astype(BF16)


def share(arrived):
    return pl.pallas_call(
        share_kernel,
        in_specs=[in_vmem()],
        out_specs=(in_vmem(),) * 2,
        **call(
            share_kernel,
            (
                jax.ShapeDtypeStruct((NY * NZ // 2 + 1, 16, LANES), BF16),
                jax.ShapeDtypeStruct((8, LANES), F32),
            ),
        ),
        name="share",
    )(arrived)


def tally_kernel(mine, got, sums):
    tails = mine[0:1, :] + jnp.sum(got[NY * NZ // 2].astype(F32), axis=0, keepdims=True)
    sums[...] = jnp.broadcast_to(jnp.sum(tails, axis=1, keepdims=True), (1, LANES))


def tally(mine, got):
    return pl.pallas_call(
        tally_kernel,
        in_specs=[in_vmem()] * 2,
        out_specs=in_vmem(),
        **call(tally_kernel, jax.ShapeDtypeStruct((1, LANES), F32)),
        name="tally",
    )(mine, got)


def finish_kernel(table, arrived, got, own, own_far, key_grad, value_grad, token):
    token[...] = jnp.zeros_like(token)
    first_core = place()[2] == 0
    inner = table[INNER : INNER + 1, :] > 0
    for z in range(NZ):
        kind = z % 2
        out = value_grad if kind else key_grad
        for y in range(NY):
            at, src = row_of(y, z), y * NZ + z
            near = arrived[src].astype(F32)[0:8]
            far = got[src // 2].astype(F32)[8 * (src % 2) : 8 * (src % 2) + 8]
            near = jnp.where(inner, near, own[kind, at : at + 8, :])
            low = ROWS + TOK * kind + at
            far = jnp.where(inner, far, own_far[low : low + 8, :])
            out[at : at + 8, 0, :] = jnp.where(first_core, near, far)
            out[at : at + 8, 1, :] = jnp.where(first_core, far, near)


def finish(*arrays):
    return pl.pallas_call(
        finish_kernel,
        in_specs=[in_vmem()] * 5,
        out_specs=(in_vmem(),) * 3,
        **call(
            finish_kernel,
            (jax.ShapeDtypeStruct((TOK, KV, HD), F32),) * 2
            + (jax.ShapeDtypeStruct((1, LANES), F32),),
        ),
        cost_estimate=SMALL,
        name="finish",
    )(*arrays)


def local(queries, keys, values, cotangent, rewards, groups, ancestors, step_ids):
    packet, own_kv = packet_of(keys, values, ancestors, groups, rewards)
    mine = swap_yz(packet)
    other = other_core(mine)
    trained = (step_ids[0] % 2 == 0)[:, None, None]
    masked = jnp.where(trained, cotangent, jnp.zeros_like(cotangent))
    picked, table, scale = plan(mine, other)
    column = swap_z(picked)
    first = deal(0, table, column, table)
    keep, send = halve(queries, masked, own_kv, table)
    q_all, g_all, kv_all = prepare(scale, keep, other_core(send))
    parts = []
    for u in range(2):
        dealt = first if u == 0 else deal(u, table, column, first[0])
        parts.append([dealt[0]] + [along_y(dealt[k], k) for k in (1, 2, 3)])
    firsts = [first_scores_of(u, table, q_all, g_all, parts[u][0], kv_all) for u in range(2)]
    after, own_0, sent, last_0 = attend(
        0, table, q_all, g_all, kv_all, parts[0], firsts[0], firsts[1][2], ()
    )
    back_0 = [None] + [along_y(sent[k], -k) for k in (1, 2, 3)]
    acc, token = combine_start(table, back_0[1], back_0[2])
    acc, late_token = combine_more((3,), 0, table, [back_0[3]], acc, table, 2)
    after, own_1, sent, last_1 = attend(
        1, table, q_all, g_all, kv_all, parts[1], firsts[1], after, (token, late_token)
    )
    back_1 = [None] + [along_y(sent[k], -k) for k in (1, 2, 3)]
    dq_0, back_0[0] = last_0(after)
    dq_1, back_1[0] = last_1(dq_0)
    near, far, squares = emit(table, (dq_0, dq_1), (own_0, own_1))
    (acc,) = combine_more((0,), 0, table, [back_0[0]], acc, squares)
    (acc,) = combine_more((1, 0), 1, table, [back_1[1], back_1[0]], acc, squares)
    (acc,) = combine_more((2,), 1, table, [back_1[2]], acc, squares)
    (acc,) = combine_more((3,), 1, table, [back_1[3]], acc, squares)
    halves = leave(acc)
    arrived = swap_yz(route(table, swap_z(halves), squares))
    shared, mine_sum = share(arrived)
    shared = other_core(shared)
    mine_sum = tally(mine_sum, shared)
    far = other_core(ship(far, mine_sum))
    query_grad, done = assemble(near, far)
    key_grad, value_grad, token = finish(table, arrived, shared, own_0, far)
    all_sum = mine_sum + (done + token)
    for k in (1, 2, 3):
        all_sum = all_sum + along_head(mine_sum, k)
    count = float(NBLK * TOK * NHEAD * (KV * RATIO + 2 * KV) * HD)
    grad_rms = jnp.sqrt(all_sum[0, 0] / count)
    return query_grad, key_grad, value_grad, grad_rms


def solution(mesh):
    in_specs = (
        P("branch", "head", None),
        P("branch", "head", None),
        P("branch", "head", None),
        P("branch", "head", None),
        P("branch"),
        P("branch"),
        P("branch", None),
        P("branch", None),
    )
    out_specs = (
        P("branch", "head", None),
        P("branch", "head", None),
        P("branch", "head", None),
        P(),
    )
    return jax.shard_map(local, mesh=mesh, in_specs=in_specs, out_specs=out_specs, check_vma=False)
```

```python
import functools
import math

import jax
import jax.numpy as jnp
from jax import lax
from jax.experimental import pallas as pl
from jax.experimental.pallas import tpu as pltpu
from jax.sharding import PartitionSpec as P

NY, NZ, NC = 4, 8, 2
NBLK = NY * NZ * NC
NHEAD = 4
GROUP = 4
DEPTH = 8
TOK = 128
HD = 128
KV = 2
RATIO = 8
LANES = 128
HALF = 8
ROWS = TOK * RATIO
QUAD = 4
PART = 32 * DEPTH
HAND = (DEPTH, QUAD, 16, LANES)
F32 = jnp.float32
BF16 = jnp.bfloat16
VMEM = pltpu.VMEM
NT = (((1,), (1,)), ((), ()))
NN = (((1,), (0,)), ((), ()))
TN = (((0,), (0,)), ((), ()))


def index_of(y, z, c):
    return ((y % NY) * NZ + z % NZ) * NC + c % NC


def every():
    return [(y, z, c) for y in range(NY) for z in range(NZ) for c in range(NC)]


def along_y(x, step):
    pairs = [(index_of(y, z, c), index_of(y + step, z, c)) for y, z, c in every()]
    return lax.ppermute(x, "branch", pairs)


def other_core(x):
    pairs = [(index_of(y, z, c), index_of(y, z, c + 1)) for y, z, c in every()]
    return lax.ppermute(x, "branch", pairs)


def along_head(x, step):
    pairs = [(i, (i + step) % NHEAD) for i in range(NHEAD)]
    return lax.ppermute(x, "head", pairs)


def swap_z(x):
    groups = [[index_of(y, z, c) for z in range(NZ)] for y in range(NY) for c in range(NC)]
    return lax.all_to_all(x, "branch", 0, 0, axis_index_groups=groups, tiled=False)


def swap_yz(x):
    groups = [[index_of(y, z, c) for y in range(NY) for z in range(NZ)] for c in range(NC)]
    return lax.all_to_all(x, "branch", 0, 0, axis_index_groups=groups, tiled=False)


def call(body, outs, scratch=(), vmem_mb=32):
    return dict(
        out_shape=outs,
        scratch_shapes=list(scratch),
        compiler_params=pltpu.CompilerParams(vmem_limit_bytes=vmem_mb << 20),
    )


def in_vmem():
    return pl.BlockSpec(memory_space=VMEM)


def place():
    b = lax.axis_index("branch")
    return b // (NZ * NC), (b // NC) % NZ, b % NC


LINE = 0
DEAL = 16
BACK = 32
HOLD = 48
INNER = 56
SELF = 72
WORDS = 88


def row_of(y, z):
    return 32 * y + 8 * (z // 2)


def packet_kernel(
    keys_far, values_far, ancestors_far, group, reward, packet, own_kv,
    keys, values, ancestors, sems,
):
    pairs = (
        (ancestors_far, ancestors),
        (keys_far, keys),
        (values_far, values),
    )
    copies = [pltpu.make_async_copy(a, b, sems.at[i]) for i, (a, b) in enumerate(pairs)]
    for copy in copies:
        copy.start()
    for copy in copies[:1]:
        copy.wait()
    row = lax.broadcasted_iota(jnp.int32, (8, LANES), 0)
    lane = lax.broadcasted_iota(jnp.int32, (8, LANES), 1)
    spot = lax.broadcasted_iota(jnp.int32, (8, DEPTH), 0) == lax.broadcasted_iota(
        jnp.int32, (8, DEPTH), 1
    )
    line = jnp.broadcast_to(ancestors[...].astype(F32), (8, DEPTH))
    line = jnp.sum(jnp.where(spot, line, 0.0), axis=1, keepdims=True)
    facts = jnp.where(
        row == 0, group[0].astype(F32), jnp.where(row == 1, reward[0].astype(F32), 0.0)
    )
    meta = jnp.where(lane < NBLK, line, facts)
    for copy in copies[1:]:
        copy.wait()
    for h in range(KV):
        own_kv[2 * h] = keys[:, h, :]
        own_kv[2 * h + 1] = values[:, h, :]
    whole = [own_kv[i].astype(F32) for i in range(2 * KV)]
    for z in range(NZ):
        for y in range(NY):
            at = row_of(y, z)
            rows = [whole[2 * h + z % 2][at : at + 8] for h in range(KV)]
            packet[y * NZ + z] = jnp.concatenate(rows + [meta], 0).astype(BF16)


def packet_of(keys, values, ancestors, group, reward):
    return pl.pallas_call(
        packet_kernel,
        in_specs=[pl.BlockSpec(memory_space=pltpu.HBM)] * 3
        + [pl.BlockSpec(memory_space=pltpu.SMEM)] * 2,
        out_specs=(in_vmem(),) * 2,
        **call(
            packet_kernel,
            (
                jax.ShapeDtypeStruct((NY * NZ, 24, LANES), BF16),
                jax.ShapeDtypeStruct((2 * KV, TOK, HD), BF16),
            ),
            [VMEM(x.shape, x.dtype) for x in (keys, values, ancestors)]
            + [pltpu.SemaphoreType.DMA((3,))],
            vmem_mb=62,
        ),
        name="packet",
    )(keys, values, ancestors, group, reward)


def pack_rows(x, base, first, count):
    row = lax.broadcasted_iota(jnp.int32, (8, LANES), 0)
    weight = jnp.zeros((8, LANES), F32)
    for i in range(count):
        weight = jnp.where(row == first + i, float(base**i), weight)
    return jnp.sum(x * weight, axis=0, keepdims=True)


def plan_kernel(mine, other, picked, table, scale):
    y, z, c = place()
    meta_m = mine[...].astype(F32)[:, 16:24, :]
    meta_o = other[...].astype(F32)[:, 16:24, :]
    row = lax.broadcasted_iota(jnp.int32, (8, LANES), 0)
    row_f = row.astype(F32)
    lane = lax.broadcasted_iota(jnp.int32, (8, LANES), 1)
    lane_f = lane.astype(F32)
    is_block = lane < NBLK
    wide_lane = lax.broadcasted_iota(jnp.int32, (NY * NZ, LANES), 1).astype(F32)
    hit = jnp.maximum(
        jnp.where(meta_m[:, 0, :] == wide_lane, 1.0, 0.0),
        jnp.where(meta_o[:, 0, :] == wide_lane, 1.0, 0.0),
    )
    inner = jnp.max(hit, axis=0, keepdims=True)
    inner = jnp.where(is_block, jnp.broadcast_to(inner, (8, LANES)), 0.0)
    before = (
        lax.broadcasted_iota(jnp.int32, (LANES, LANES), 0)
        < lax.broadcasted_iota(jnp.int32, (LANES, LANES), 1)
    ).astype(F32).astype(BF16)
    rank = lax.dot_general(inner.astype(BF16), before, NN, preferred_element_type=F32)
    slots = jnp.where(inner > 0.0, rank + 1.0, 0.0)

    words = []
    for first in (0, 8):
        wanted = row_f + float(first + 1)
        index = jnp.sum(jnp.where(slots == wanted, lane_f, 0.0), axis=1, keepdims=True)
        index = jnp.broadcast_to(index, (8, LANES))
        words += [pack_rows(index, 64, at, 4).astype(jnp.int32)[0, 0] for at in (0, 4)]
    pieces = []
    for s in range(2 * HALF):
        block = (words[s // 4] >> (6 * (s % 4))) & 63
        at = block >> 1
        piece = jnp.where((block & 1) == c, mine[at].astype(F32), other[at].astype(F32))
        pieces.append(jnp.where(c == 0, piece[0:8], piece[8:16]))
    for j in range(HALF):
        pair = jnp.concatenate(pieces[2 * j : 2 * j + 2], 0).astype(BF16)
        picked[:, j] = jnp.broadcast_to(pair[None], (NZ, 16, LANES))

    for k in range(NY):
        yy = lax.rem(y + k, NY)
        for u, side in enumerate((mine, other)):
            line = side[yy * NZ + z].astype(F32)[16:24, :]
            same = (line == lane_f) & is_block
            slot = jnp.sum(jnp.where(same, slots, 0.0), axis=1, keepdims=True)
            slot = jnp.broadcast_to(slot, (8, LANES))
            block = (yy * NZ + z) * NC + (c if u == 0 else 1 - c)
            own = jnp.sum(jnp.where(lane == block, slots, 0.0), axis=1, keepdims=True)
            own = jnp.broadcast_to(own, (8, LANES))
            depth = jnp.sum(jnp.where(slot > 0.0, 1.0, 0.0), axis=0, keepdims=True)
            entry = jnp.where(row_f == depth, own, slot)
            dealt = jnp.maximum(slot - 1.0, 0.0)
            for half in range(2):
                at = 8 * u + 2 * k + half
                word = pack_rows(dealt, 16, 4 * half, 4)
                table[DEAL + at : DEAL + at + 1, :] = word.astype(jnp.int32)
                word = pack_rows(entry, 32, 4 * half, 4)
                table[BACK + at : BACK + at + 1, :] = word.astype(jnp.int32)
            if k == 0:
                at = 8 * u
                table[LINE + at : LINE + at + 8, :] = slot.astype(jnp.int32)
                table[INNER + at : INNER + at + 8, :] = own.astype(jnp.int32)
                mark = jnp.where(row_f == depth, own, 0.0)
                table[SELF + at : SELF + at + 8, :] = mark.astype(jnp.int32)
    for i in range(6):
        word = jnp.zeros((8, 1), F32)
        for j in range(3):
            held = jnp.where(slots == float(3 * i + j + 1), lane_f + 1.0, 0.0)
            word = word + jnp.sum(held, axis=1, keepdims=True) * float(128**j)
        table[HOLD + i : HOLD + i + 1, :] = jnp.broadcast_to(word, (8, LANES)).astype(jnp.int32)[0:1]

    for u, side in enumerate((mine, other)):
        here = side[y * NZ + z].astype(F32)[16:24, :]
        group, reward = here[0:1, :], here[1:2, :]
        in_m = jnp.where(meta_m[:, 0, :] == group, meta_m[:, 1, :], 0.0)
        in_o = jnp.where(meta_o[:, 0, :] == group, meta_o[:, 1, :], 0.0)
        total = jnp.sum(in_m + in_o, axis=0, keepdims=True)
        squares = jnp.sum(in_m * in_m + in_o * in_o, axis=0, keepdims=True)
        mean = total / GROUP
        spread = jnp.sqrt(jnp.maximum(squares / GROUP - mean * mean, 0.25))
        advantage = (reward - mean) / spread
        advantage = jnp.sum(jnp.where(lane[0:1] == NBLK, advantage, 0.0), axis=1, keepdims=True)
        scale[8 * u : 8 * u + 8] = jnp.broadcast_to(advantage, (8, LANES))


def plan(mine, other):
    return pl.pallas_call(
        plan_kernel,
        in_specs=[in_vmem()] * 2,
        out_specs=(in_vmem(),) * 3,
        **call(
            plan_kernel,
            (
                jax.ShapeDtypeStruct((NZ, HALF, 16, LANES), BF16),
                jax.ShapeDtypeStruct((WORDS, LANES), jnp.int32),
                jax.ShapeDtypeStruct((16, LANES), F32),
            ),
        ),
        name="plan",
    )(mine, other)


def deal_kernel(u, table, column, after, *outs):
    words = table[DEAL + 8 * u : DEAL + 8 * u + 8, :]
    for k in range(NY):
        for d in range(DEPTH):
            slot = (words[2 * k + d // 4, 0] >> (4 * (d % 4))) & 15
            pair = column[:, slot >> 1].astype(F32)
            rows = jnp.where((slot & 1) == 1, pair[:, 8:16], pair[:, 0:8])
            for kind in range(2):
                whole = jnp.concatenate([rows[2 * i + kind] for i in range(4)], 0)
                outs[k][d, 2 * kind : 2 * kind + 2] = whole.astype(BF16).reshape(2, 16, LANES)


def deal(u, table, column, after):
    return pl.pallas_call(
        functools.partial(deal_kernel, u),
        in_specs=[in_vmem()] * 2 + [pl.BlockSpec(memory_space=pl.ANY)],
        out_specs=(in_vmem(),) * NY,
        **call(deal_kernel, (jax.ShapeDtypeStruct(HAND, BF16),) * NY),
        name="deal",
    )(table, column, after)


def halve_kernel(queries, cotangent, own_kv, after, keep, send):
    first_core = place()[2] == 0
    for at, far in ((0, queries), (ROWS, cotangent)):
        whole = far[...].astype(F32)
        low = whole[:, 0:RATIO].reshape(ROWS, HD).astype(BF16)
        high = whole[:, RATIO:].reshape(ROWS, HD).astype(BF16)
        keep[at : at + ROWS] = jnp.where(first_core, low, high)
        send[at : at + ROWS] = jnp.where(first_core, high, low)
    for kind in range(2):
        at = 2 * ROWS + TOK * kind
        low, high = own_kv[kind], own_kv[2 + kind]
        keep[at : at + TOK] = jnp.where(first_core, low, high)
        send[at : at + TOK] = jnp.where(first_core, high, low)


def halve(queries, cotangent, own_kv, after):
    return pl.pallas_call(
        halve_kernel,
        in_specs=[in_vmem()] * 3 + [pl.BlockSpec(memory_space=pl.ANY)],
        out_specs=(in_vmem(),) * 2,
        **call(halve_kernel, (jax.ShapeDtypeStruct((2 * ROWS + 2 * TOK, HD), BF16),) * 2),
        name="halve",
    )(queries, cotangent, own_kv, after)


def prepare_kernel(scale, keep, got, q_all, g_all, kv_all):
    for u, side in enumerate((keep, got)):
        q_all[u] = side[0:ROWS]
        weight = scale[8 * u : 8 * u + 1, :]
        g_all[u] = (side[ROWS : 2 * ROWS].astype(F32) * weight).astype(BF16)
        for kind in range(2):
            at = 2 * ROWS + TOK * kind
            kv_all[2 * u + kind] = side[at : at + TOK]


def prepare(scale, keep, got):
    return pl.pallas_call(
        prepare_kernel,
        in_specs=[in_vmem()] * 3,
        out_specs=(in_vmem(),) * 3,
        **call(
            prepare_kernel,
            (jax.ShapeDtypeStruct((2, ROWS, HD), BF16),) * 2
            + (jax.ShapeDtypeStruct((4, TOK, HD), BF16),),
        ),
        name="prepare",
    )(scale, keep, got)


def rows_of(part, kind):
    return part[:, 2 * kind : 2 * kind + 2].reshape(PART, HD)


def one_part(keys, values, q, g, mask, exps, pgs, stats, at):
    s = lax.dot_general(keys, q, NT, preferred_element_type=F32) * (
        math.log2(math.e) / math.sqrt(HD)
    )
    s = mask(s)
    top = jnp.max(s, axis=0, keepdims=True)
    e = jnp.exp2(s - top)
    pg = lax.dot_general(values, g, NT, preferred_element_type=F32)
    exps[...] = e
    pgs[...] = pg
    stats[at : at + 1, :] = top
    stats[at + 1 : at + 2, :] = jnp.sum(e, axis=0, keepdims=True)
    stats[at + 2 : at + 3, :] = jnp.sum(e * pg, axis=0, keepdims=True)


def causal(s):
    key_pos = lax.broadcasted_iota(jnp.int32, s.shape, 0)
    query_pos = lax.broadcasted_iota(jnp.int32, s.shape, 1) // RATIO
    return jnp.where(key_pos <= query_pos, s, -1e30)


def listed(h, table):
    def mask(s):
        parts = []
        for d in range(DEPTH):
            seen = jnp.concatenate([table[LINE + 8 * h + d : LINE + 8 * h + d + 1, :]] * (ROWS // LANES), 1) > 0
            parts.append(jnp.where(seen, s[32 * d : 32 * d + 32], -1e30))
        return jnp.concatenate(parts, 0)

    return mask


def scores_kernel(h, table, q_all, g_all, part, after, exps, pgs, stats):
    keys, values = rows_of(part, 0), rows_of(part, 1)
    one_part(keys, values, q_all[h], g_all[h], listed(h, table), exps, pgs, stats, 0)


def first_scores_kernel(h, table, q_all, g_all, part, own_kv, exps, pgs, stats, own_exps, own_pgs):
    keys, values = rows_of(part, 0), rows_of(part, 1)
    q, g = q_all[h], g_all[h]
    one_part(keys, values, q, g, listed(h, table), exps, pgs, stats, 0)
    one_part(own_kv[2 * h], own_kv[2 * h + 1], q, g, causal, own_exps, own_pgs, stats, 4)


def all_scores_kernel(h, table, q_all, g_all, p1, p2, p3, after, *outs):
    for i, part in enumerate((p1, p2, p3)):
        keys, values = rows_of(part, 0), rows_of(part, 1)
        one_part(
            keys, values, q_all[h], g_all[h], listed(h, table), *outs[3 * i : 3 * i + 3], 0
        )


def all_scores_of(h, table, q_all, g_all, parts, after):
    return pl.pallas_call(
        functools.partial(all_scores_kernel, h),
        in_specs=[in_vmem()] * 6 + [pl.BlockSpec(memory_space=pl.ANY)],
        out_specs=(in_vmem(),) * 9,
        **call(all_scores_kernel, (wide(PART), wide(PART), STATS) * 3, vmem_mb=16),
        cost_estimate=cost(3 * PART, 2),
        name="scores_all",
    )(table, q_all, g_all, *parts, after)


def wide(keys):
    return jax.ShapeDtypeStruct((keys, ROWS), F32)


STATS = jax.ShapeDtypeStruct((8, TOK * RATIO), F32)


def scores_of(h, table, q_all, g_all, part, after):
    return pl.pallas_call(
        functools.partial(scores_kernel, h),
        in_specs=[in_vmem()] * 4 + [pl.BlockSpec(memory_space=pl.ANY)],
        out_specs=(in_vmem(),) * 3,
        **call(scores_kernel, (wide(PART), wide(PART), STATS), vmem_mb=16),
        cost_estimate=cost(PART, 2),
        name="scores",
    )(table, q_all, g_all, part, after)


def first_scores_of(h, table, q_all, g_all, part, own_kv):
    return pl.pallas_call(
        functools.partial(first_scores_kernel, h),
        in_specs=[in_vmem()] * 5,
        out_specs=(in_vmem(),) * 5,
        **call(
            first_scores_kernel,
            (wide(PART), wide(PART), STATS, wide(TOK), wide(TOK)),
            vmem_mb=16,
        ),
        cost_estimate=cost(PART + TOK, 2),
        name="scores_first",
    )(table, q_all, g_all, part, own_kv)


def cost(keys, products):
    return pl.CostEstimate(
        flops=2 * products * ROWS * keys * HD,
        bytes_accessed=8 * ROWS * keys,
        transcendentals=ROWS * keys,
    )


SMALL = pl.CostEstimate(flops=1000, bytes_accessed=1000, transcendentals=0)


def merge(stats):
    rows = [(ref, 0) for ref in stats] + [(stats[0], 4)]
    tops = [ref[at : at + 1, :] for ref, at in rows]
    top = tops[0]
    for t in tops[1:]:
        top = jnp.maximum(top, t)
    shares = [jnp.exp2(t - top) for t in tops]
    norm = sum(s * ref[at + 1 : at + 2, :] for s, (ref, at) in zip(shares, rows))
    norm = 1.0 / norm
    shares = [s * norm for s in shares]
    delta = sum(s * ref[at + 2 : at + 3, :] for s, (ref, at) in zip(shares, rows))
    return shares, delta


def one_grad(e, pg, share, delta, q, g, keys):
    p = e * share
    low = p.astype(BF16)
    ds = (p * (pg - delta)).astype(BF16)
    factor = 1.0 / math.sqrt(HD)
    dv = lax.dot_general(low, g, NN, preferred_element_type=F32)
    dk = lax.dot_general(ds, q, NN, preferred_element_type=F32) * factor
    turned = keys.astype(F32).T.astype(BF16)
    dq = lax.dot_general(turned, ds, NN, preferred_element_type=F32)
    return dq, dk, dv


def part_grad(k, h, table, stats, exps, pgs, q_all, g_all, part, own_grad, contrib):
    shares, delta = merge(stats)
    dq, dk, dv = one_grad(
        exps[...], pgs[...], shares[k], delta, q_all[h], g_all[h], rows_of(part, 0)
    )
    piece = lax.rem(place()[0] + NY - k, NY)
    for kind, grad in enumerate((dk, dv)):
        own = own_grad[kind, pl.ds(pl.multiple_of(piece * 32, 32), 32), :]
        for d in range(DEPTH):
            mark = table[SELF + 8 * h + d : SELF + 8 * h + d + 1, :] > 0
            both = jnp.where(mark, own, grad[32 * d : 32 * d + 32])
            contrib[d, 2 * kind : 2 * kind + 2] = both.astype(BF16).reshape(2, 16, HD)
    return dq


def first_grads_kernel(
    k, h, table, s0, s1, s2, s3, exps, pgs, q_all, g_all, part, own_exps, own_pgs, own_kv,
    dq_sum, own_grad, contrib,
):
    stats = (s0, s1, s2, s3)
    shares, delta = merge(stats)
    dq, dk, dv = one_grad(
        own_exps[...], own_pgs[...], shares[NY], delta, q_all[h], g_all[h], own_kv[2 * h]
    )
    own_grad[0] = dk
    own_grad[1] = dv
    dq_sum[...] = dq + part_grad(
        k, h, table, stats, exps, pgs, q_all, g_all, part, own_grad, contrib
    )


def grads_kernel(
    k, h, table, s0, s1, s2, s3, exps, pgs, q_all, g_all, part, own_grad, dq_in, *outs
):
    dq_sum, contrib = outs[-2:]
    dq_sum[...] = dq_in[...] + part_grad(
        k, h, table, (s0, s1, s2, s3), exps, pgs, q_all, g_all, part, own_grad, contrib
    )


def emit_kernel(table, dq_0, dq_1, own_0, own_1, keep, send, squares):
    total = jnp.zeros((8, HD), F32)
    for u, (dq, own, out) in enumerate(((dq_0, own_0, keep), (dq_1, own_1, send))):
        dq = dq[...].T * (1.0 / math.sqrt(HD))
        total = total + jnp.sum((dq * dq).reshape(ROWS // 8, 8, HD), axis=0)
        out[0:ROWS] = dq
        own = own[...]
        own_squares = jnp.sum((own * own).reshape(2 * TOK // 8, 8, HD), axis=0)
        inner = table[INNER + 8 * u : INNER + 8 * u + 8, :] > 0
        total = total + jnp.where(inner, 0.0, own_squares)
    send[ROWS : ROWS + TOK] = own_1[0]
    send[ROWS + TOK :] = own_1[1]
    squares[...] = total


def emit(table, dqs, owns):
    return pl.pallas_call(
        emit_kernel,
        in_specs=[in_vmem()] * 5,
        out_specs=(in_vmem(),) * 3,
        **call(
            emit_kernel,
            (
                jax.ShapeDtypeStruct((ROWS, HD), F32),
                jax.ShapeDtypeStruct((ROWS + 2 * TOK, HD), F32),
                jax.ShapeDtypeStruct((8, LANES), F32),
            ),
            vmem_mb=16,
        ),
        cost_estimate=SMALL,
        name="emit",
    )(table, *dqs, *owns)


def ship_kernel(far, after, out):
    pass


def ship(far, after):
    return pl.pallas_call(
        ship_kernel,
        in_specs=[in_vmem(), pl.BlockSpec(memory_space=pl.ANY)],
        out_specs=in_vmem(),
        input_output_aliases={0: 0},
        **call(ship_kernel, jax.ShapeDtypeStruct(far.shape, F32), vmem_mb=16),
        cost_estimate=SMALL,
        name="ship",
    )(far, after)


def assemble_kernel(keep, got, query_grad, token):
    first_core = place()[2] == 0
    near, far = keep[...], got[0:ROWS]
    low, high = jnp.where(first_core, near, far), jnp.where(first_core, far, near)
    query_grad[:, 0:RATIO, :] = low.reshape(TOK, RATIO, HD)
    query_grad[:, RATIO:, :] = high.reshape(TOK, RATIO, HD)
    token[...] = jnp.zeros_like(token)


def assemble(keep, got):
    return pl.pallas_call(
        assemble_kernel,
        in_specs=[in_vmem()] * 2,
        out_specs=(in_vmem(),) * 2,
        **call(
            assemble_kernel,
            (
                jax.ShapeDtypeStruct((TOK, KV * RATIO, HD), F32),
                jax.ShapeDtypeStruct((1, LANES), F32),
            ),
            vmem_mb=16,
        ),
        cost_estimate=SMALL,
        name="assemble",
    )(keep, got)


def grads_of(body, name, outs, k, h, *arrays):
    return pl.pallas_call(
        functools.partial(body, k, h),
        in_specs=[in_vmem()] * len(arrays),
        out_specs=(in_vmem(),) * len(outs),
        **call(body, outs, vmem_mb=16),
        cost_estimate=SMALL,
        name=name,
    )(*arrays)


def attend(h, table, q_all, g_all, own_kv, parts, first, after, hints):
    e, pg, st = [None] * NY, [None] * NY, [None] * NY
    e[0], pg[0], st[0], own_e, own_pg = first
    if h == 0:
        for k in (1, 2, 3):
            e[k], pg[k], st[k] = scores_of(h, table, q_all, g_all, parts[k], after)
            after = st[0] if k == 1 else st[k]
    else:
        outs = all_scores_of(h, table, q_all, g_all, parts[1:], after)
        for k in (1, 2, 3):
            e[k], pg[k], st[k] = outs[3 * k - 3 : 3 * k]
    back = [None] * NY
    dq_type = jax.ShapeDtypeStruct((HD, ROWS), F32)
    own_type = jax.ShapeDtypeStruct((2, TOK, HD), F32)
    contrib_type = jax.ShapeDtypeStruct(HAND, BF16)

    def shared(k):
        return (table, *st, e[k], pg[k], q_all, g_all, parts[k])

    dq, own_grad, back[2] = grads_of(
        first_grads_kernel, "grads_first", (dq_type, own_type, contrib_type), 2, h,
        *shared(2), own_e, own_pg, own_kv,
    )
    for k, hint in ((1, hints[:1]), (3, hints[1:])):
        dq, back[k] = grads_of(
            grads_kernel, "grads", (dq_type, contrib_type), k, h, *shared(k), own_grad, dq, *hint
        )

    def last(after):
        return grads_of(
            grads_kernel, "grads_last", (dq_type, contrib_type), 0, h, *shared(0), own_grad, dq, after
        )

    return dq, own_grad, back, last


def add_part(k, u, table, part, acc):
    at = BACK + 8 * u + 2 * k
    words = table[at : at + 2, :]
    for d in range(DEPTH):
        slot = (words[d // 4, 0] >> (5 * (d % 4))) & 31
        acc[jnp.maximum(slot - 1, 0)] += jnp.where(slot > 0, part[d].astype(F32), 0.0)


def combine_first_kernel(table, part_1, part_2, acc, token):
    acc[...] = jnp.zeros_like(acc)
    add_part(1, 0, table, part_1, acc)
    add_part(2, 0, table, part_2, acc)
    token[...] = jnp.zeros_like(token)


def combine_kernel(ks, u, table, *refs):
    acc = refs[len(ks) + 2]
    for token in refs[len(ks) + 3 :]:
        token[...] = jnp.zeros_like(token)
    for k, part in zip(ks, refs):
        add_part(k, u, table, part, acc)


def leave_kernel(acc, halves):
    for z in range(NZ):
        at = 2 * (z % 2) + z // 4
        rows = slice(8 * (z // 2 % 2), 8 * (z // 2 % 2) + 8)
        halves[z] = acc[:, at, rows, :].reshape(HALF, 16, LANES).astype(BF16)


ACC = (2 * HALF, QUAD, 16, LANES)


def acc_and_token():
    return jax.ShapeDtypeStruct(ACC, F32), jax.ShapeDtypeStruct((8, LANES), F32)


def combine_start(table, part_1, part_2):
    return pl.pallas_call(
        combine_first_kernel,
        in_specs=[in_vmem()] * 3,
        out_specs=(in_vmem(),) * 2,
        **call(combine_first_kernel, acc_and_token(), vmem_mb=16),
        cost_estimate=SMALL,
        name="combine_first",
    )(table, part_1, part_2)


def combine_more(ks, u, table, parts, acc, after, outs=1):
    return pl.pallas_call(
        functools.partial(combine_kernel, ks, u),
        in_specs=[in_vmem()] * (2 + len(parts)) + [pl.BlockSpec(memory_space=pl.ANY)],
        out_specs=(in_vmem(),) * outs,
        input_output_aliases={1 + len(parts): 0},
        **call(combine_kernel, acc_and_token()[:outs], vmem_mb=16),
        cost_estimate=SMALL,
        name="combine",
    )(table, *parts, acc, after)


def leave(acc):
    return pl.pallas_call(
        leave_kernel,
        in_specs=[in_vmem()],
        out_specs=in_vmem(),
        **call(leave_kernel, jax.ShapeDtypeStruct((NZ, HALF, 16, LANES), BF16), vmem_mb=16),
        cost_estimate=SMALL,
        name="leave",
    )(acc)


def split_rows(value, rows):
    high = value.astype(BF16).astype(F32)
    middle = (value - high).astype(BF16).astype(F32)
    low = value - high - middle
    row = lax.broadcasted_iota(jnp.int32, (8, LANES), 0)
    tile = jnp.where(row == 0, high, jnp.where(row == 1, middle, jnp.where(row == 2, low, 0.0)))
    if rows > 8:
        tile = jnp.concatenate([tile, jnp.zeros((rows - 8, LANES), F32)], 0)
    return tile


def total_kernel(parts, squares, totals, sums):
    sums_now = parts[0].astype(F32)
    for z in range(1, NZ):
        sums_now = sums_now + parts[z].astype(F32)
    totals[...] = sums_now
    tile = squares[...] + jnp.sum((sums_now * sums_now).reshape(HALF * 2, 8, LANES), axis=0)
    sums[...] = jnp.broadcast_to(jnp.sum(tile, axis=0, keepdims=True), (8, LANES))


def route_kernel(table, parts, squares, out, room, totals, sums):
    total_kernel(parts, squares, totals, sums)
    c = place()[2]
    words = table[HOLD : HOLD + 8, :]
    room[...] = jnp.zeros_like(room)
    for s in range(2 * HALF):
        block = ((words[s // 3, 0] >> (7 * (s % 3))) & 127) - 1
        side = jnp.where((block & 1) == c, 0, 1)
        to = jnp.where(block >= 0, (block >> 1) * 2 + side, NBLK)
        room[to] = totals[s // 2, 8 * (s % 2) : 8 * (s % 2) + 8, :]
    tails = jnp.broadcast_to(split_rows(sums[...], 8)[None], (NY * NZ, 8, LANES))
    rows = room[0:NBLK].reshape(NY * NZ, 16, LANES)
    out[...] = jnp.concatenate([rows, tails], 1).astype(BF16)


def route(table, parts, squares):
    return pl.pallas_call(
        route_kernel,
        in_specs=[in_vmem()] * 3,
        out_specs=in_vmem(),
        **call(
            route_kernel,
            jax.ShapeDtypeStruct((NY * NZ, 24, LANES), BF16),
            [
                VMEM((NBLK + 1, 8, LANES), F32),
                VMEM((HALF, 16, LANES), F32),
                VMEM((8, LANES), F32),
            ],
        ),
        name="route",
    )(table, parts, squares)


def share_kernel(arrived, send, sums):
    whole = arrived[...].astype(F32)
    for i in range(NY * NZ // 2):
        pair = [whole[2 * i + j, 8:16, :] for j in range(2)]
        send[i] = jnp.concatenate(pair, 0).astype(BF16)
    tails = jnp.sum(jnp.sum(whole[:, 16:24, :], axis=0), axis=0, keepdims=True)
    value = jnp.broadcast_to(tails, (8, LANES))
    sums[...] = value
    send[NY * NZ // 2] = split_rows(value, 16).astype(BF16)


def share(arrived):
    return pl.pallas_call(
        share_kernel,
        in_specs=[in_vmem()],
        out_specs=(in_vmem(),) * 2,
        **call(
            share_kernel,
            (
                jax.ShapeDtypeStruct((NY * NZ // 2 + 1, 16, LANES), BF16),
                jax.ShapeDtypeStruct((8, LANES), F32),
            ),
        ),
        name="share",
    )(arrived)


def tally_kernel(mine, got, sums):
    tails = mine[0:1, :] + jnp.sum(got[NY * NZ // 2].astype(F32), axis=0, keepdims=True)
    sums[...] = jnp.broadcast_to(jnp.sum(tails, axis=1, keepdims=True), (1, LANES))


def tally(mine, got):
    return pl.pallas_call(
        tally_kernel,
        in_specs=[in_vmem()] * 2,
        out_specs=in_vmem(),
        **call(tally_kernel, jax.ShapeDtypeStruct((1, LANES), F32)),
        name="tally",
    )(mine, got)


def finish_kernel(table, arrived, got, own, own_far, key_grad, value_grad, token):
    token[...] = jnp.zeros_like(token)
    first_core = place()[2] == 0
    inner = table[INNER : INNER + 1, :] > 0
    for z in range(NZ):
        kind = z % 2
        out = value_grad if kind else key_grad
        for y in range(NY):
            at, src = row_of(y, z), y * NZ + z
            near = arrived[src].astype(F32)[0:8]
            far = got[src // 2].astype(F32)[8 * (src % 2) : 8 * (src % 2) + 8]
            near = jnp.where(inner, near, own[kind, at : at + 8, :])
            low = ROWS + TOK * kind + at
            far = jnp.where(inner, far, own_far[low : low + 8, :])
            out[at : at + 8, 0, :] = jnp.where(first_core, near, far)
            out[at : at + 8, 1, :] = jnp.where(first_core, far, near)


def finish(*arrays):
    return pl.pallas_call(
        finish_kernel,
        in_specs=[in_vmem()] * 5,
        out_specs=(in_vmem(),) * 3,
        **call(
            finish_kernel,
            (jax.ShapeDtypeStruct((TOK, KV, HD), F32),) * 2
            + (jax.ShapeDtypeStruct((1, LANES), F32),),
        ),
        cost_estimate=SMALL,
        name="finish",
    )(*arrays)


def local(queries, keys, values, cotangent, rewards, groups, ancestors, step_ids):
    packet, own_kv = packet_of(keys, values, ancestors, groups, rewards)
    mine = swap_yz(packet)
    other = other_core(mine)
    trained = (step_ids[0] % 2 == 0)[:, None, None]
    masked = jnp.where(trained, cotangent, jnp.zeros_like(cotangent))
    picked, table, scale = plan(mine, other)
    column = swap_z(picked)
    first = deal(0, table, column, table)
    keep, send = halve(queries, masked, own_kv, table)
    q_all, g_all, kv_all = prepare(scale, keep, other_core(send))
    parts = []
    for u in range(2):
        dealt = first if u == 0 else deal(u, table, column, first[0])
        parts.append([dealt[0]] + [along_y(dealt[k], k) for k in (1, 2, 3)])
    firsts = [first_scores_of(u, table, q_all, g_all, parts[u][0], kv_all) for u in range(2)]
    after, own_0, sent, last_0 = attend(
        0, table, q_all, g_all, kv_all, parts[0], firsts[0], firsts[1][2], ()
    )
    back_0 = [None] + [along_y(sent[k], -k) for k in (1, 2, 3)]
    acc, token = combine_start(table, back_0[1], back_0[2])
    acc, late_token = combine_more((3,), 0, table, [back_0[3]], acc, table, 2)
    after, own_1, sent, last_1 = attend(
        1, table, q_all, g_all, kv_all, parts[1], firsts[1], after, (token, late_token)
    )
    back_1 = [None] + [along_y(sent[k], -k) for k in (1, 2, 3)]
    dq_0, back_0[0] = last_0(after)
    dq_1, back_1[0] = last_1(dq_0)
    near, far, squares = emit(table, (dq_0, dq_1), (own_0, own_1))
    (acc,) = combine_more((0,), 0, table, [back_0[0]], acc, squares)
    (acc,) = combine_more((1, 0), 1, table, [back_1[1], back_1[0]], acc, squares)
    (acc,) = combine_more((2,), 1, table, [back_1[2]], acc, squares)
    (acc,) = combine_more((3,), 1, table, [back_1[3]], acc, squares)
    halves = leave(acc)
    arrived = swap_yz(route(table, swap_z(halves), squares))
    shared, mine_sum = share(arrived)
    shared = other_core(shared)
    mine_sum = tally(mine_sum, shared)
    far = other_core(ship(far, mine_sum))
    query_grad, done = assemble(near, far)
    key_grad, value_grad, token = finish(table, arrived, shared, own_0, far)
    all_sum = mine_sum + (done + token)
    for k in (1, 2, 3):
        all_sum = all_sum + along_head(mine_sum, k)
    count = float(NBLK * TOK * NHEAD * (KV * RATIO + 2 * KV) * HD)
    grad_rms = jnp.sqrt(all_sum[0, 0] / count)
    return query_grad, key_grad, value_grad, grad_rms


def solution(mesh):
    in_specs = (
        P("branch", "head", None),
        P("branch", "head", None),
        P("branch", "head", None),
        P("branch", "head", None),
        P("branch"),
        P("branch"),
        P("branch", None),
        P("branch", None),
    )
    out_specs = (
        P("branch", "head", None),
        P("branch", "head", None),
        P("branch", "head", None),
        P(),
    )
    return jax.shard_map(local, mesh=mesh, in_specs=in_specs, out_specs=out_specs, check_vma=False)
```
